32 devices in a mesh: seq: 8 (over z, x), tp: 4 (over y, core).
Axes of the slice: x: 2, y: 2, z: 4, core: 2. Of those that a mesh axis runs over, the one named last changes fastest.
Arguments:
- latents_in: bfloat16 [16384, 1024], P(('seq', 'tp')), may hold values from -6 to 6
- gain_one: float32 [1024], replicated, may hold values from 0.5 to 1.5
- w_qkv: bfloat16 [1024, 3, 1024], P(None, None, 'tp'), may hold values from -0.1875 to 0.1875
- w_out: bfloat16 [1024, 1024], P(None, 'tp'), may hold values from -0.75 to 0.75
- gain_two: float32 [1024], replicated, may hold values from 0.5 to 1.5
- w_gate: bfloat16 [1024, 2816], P(None, 'tp'), may hold values from -0.1875 to 0.1875
- w_up: bfloat16 [1024, 2816], P(None, 'tp'), may hold values from -0.1875 to 0.1875
- w_down: bfloat16 [1024, 2816], P(None, 'tp'), may hold values from -0.109375 to 0.109375
- cotangent: bfloat16 [16384, 1024], P(('seq', 'tp')), may hold values from -6 to 6
- doc_lengths: int32 [8, 3], P('seq'), may hold values from 256 to 1024, as said below
- valid_lengths: int32 [8, 3], P('seq'), may hold values from 192 to 1024, as said below
- hash_ids: int32 [6, 16384], P(None, ('seq', 'tp')), may hold values from 0 to 500001
- hash_weights: float32 [6, 16384], P(None, ('seq', 'tp')), may hold values from -6 to 6
Outputs:
- latents_out: bfloat16 [16384, 1024], P(('seq', 'tp'))
- grad_latents: float32 [16384, 1024], P(('seq', 'tp'))
- grad_gain_one: float32 [1024], replicated
- grad_w_qkv: float32 [1024, 3, 1024], P('seq', None, 'tp')
- grad_w_out: float32 [1024, 1024], P('seq', 'tp')
- grad_gain_two: float32 [1024], replicated
- grad_w_gate: float32 [1024, 2816], P('seq', 'tp')
- grad_w_up: float32 [1024, 2816], P('seq', 'tp')
- grad_w_down: float32 [1024, 2816], P('seq', 'tp')
- hash_counts: float32 [6, 500002], replicated
The draws below stay inside these ranges and needn't reach their ends.
Inputs may be any that keep to these rules, and one draw needn't show every extreme that they name: `doc_lengths`: in each group the 3 lengths sum to 2048; one of them is 1024, the others at least one eighth of 2048. `valid_lengths`: each sequence's valid patches are at least three quarters of its length and come first in it.
All inputs are finite; a program needn't handle non-finite values.
Results may differ from the reference program's by a relative error of at most 0.018.
Values may be sent and summed in bfloat16 or wider, within the bound.
A program may use at most 256 MiB of HBM per device.

```python
import math
import jax
import jax.numpy as jnp
import numpy as np
from jax import lax

D = 1024
HEADS = 16
HEAD_DIM = 64
FF = 2816
HASH_ROWS = 500002
NGRAMS = 6
GROUP_TOK = 2048
DOCS = 3
TOKENS = 16384
N_SEQ = 8


def doc_plan(seed_key):
    longest = GROUP_TOK // 2
    lowest = GROUP_TOK // 8
    key_len, key_turn, key_pad = jax.random.split(seed_key, 3)
    second = jax.random.randint(key_len, (N_SEQ,), lowest, longest - lowest + 1)
    third_len = GROUP_TOK - longest - second
    base = jnp.stack([jnp.full((N_SEQ,), longest, jnp.int32), second.astype(jnp.int32), third_len.astype(jnp.int32)], axis=1)
    rotation = jax.random.randint(key_turn, (N_SEQ, 1), 0, DOCS)
    order = (jnp.arange(DOCS, dtype=jnp.int32)[None, :] + rotation) % DOCS
    lengths = jnp.take_along_axis(base, order, axis=1)
    padding = jax.random.randint(key_pad, (N_SEQ, DOCS), 0, lengths // 4 + 1)
    first_group = jnp.arange(N_SEQ)[:, None] == 0
    padding = jnp.where(first_group & (lengths == longest), 0, padding)
    return (lengths.astype(jnp.int32), (lengths - padding).astype(jnp.int32))


def draw_doc_lengths(key, part):
    return doc_plan(key)[0]


def draw_valid_lengths(key, part):
    return doc_plan(key)[1]


def plant(drawn, rng, low, top_value):
    extent = drawn.shape
    index_at = [jax.random.randint(jax.random.fold_in(rng, axis), (), 0, extent[axis]) for axis in range(len(extent))]
    drawn = drawn.at[tuple(index_at)].set(low)
    longest = extent.index(max(extent))
    index_at[longest] = (index_at[longest] + 1) % extent[longest]
    return drawn.at[tuple(index_at)].set(top_value)


def level_of(rng, extent, cuts, low, high):
    def one(dim, shards_of):
        steps = jax.random.uniform(jax.random.fold_in(jax.random.fold_in(rng, 6), dim), (shards_of,), jnp.float32, low / len(cuts), high / len(cuts))
        return jnp.repeat(jnp.exp(steps), extent[dim] // shards_of).reshape((-1,) + (1,) * (len(extent) - dim - 1))

    level = one(*cuts[0])
    for cut in cuts[1:]:
        level = level * one(*cut)
    return level


def skewed_wide(key, dims, amount, skew):
    portions = [min(1 << octave, amount + 1 - (1 << octave)) * (1 << 20) // math.isqrt((1 << octave) ** skew) + 1 for octave in range((amount + 1).bit_length()) if 1 << octave <= amount]
    spread = 1 + sum(portions) // (1 << 30)
    table = np.cumsum(np.array([max(1, weight // spread) for weight in portions]))
    ticket = jax.random.randint(jax.random.fold_in(key, 1), dims, 0, int(table[len(portions) - 1]))
    start = jnp.left_shift(1, jnp.searchsorted(jnp.asarray(table, jnp.int32), ticket, side="right").astype(jnp.int32))
    grade = start - 1 + jax.random.randint(jax.random.fold_in(key, 4), dims, 0, 1 << 30) % jnp.minimum(start, amount + 1 - start)
    return jax.random.permutation(jax.random.fold_in(key, 2), amount)[grade].astype(jnp.int32)


def scatter_about(own_key, dims, deviation, limit, cuts=(), kind=jnp.bfloat16):
    values = jax.random.normal(own_key, dims, jnp.float32) * deviation
    if len(cuts) > 0:
        values = level_of(own_key, dims, cuts, -0.22, 0.18) * values
    return jnp.clip(values, min=-limit, max=limit).astype(kind)


def setup_inputs(seed: int = 0) -> dict:
    seeds = jax.random.split(jax.random.key(seed), 14)
    latents_in = scatter_about(seeds[0], (TOKENS, D), 1.0, 6.0, ((0, 32),))
    gain_one = jnp.clip(1.0 + 0.1 * jax.random.normal(seeds[1], (D,), jnp.float32), 0.5, 1.5)
    w_qkv = scatter_about(seeds[2], (D, 3, D), D ** -0.5, 0.1875, ((2, 4),))
    w_out = scatter_about(seeds[3], (D, D), (D // 16) ** -0.5, 0.75, ((1, 4),))
    gain_two = jnp.clip(1.0 + 0.1 * jax.random.normal(seeds[4], (D,), jnp.float32), 0.5, 1.5)
    w_gate = scatter_about(seeds[5], (D, FF), D ** -0.5, 0.1875, ((1, 4),))
    w_up = scatter_about(seeds[6], (D, FF), D ** -0.5, 0.1875, ((1, 4),))
    w_down = scatter_about(seeds[7], (D, FF), FF ** -0.5, 0.109375, ((1, 4),))
    cotangent = scatter_about(seeds[8], (TOKENS, D), 1.0, 6.0, ((0, 32),))
    doc_lengths = draw_doc_lengths(jax.random.fold_in(seeds[13], 71), 0)
    valid_lengths = draw_valid_lengths(jax.random.fold_in(seeds[13], 71), 0)
    hash_ids = plant(skewed_wide(seeds[11], (NGRAMS, TOKENS), HASH_ROWS, 2), jax.random.fold_in(seeds[11], 3), 0, HASH_ROWS - 1).astype(jnp.int32)
    hash_weights = scatter_about(seeds[12], (NGRAMS, TOKENS), 1.0, 6.0, ((1, 32),), jnp.float32)
    return {"latents_in": latents_in, "gain_one": gain_one, "w_qkv": w_qkv, "w_out": w_out, "gain_two": gain_two, "w_gate": w_gate, "w_up": w_up, "w_down": w_down, "cotangent": cotangent, "doc_lengths": doc_lengths, "valid_lengths": valid_lengths, "hash_ids": hash_ids, "hash_weights": hash_weights}


@jax.custom_vjp
def low(v):
    return lax.optimization_barrier(v.astype(jnp.bfloat16)).astype(jnp.float32)

@jax.custom_vjp
def low_back(v):
    return v

def low_keep(v):
    return (low(v), None)

def low_pass(kept, grad):
    return (grad,)

def back_keep(v):
    return (v, None)

def back_low(kept, grad):
    return (low(grad),)
low.defvjp(low_keep, low_pass)
low_back.defvjp(back_keep, back_low)
EPSILON = 1e-05
HIGHEST = lax.Precision.HIGHEST
MASKED = -1e+30

def rms_norm(row_data, gain):
    scaling = lax.rsqrt(lax.optimization_barrier(jnp.mean(row_data * row_data, axis=-1, keepdims=True)) + EPSILON)
    return row_data * scaling * gain

def doc_masks(lengths, valid_count):
    doc_ends = jnp.cumsum(lengths)
    doc_starts = doc_ends - lengths
    positions = jnp.arange(GROUP_TOK, dtype=jnp.int32)
    doc_ids = lax.optimization_barrier(jnp.sum((positions[:, None] >= doc_ends[None, :]).astype(jnp.int32), axis=1))
    usable = jnp.any((positions[:, None] >= doc_starts[None, :]) & (positions[:, None] < (doc_starts + valid_count)[None, :]), axis=1)
    return (doc_ids, usable)

def attend(queries, key_rows, value_rows, doc_ids, usable):
    block_rows = min(512, GROUP_TOK)
    number = GROUP_TOK // block_rows
    positions = jnp.arange(GROUP_TOK, dtype=jnp.int32)

    def one_block(inputs):
        query_block, block_places = inputs
        scores = jnp.einsum('qhd,khd->hqk', query_block, key_rows, precision=HIGHEST) * HEAD_DIM ** (-0.5)
        scores = low_back(scores)
        allowed = (positions[None, :] <= block_places[:, None]) & (doc_ids[block_places][:, None] == doc_ids[None, :]) & usable[None, :]
        scores = jnp.where(allowed[None], scores, MASKED)
        attn_probs = low(jax.nn.softmax(scores, axis=-1))
        return jnp.einsum('hqk,khd->qhd', attn_probs, value_rows, precision=HIGHEST)
    blocks = lax.map(jax.checkpoint(one_block), (queries.reshape(number, block_rows, HEADS, HEAD_DIM), positions.reshape(number, block_rows)))
    return blocks.reshape(GROUP_TOK, D)

def layer(row_data, gain_one, w_qkv, w_out, gain_two, w_gate, w_up, w_down, doc_ids, usable):
    normed = low(rms_norm(row_data, gain_one))
    mixed_qkv = jnp.einsum('td,dch->tch', normed, w_qkv, precision=HIGHEST)
    mixed_qkv = low_back(low(mixed_qkv))
    queries = mixed_qkv[:, 0].reshape(GROUP_TOK, HEADS, HEAD_DIM)
    key_rows = mixed_qkv[:, 1].reshape(GROUP_TOK, HEADS, HEAD_DIM)
    value_rows = mixed_qkv[:, 2].reshape(GROUP_TOK, HEADS, HEAD_DIM)
    heads_out = low_back(low(attend(queries, key_rows, value_rows, doc_ids, usable)))
    branch = low_back(jnp.dot(heads_out, w_out.T, precision=HIGHEST))
    hidden = row_data + branch
    normed_two = low(rms_norm(hidden, gain_two))
    gate_val = low_back(jnp.dot(normed_two, w_gate, precision=HIGHEST))
    up_val = low_back(jnp.dot(normed_two, w_up, precision=HIGHEST))
    activation = low(jax.nn.silu(gate_val) * up_val)
    return hidden + jnp.dot(activation, w_down.T, precision=HIGHEST)

def reference(latents_in, gain_one, w_qkv, w_out, gain_two, w_gate, w_up, w_down, cotangent, doc_lengths, valid_lengths, hash_ids, hash_weights):
    weights = tuple((item.astype(jnp.float32) for item in (gain_one, w_qkv, w_out, gain_two, w_gate, w_up, w_down)))
    rows_all = latents_in.astype(jnp.float32).reshape(N_SEQ, GROUP_TOK, D)
    grads_all = cotangent.astype(jnp.float32).reshape(N_SEQ, GROUP_TOK, D)

    def group_step(totals, inputs):
        row_data, grad_rows, lengths, valid_count = inputs
        doc_ids, usable = doc_masks(lengths, valid_count)

        def runner(row_input, *params):
            return layer(row_input, *params, doc_ids, usable)
        result, pullback = jax.vjp(runner, row_data, *weights)
        pieces = pullback(grad_rows)
        totals = tuple((total + piece for total, piece in zip(totals, pieces[1:])))
        return (totals, (result.astype(jnp.bfloat16), pieces[0]))
    zero_grads = tuple((jnp.zeros_like(item) for item in weights))
    totals, (outputs, grad_latents) = lax.scan(group_step, zero_grads, (rows_all, grads_all, doc_lengths, valid_lengths))
    offsets = jnp.arange(NGRAMS, dtype=jnp.int32)[:, None] * HASH_ROWS
    flat_ids = (hash_ids + offsets).reshape(-1)
    flat_weights = hash_weights.astype(jnp.float32).reshape(-1)
    hash_counts = jax.ops.segment_sum(flat_weights, flat_ids, num_segments=NGRAMS * HASH_ROWS).reshape(NGRAMS, HASH_ROWS)
    return (outputs.reshape(TOKENS, D), grad_latents.reshape(TOKENS, D), totals[0], totals[1], totals[2], totals[3], totals[4], totals[5], totals[6], hash_counts)
```

```python
import functools

import jax
import jax.numpy as jnp
from jax import lax
from jax.experimental import pallas as pl
from jax.experimental.pallas import tpu as pltpu
from jax.sharding import PartitionSpec as P

HEAD_DIM = 64
EPSILON = 1e-05
MASKED = -1e30
BF = jnp.bfloat16
F32 = jnp.float32
QB = 256
VMEM_BYTES = 56 * 1024 * 1024


def flip(x, axis, bits):
    count = lax.axis_size(axis)
    return lax.ppermute(x, axis, [(i, i ^ bits) for i in range(count)])


def dot(a, b):
    return lax.dot_general(a, b, (((1,), (0,)), ((), ())), preferred_element_type=F32)


def cost(flops, moved):
    return pl.CostEstimate(flops=flops, bytes_accessed=moved, transcendentals=0)


def params():
    return pltpu.CompilerParams(vmem_limit_bytes=VMEM_BYTES)


def whole(shape):
    return pl.BlockSpec(shape, lambda i, sc: (0,) * len(shape))


def gather_rows(x):
    across = flip(x, "tp", 2)
    return [x, flip(x, "tp", 1), across, flip(across, "tp", 1)]


def scatter_far(part_two, part_three):
    both = (part_two.astype(F32) + flip(part_three, "tp", 1).astype(F32)).astype(BF)
    return flip(both, "tp", 2)


def scatter_sum(part_zero, part_one, far):
    return part_zero.astype(F32) + flip(part_one, "tp", 1).astype(F32) + far.astype(F32)


def norm_rows(row_data, gain):
    scaling = lax.rsqrt(jnp.mean(row_data * row_data, axis=-1, keepdims=True) + EPSILON)
    return (row_data * scaling * gain, scaling)


def norm_back(row_data, scaling, gain, grad_norm):
    weighted = grad_norm * gain
    inner_mean = jnp.mean(weighted * row_data, axis=-1, keepdims=True)
    grad_rows = scaling * weighted - row_data * scaling * scaling * scaling * inner_mean
    grad_gain = jnp.sum(grad_norm * row_data * scaling, axis=0)
    return (grad_rows, grad_gain)


def qkv_kernel(sc, a_ref, b_ref, w_ref, *rest):
    out_ref = rest[-1]
    step = pl.program_id(0)

    @pl.when(step < 2)
    def _():
        out_ref[...] = dot(a_ref[...], w_ref[...]).astype(BF)

    @pl.when(step >= 2)
    def _():
        out_ref[...] = dot(b_ref[...], w_ref[...]).astype(BF)


def qkv_call(sc, first, a, b, w, into):
    half, width = a.shape[0] // 2, w.shape[1]
    rows = 4 * a.shape[0]
    pair = lambda which: pl.BlockSpec(
        (half, a.shape[1]), lambda i, sc: (jnp.clip(i - 2 * which, 0, 1), 0)
    )
    extra = [] if into is None else [into]
    return pl.pallas_call(
        qkv_kernel,
        grid_spec=pltpu.PrefetchScalarGridSpec(
            num_scalar_prefetch=1,
            grid=(4,),
            in_specs=[pair(0), pair(1), whole(w.shape)] + [pl.BlockSpec(memory_space=pl.ANY)] * len(extra),
            out_specs=pl.BlockSpec(
                (half, width), lambda i, sc: ((sc[0] ^ (first + i // 2)) * 2 + i % 2, 0)
            ),
        ),
        out_shape=jax.ShapeDtypeStruct((rows, width), BF),
        input_output_aliases={4: 0} if extra else {},
        compiler_params=params(),
        cost_estimate=cost(2 * 2 * a.shape[0] * a.shape[1] * width, 4_000_000),
        name="qkv",
    )(sc, a, b, w, *extra)


def doc_bounds(sc, places):
    low = jnp.where(places >= sc[2], sc[2], jnp.where(places >= sc[1], sc[1], 0))
    end = jnp.where(places >= sc[2], sc[5], jnp.where(places >= sc[1], sc[4], sc[3]))
    return low, jnp.minimum(places, end - 1)


def head_rows(x, h):
    where = lax.broadcasted_iota(jnp.int32, x.shape, 0) // HEAD_DIM
    return jnp.where(where == h, x, jnp.zeros_like(x))


def head_lanes(x, h):
    where = lax.broadcasted_iota(jnp.int32, x.shape, 1) // HEAD_DIM
    return jnp.where(where == h, x, jnp.zeros_like(x))


def attend_kernel(first, heads, sc, qkv_ref, wo_ref, *rest):
    heads_ref, lse_ref, pa_ref, pb_ref, vt_ref, qt_ref, acc_ref = rest[-7:]
    width = heads * HEAD_DIM
    step = pl.program_id(0)

    @pl.when(step == 0)
    def _():
        for n in range(qkv_ref.shape[0] // QB):
            vt_ref[:, n * QB : (n + 1) * QB] = qkv_ref[n * QB : (n + 1) * QB, 2 * width :].T

    rank = first + 1 - step // 2
    start = (sc[0] ^ rank) * (2 * QB) + (step % 2) * QB
    start = pl.multiple_of(start, QB)
    q_t = qkv_ref[pl.ds(start, QB), :width].T * jnp.asarray(HEAD_DIM**-0.5, BF)
    for h in range(heads):
        qt_ref[h] = head_rows(q_t, h)
    acc_ref[...] = jnp.zeros_like(acc_ref)
    places = start + lax.broadcasted_iota(jnp.int32, (1, QB), 1)
    low, high = doc_bounds(sc, places)
    low_first, _ = doc_bounds(sc, start)

    def body(kb, state):
        at = pl.multiple_of(kb * QB, QB)
        keys = qkv_ref[pl.ds(at, QB), width : 2 * width]
        value_t = vt_ref[:, pl.ds(at, QB)]
        spot = at + lax.broadcasted_iota(jnp.int32, (QB, QB), 0)
        allowed = (spot >= low) & (spot <= high)
        fresh = []
        for h in range(heads):
            top, total = state[h]
            scores = jnp.where(allowed, dot(keys, qt_ref[h]), MASKED)
            new_top = jnp.maximum(top, jnp.max(scores, axis=0, keepdims=True))
            fade = jnp.exp(top - new_top)
            probs = jnp.exp(scores - new_top)
            total = total * fade + jnp.sum(probs, axis=0, keepdims=True)
            part = slice(h * HEAD_DIM, (h + 1) * HEAD_DIM)
            acc_ref[part] = acc_ref[part] * fade + dot(value_t[part], probs.astype(BF))
            fresh.append((new_top, total))
        return tuple(fresh)

    begin = tuple(
        (jnp.full((1, QB), MASKED, F32), jnp.zeros((1, QB), F32)) for _ in range(heads)
    )
    state = lax.fori_loop(low_first // QB, start // QB + 1, body, begin)
    lse_ref[...] = jnp.zeros_like(lse_ref)
    for h in range(heads):
        top, total = state[h]
        part = slice(h * HEAD_DIM, (h + 1) * HEAD_DIM)
        acc_ref[part] = acc_ref[part] * (1.0 / total)
        lse_ref[h : h + 1] = top + jnp.log(total)
    out = acc_ref[...].T.astype(BF)
    heads_ref[...] = out
    partial = dot(out, wo_ref[...]).astype(BF)

    @pl.when(step < 2)
    def _():
        pa_ref[...] = partial

    @pl.when(step >= 2)
    def _():
        pb_ref[...] = partial


def attend_call(sc, first, qkv, wo_t, heads_into, lse_into):
    rows, width = qkv.shape[0], qkv.shape[1] // 3
    heads = width // HEAD_DIM
    model = wo_t.shape[1]
    half = rows // 8
    assert half == QB
    extra = [] if heads_into is None else [heads_into, lse_into]
    spot = lambda i: 2 * (first + 1 - i // 2) + i % 2
    pair = lambda which: pl.BlockSpec(
        (half, model), lambda i, sc: (jnp.clip(i - 2 * which, 0, 1), 0)
    )
    return pl.pallas_call(
        functools.partial(attend_kernel, first, heads),
        grid_spec=pltpu.PrefetchScalarGridSpec(
            num_scalar_prefetch=1,
            grid=(4,),
            in_specs=[whole(qkv.shape), whole(wo_t.shape)]
            + [pl.BlockSpec(memory_space=pl.ANY)] * len(extra),
            out_specs=[
                pl.BlockSpec((half, width), lambda i, sc: (spot(i), 0)),
                pl.BlockSpec((8, half), lambda i, sc: (0, spot(i))),
                pair(0),
                pair(1),
            ],
            scratch_shapes=[
                pltpu.VMEM((width, rows), BF),
                pltpu.VMEM((heads, width, QB), BF),
                pltpu.VMEM((width, QB), F32),
            ],
        ),
        out_shape=[
            jax.ShapeDtypeStruct((rows, width), BF),
            jax.ShapeDtypeStruct((8, rows), F32),
            jax.ShapeDtypeStruct((rows // 4, model), BF),
            jax.ShapeDtypeStruct((rows // 4, model), BF),
        ],
        input_output_aliases={3: 0, 4: 1} if extra else {},
        compiler_params=params(),
        cost_estimate=cost(6_000_000_000, 8_000_000),
        name="attend",
    )(sc, qkv, wo_t, *extra)


def attend_back_kernel(first, last, heads, sc, ga_ref, gb_ref, wo_ref, qkv_ref, heads_ref, lse_ref, *rest):
    width = heads * HEAD_DIM
    kt_ref, qt_ref, gt_ref, qs_ref, gs_ref, dqt_ref = rest[-6:]
    if last:
        dq_in, dk_in, dv_in, mixed_ref, dk_ref, dv_ref = rest[:-6]
    else:
        dq_ref, dk_ref, dv_ref = rest[:-6]
    step = pl.program_id(0)
    rows = qkv_ref.shape[0]

    @pl.when(step == 0)
    def _():
        for n in range(rows // QB):
            kt_ref[:, n * QB : (n + 1) * QB] = qkv_ref[n * QB : (n + 1) * QB, width : 2 * width].T
        if last:
            dk_ref[...] = dk_in[...]
            dv_ref[...] = dv_in[...]
            mixed_ref[: rows // 2, :width] = dq_in[...]
        else:
            dk_ref[...] = jnp.zeros_like(dk_ref)
            dv_ref[...] = jnp.zeros_like(dv_ref)

    rank = first + step // 2
    start = (sc[0] ^ rank) * (2 * QB) + (step % 2) * QB
    start = pl.multiple_of(start, QB)

    @pl.when(step < 2)
    def _():
        gs_ref[:QB] = dot(ga_ref[...], wo_ref[...]).astype(BF)

    @pl.when(step >= 2)
    def _():
        gs_ref[:QB] = dot(gb_ref[...], wo_ref[...]).astype(BF)

    grad = gs_ref[:QB]
    grad_t = grad.T
    out_t = heads_ref[...].T
    product = grad_t.astype(F32) * out_t.astype(F32)
    query = qkv_ref[pl.ds(start, QB), :width] * jnp.asarray(HEAD_DIM**-0.5, BF)
    q_t = query.T
    inner = []
    for h in range(heads):
        part = slice(h * HEAD_DIM, (h + 1) * HEAD_DIM)
        inner.append(jnp.sum(product[part], axis=0, keepdims=True))
        qt_ref[h] = head_rows(q_t, h)
        gt_ref[h] = head_rows(grad_t, h)
        qs_ref[h * QB : (h + 1) * QB] = head_lanes(query, h)
        gs_ref[h * QB : (h + 1) * QB] = head_lanes(grad, h)
    dqt_ref[...] = jnp.zeros_like(dqt_ref)
    places = start + lax.broadcasted_iota(jnp.int32, (1, QB), 1)
    low, high = doc_bounds(sc, places)
    low_first, _ = doc_bounds(sc, start)

    def body(kb, carry):
        at = pl.multiple_of(kb * QB, QB)
        keys = qkv_ref[pl.ds(at, QB), width : 2 * width]
        values = qkv_ref[pl.ds(at, QB), 2 * width :]
        spot = at + lax.broadcasted_iota(jnp.int32, (QB, QB), 0)
        allowed = (spot >= low) & (spot <= high)
        all_probs, all_grads = [], []
        for h in range(heads):
            part = slice(h * HEAD_DIM, (h + 1) * HEAD_DIM)
            scores = jnp.where(allowed, dot(keys, qt_ref[h]), MASKED)
            probs = jnp.exp(scores - lse_ref[h : h + 1])
            grad_probs = dot(values, gt_ref[h])
            grad_scores = (probs * (grad_probs - inner[h])).astype(BF)
            all_probs.append(probs.astype(BF))
            all_grads.append(grad_scores)
            dqt_ref[part] += dot(kt_ref[part, pl.ds(at, QB)], grad_scores)
        dv_ref[pl.ds(at, QB)] += dot(jnp.concatenate(all_probs, axis=1), gs_ref[...])
        dk_ref[pl.ds(at, QB)] += dot(jnp.concatenate(all_grads, axis=1), qs_ref[...])
        return carry

    lax.fori_loop(low_first // QB, start // QB + 1, body, 0)
    dq = (dqt_ref[...] * HEAD_DIM**-0.5).T.astype(BF)
    if not last:
        dq_ref[...] = dq
    else:
        to = rows // 2 + step * QB
        mixed_ref[pl.ds(pl.multiple_of(to, QB), QB), :width] = dq

        @pl.when(step == 3)
        def _():
            for r in range(4):
                take = pl.ds(pl.multiple_of((sc[0] ^ r) * 2 * QB, QB), 2 * QB)
                put = slice(r * 2 * QB, (r + 1) * 2 * QB)
                mixed_ref[put, width : 2 * width] = dk_ref[take].astype(BF)
                mixed_ref[put, 2 * width :] = dv_ref[take].astype(BF)


def attend_back_call(sc, first, ga, gb, wo, qkv, heads_out, lse, earlier):
    rows, width = qkv.shape[0], qkv.shape[1] // 3
    heads = width // HEAD_DIM
    model = wo.shape[0]
    half = rows // 8
    last = earlier is not None
    pair = lambda which: pl.BlockSpec(
        (half, model), lambda i, sc: (jnp.clip(i - 2 * which, 0, 1), 0)
    )
    in_specs = [
        pair(0),
        pair(1),
        whole(wo.shape),
        whole(qkv.shape),
        pl.BlockSpec((half, width), lambda i, sc: (2 * first + i, 0)),
        pl.BlockSpec((8, half), lambda i, sc: (0, 2 * first + i)),
    ]
    sums = jax.ShapeDtypeStruct((rows, width), F32)
    scratch = [
        pltpu.VMEM((width, rows), BF),
        pltpu.VMEM((heads, width, QB), BF),
        pltpu.VMEM((heads, width, QB), BF),
        pltpu.VMEM((heads * QB, width), BF),
        pltpu.VMEM((heads * QB, width), BF),
        pltpu.VMEM((width, QB), F32),
    ]
    if last:
        in_specs += [whole((rows // 2, width)), whole((rows, width)), whole((rows, width))]
        out_shape = jax.ShapeDtypeStruct((rows, 3 * width), BF)
        out_specs = whole((rows, 3 * width))
        scratch = [pltpu.VMEM((rows, width), F32), pltpu.VMEM((rows, width), F32)] + scratch
    else:
        out_shape = [jax.ShapeDtypeStruct((rows // 2, width), BF), sums, sums]
        out_specs = [
            pl.BlockSpec((half, width), lambda i, sc: (i, 0)),
            whole((rows, width)),
            whole((rows, width)),
        ]
    return pl.pallas_call(
        functools.partial(attend_back_kernel, first, last, heads),
        grid_spec=pltpu.PrefetchScalarGridSpec(
            num_scalar_prefetch=1,
            grid=(4,),
            in_specs=in_specs,
            out_specs=out_specs,
            scratch_shapes=scratch,
        ),
        out_shape=out_shape,
        compiler_params=params(),
        cost_estimate=cost(12_000_000_000, 12_000_000),
        name="attend_back",
    )(sc, ga, gb, wo, qkv, heads_out, lse, *(earlier or ()))


def feed_kernel(na_ref, nb_ref, ca_ref, cb_ref, wg_ref, wu_ref, wd_ref, wgt_ref, wut_ref, wdt_ref, *rest):
    act_ref, gg_ref, gu_ref, nall_ref, call_ref, da_ref, db_ref, xa_ref, xb_ref = rest[-9:]
    step = pl.program_id(0)

    @pl.when(step < 2)
    def _():
        nall_ref[...] = na_ref[...]
        call_ref[...] = ca_ref[...]

    @pl.when(step >= 2)
    def _():
        nall_ref[...] = nb_ref[...]
        call_ref[...] = cb_ref[...]

    normed = nall_ref[...]
    gate = dot(normed, wg_ref[...])
    up = dot(normed, wu_ref[...])
    sig = jax.nn.sigmoid(gate)
    silu = gate * sig
    act = (silu * up).astype(BF)
    act_ref[...] = act
    grad_act = dot(call_ref[...], wd_ref[...])
    grad_gate = (grad_act * up * sig * (1.0 + gate * (1.0 - sig))).astype(BF)
    grad_up = (grad_act * silu).astype(BF)
    gg_ref[...] = grad_gate
    gu_ref[...] = grad_up
    back = (dot(grad_gate, wgt_ref[...]) + dot(grad_up, wut_ref[...])).astype(BF)
    down = dot(act, wdt_ref[...]).astype(BF)

    @pl.when(step < 2)
    def _():
        xa_ref[...] = back
        da_ref[...] = down

    @pl.when(step >= 2)
    def _():
        xb_ref[...] = back
        db_ref[...] = down


def feed_call(order, na, nb, ca, cb, weights, into):
    rows, model = na.shape
    half = rows // 2
    units = weights[0].shape[1]
    total = 4 * rows
    one = lambda shape: pl.BlockSpec(shape, lambda i: (0, 0))
    pair = lambda which: pl.BlockSpec((half, model), lambda i: (jnp.clip(i - 2 * which, 0, 1), 0))
    spot = lambda i: 2 * jnp.where(i < 2, order[0], order[1]) + i % 2
    place = lambda wide: pl.BlockSpec((half, wide), lambda i: (spot(i), 0))
    extra = [] if into is None else list(into)
    shape = lambda r, c: jax.ShapeDtypeStruct((r, c), BF)
    return pl.pallas_call(
        feed_kernel,
        grid=(4,),
        in_specs=[pair(0), pair(1), pair(0), pair(1)]
        + [one(w.shape) for w in weights]
        + [pl.BlockSpec(memory_space=pl.ANY)] * len(extra),
        out_specs=[place(units)] * 3 + [place(model)] * 2 + [pair(0), pair(1), pair(0), pair(1)],
        out_shape=[shape(total, units)] * 3 + [shape(total, model)] * 2 + [shape(rows, model)] * 4,
        input_output_aliases={10 + k: k for k in range(len(extra))},
        compiler_params=params(),
        cost_estimate=cost(6 * 2 * 2 * rows * model * units, 20_000_000),
        name="feed",
    )(na, nb, ca, cb, *weights, *extra)


LANES = 256
CHUNK = 1024


def hash_kernel(tables, base_ref, pack_ref, out_ref):
    table = base_ref[0] + pl.program_id(0)
    places = out_ref.shape[1]
    count = pack_ref.shape[1] // CHUNK

    def body(n, total):
        cut = pl.ds(pl.multiple_of(n * CHUNK, CHUNK), CHUNK)
        ids = pack_ref[pl.ds(table, 1), cut].astype(jnp.int32) - base_ref[1]
        weights = pack_ref[pl.ds(table + tables, 1), cut]
        high = lax.broadcasted_iota(jnp.int32, (places, CHUNK), 0) == (ids >> 8)
        low = lax.broadcasted_iota(jnp.int32, (LANES, CHUNK), 0) == (ids & (LANES - 1))
        high = jnp.where(high, 1.0, 0.0).astype(BF)
        low = jnp.where(low, weights, 0.0).astype(BF)
        return total + lax.dot_general(
            high, low, (((1,), (1,)), ((), ())), preferred_element_type=F32
        )

    total = lax.fori_loop(0, count, body, jnp.zeros((places, LANES), F32))
    out_ref[0] = total.astype(BF)


def hash_call(pack, tables, core, seq, places):
    mine = tables // 2
    return pl.pallas_call(
        functools.partial(hash_kernel, tables),
        grid_spec=pltpu.PrefetchScalarGridSpec(
            num_scalar_prefetch=1,
            grid=(mine,),
            in_specs=[whole(pack.shape)],
            out_specs=pl.BlockSpec((1, places, LANES), lambda i, sc: (i, 0, 0)),
        ),
        out_shape=jax.ShapeDtypeStruct((mine, places, LANES), BF),
        compiler_params=params(),
        cost_estimate=cost(20_000_000_000, 2_000_000),
        name="hash_sums",
    )(jnp.stack([core * mine, seq * places * LANES]).astype(jnp.int32), pack)


def spread_kernel(sc, em_ref, om_ref, es_ref, os_ref, out_ref, flat_ref):
    mine, places = em_ref.shape[1], em_ref.shape[2]
    odd = (pl.program_id(0) ^ sc[1]) % 2

    def put(m_ref, s_ref):
        for k in range(mine):
            for ref, first in ((m_ref, sc[0] * mine), (s_ref, (1 - sc[0]) * mine)):
                at = pl.multiple_of((first + k) * places, 8)
                flat_ref[pl.ds(at, places)] = ref[0, k].astype(F32)

    @pl.when(odd == 0)
    def _():
        put(em_ref, es_ref)

    @pl.when(odd == 1)
    def _():
        put(om_ref, os_ref)

    def body(n, carry):
        for u in range(8):
            row = n * 8 + u
            out_ref[:, pl.ds(pl.multiple_of(row * LANES, LANES), LANES)] = jnp.concatenate(
                [flat_ref[pl.ds(k * places + row, 1), :] for k in range(2 * mine)], axis=0
            )
        return carry

    lax.fori_loop(0, places // 8, body, 0)


def spread_call(even_mine, odd_mine, even_sib, odd_sib, core, seq, hash_rows):
    halves, mine, places, lanes = even_mine.shape
    piece = pl.BlockSpec((1, mine, places, lanes), lambda i, sc: ((i ^ sc[1]) // 2, 0, 0, 0))
    return pl.pallas_call(
        spread_kernel,
        grid_spec=pltpu.PrefetchScalarGridSpec(
            num_scalar_prefetch=1,
            grid=(2 * halves,),
            in_specs=[piece] * 4,
            out_specs=pl.BlockSpec((2 * mine, places * lanes), lambda i, sc: (0, i)),
            scratch_shapes=[pltpu.VMEM((2 * mine * places, lanes), F32)],
        ),
        out_shape=jax.ShapeDtypeStruct((2 * mine, hash_rows), F32),
        compiler_params=params(),
        cost_estimate=cost(1_000_000, 24_000_000),
        name="hash_spread",
    )(jnp.stack([core, seq]).astype(jnp.int32), even_mine, odd_mine, even_sib, odd_sib)


HASH_ROWS = 500002


def hash_tables(hash_ids, hash_weights, core, seq):
    tables = hash_ids.shape[0]
    seq_count = lax.axis_size("seq")
    per_seq = -(-HASH_ROWS // seq_count)
    places = -(-per_seq // (LANES * 8)) * 8
    blank = jnp.zeros((16 - 2 * tables, hash_ids.shape[1]), F32)
    pack = jnp.concatenate([hash_ids.astype(F32), hash_weights, blank], axis=0)
    pack = lax.all_gather(pack, ("seq", "tp"), axis=1, tiled=True)
    mine = hash_call(pack, tables, core, seq, places)
    even = jnp.stack([mine] + [flip(mine, "seq", 2 * j) for j in range(1, seq_count // 2)])
    odd = flip(even, "seq", 1)
    return spread_call(
        even, odd, flip(even, "tp", 1), flip(odd, "tp", 1), core, seq, HASH_ROWS
    )


def contract_rows(left, right):
    return lax.dot_general(
        left, right, (((0,), (0,)), ((), ())), preferred_element_type=F32
    )


def scatter_weights(grad, seq):
    count = lax.axis_size("seq")
    rows, wide = grad.shape
    parts = grad.astype(BF).reshape(count // 2, 2, rows // count, wide)
    bit = seq % 2
    keep = lax.dynamic_index_in_dim(parts, bit, 1, keepdims=False)
    send = lax.dynamic_index_in_dim(parts, 1 - bit, 1, keepdims=False)
    half = (keep.astype(F32) + flip(send, "seq", 1).astype(F32)).astype(BF)
    place = seq // 2
    total = lax.dynamic_index_in_dim(half, place, 0, keepdims=False).astype(F32)
    for j in range(1, count // 2):
        piece = lax.dynamic_index_in_dim(half, place ^ j, 0, keepdims=False)
        total = total + flip(piece, "seq", 2 * j).astype(F32)
    return total


def shards(
    latents_in,
    gain_one,
    w_qkv,
    w_out,
    gain_two,
    w_gate,
    w_up,
    w_down,
    cotangent,
    doc_lengths,
    valid_lengths,
    hash_ids,
    hash_weights,
):
    local_rows, model_width = latents_in.shape
    local_width = w_qkv.shape[2]
    rank = lax.axis_index("tp")
    seq = lax.axis_index("seq")
    core = rank % 2
    lengths, valid = doc_lengths[0], valid_lengths[0]
    start_one = lengths[0]
    start_two = lengths[0] + lengths[1]
    sc = jnp.stack(
        [rank, start_one, start_two, valid[0], start_one + valid[1], start_two + valid[2]]
    ).astype(jnp.int32)

    row_data = latents_in.astype(F32)
    normed, scale_one = norm_rows(row_data, gain_one)
    one = gather_rows(normed.astype(BF))
    qkv_weight = w_qkv.reshape(model_width, 3 * local_width)
    qkv = qkv_call(sc, 0, one[0], one[1], qkv_weight, None)
    qkv = qkv_call(sc, 2, one[2], one[3], qkv_weight, qkv)
    wo_t = w_out.T
    heads_out, lse, part_three, part_two = attend_call(sc, 2, qkv, wo_t, None, None)
    far = scatter_far(part_two, part_three)
    heads_out, lse, part_one, part_zero = attend_call(sc, 0, qkv, wo_t, heads_out, lse)
    hidden = row_data + scatter_sum(part_zero, part_one, far)
    normed_two, scale_two = norm_rows(hidden, gain_two)
    two = gather_rows(normed_two.astype(BF))
    cot = gather_rows(cotangent)
    weights = (w_gate, w_up, w_down, w_gate.T, w_up.T, w_down.T)
    *kept, down_zero, down_one, back_zero, back_one = feed_call(
        (0, 1), two[0], two[1], cot[0], cot[1], weights, None
    )
    *kept, down_three, down_two, back_three, back_two = feed_call(
        (3, 2), two[3], two[2], cot[3], cot[2], weights, kept
    )
    act, grad_gate, grad_up, two_all, cot_all = kept
    grad_normed_two = scatter_sum(back_zero, back_one, scatter_far(back_two, back_three))
    grad_hidden_norm, grad_gain_two = norm_back(hidden, scale_two, gain_two, grad_normed_two)
    grad_hidden = cotangent.astype(F32) + grad_hidden_norm
    branch = gather_rows(grad_hidden.astype(BF))
    early = attend_back_call(sc, 0, branch[0], branch[1], w_out, qkv, heads_out, lse, None)
    mixed = attend_back_call(sc, 2, branch[2], branch[3], w_out, qkv, heads_out, lse, early)
    qkv_weight_t = qkv_weight.T
    parts = [
        dot(mixed[r * local_rows : (r + 1) * local_rows], qkv_weight_t).astype(BF)
        for r in range(4)
    ]
    grad_normed = scatter_sum(parts[0], parts[1], scatter_far(parts[2], parts[3]))
    grad_rows_norm, grad_gain_one = norm_back(row_data, scale_one, gain_one, grad_normed)
    grad_latents = grad_hidden + grad_rows_norm

    down_total = scatter_weights(contract_rows(cot_all, act), seq)
    gate_total = scatter_weights(contract_rows(two_all, grad_gate), seq)
    up_total = scatter_weights(contract_rows(two_all, grad_up), seq)
    out_total = scatter_weights(contract_rows(jnp.concatenate(branch, axis=0), heads_out), seq)
    qkv_total = scatter_weights(contract_rows(jnp.concatenate(one, axis=0), mixed), seq)
    qkv_total = qkv_total.reshape(-1, 3, local_width)

    result = hidden + scatter_sum(down_zero, down_one, scatter_far(down_two, down_three))
    latents_out = result.astype(BF)
    gain_one_total, gain_two_total = lax.psum((grad_gain_one, grad_gain_two), ("seq", "tp"))
    hash_counts = hash_tables(hash_ids, hash_weights, core, seq)
    return (
        latents_out,
        grad_latents,
        gain_one_total,
        qkv_total,
        out_total,
        gain_two_total,
        gate_total,
        up_total,
        down_total,
        hash_counts,
    )


def solution(mesh):
    in_specs = (
        P(("seq", "tp"), None),
        P(),
        P(None, None, "tp"),
        P(None, "tp"),
        P(),
        P(None, "tp"),
        P(None, "tp"),
        P(None, "tp"),
        P(("seq", "tp"), None),
        P("seq", None),
        P("seq", None),
        P(None, ("seq", "tp")),
        P(None, ("seq", "tp")),
    )
    out_specs = (
        P(("seq", "tp"), None),
        P(("seq", "tp"), None),
        P(),
        P("seq", None, "tp"),
        P("seq", "tp"),
        P(),
        P("seq", "tp"),
        P("seq", "tp"),
        P("seq", "tp"),
        P(),
    )
    return jax.shard_map(shards, mesh=mesh, in_specs=in_specs, out_specs=out_specs, check_vma=False)
```

```python
import functools

import jax
import jax.numpy as jnp
from jax import lax
from jax.experimental import pallas as pl
from jax.experimental.pallas import tpu as pltpu
from jax.sharding import PartitionSpec as P

HEAD_DIM = 64
HASH_ROWS = 500002
EPSILON = 1e-05
MASKED = -1e30
BF = jnp.bfloat16
F32 = jnp.float32
QB = 256
LANES = 256
STEPS = 4
VMEM_BYTES = 60 * 1024 * 1024
MESH = pl.DeviceIdType.MESH


def flip(x, axis, bits):
    count = lax.axis_size(axis)
    return lax.ppermute(x, axis, [(i, i ^ bits) for i in range(count)])


def dot(a, b):
    return lax.dot_general(a, b, (((1,), (0,)), ((), ())), preferred_element_type=F32)


def dot_nt(a, b):
    return lax.dot_general(a, b, (((1,), (1,)), ((), ())), preferred_element_type=F32)


def dot_tn(a, b):
    return lax.dot_general(a, b, (((0,), (0,)), ((), ())), preferred_element_type=F32)


def cost(flops, moved):
    return pl.CostEstimate(flops=flops, bytes_accessed=moved, transcendentals=0)


def params(**more):
    return pltpu.CompilerParams(vmem_limit_bytes=VMEM_BYTES, **more)


def whole(shape):
    return pl.BlockSpec(shape, lambda i, sc: (0,) * len(shape))


VM = pl.BlockSpec(memory_space=pltpu.VMEM)
ANY = pl.BlockSpec(memory_space=pl.ANY)


def places():
    me = lax.axis_index("tp")
    core = lax.rem(me, 2)
    sib = me + 1 - 2 * core
    far = lax.rem(me + 2, 4)
    return me, sib, far, lax.rem(sib + 2, 4), core


def push(src, dst, send, recv, where):
    return pltpu.make_async_remote_copy(
        src_ref=src,
        dst_ref=dst,
        send_sem=send,
        recv_sem=recv,
        device_id={"seq": where[0], "tp": where[1]},
        device_id_type=MESH,
    )


def greet(others):
    barrier = pltpu.get_barrier_semaphore()
    for seq, tp in others:
        pl.semaphore_signal(
            barrier, inc=1, device_id={"seq": seq, "tp": tp}, device_id_type=MESH
        )
    pl.semaphore_wait(barrier, len(others))


def chunk(k, size):
    return pl.ds(pl.multiple_of(k * size, size), size)


def norm_rows(row_data, gain):
    scaling = lax.rsqrt(jnp.mean(row_data * row_data, axis=-1, keepdims=True) + EPSILON)
    return (row_data * scaling * gain, scaling)


def norm_back(row_data, scaling, gain, grad_norm):
    weighted = grad_norm * gain
    inner_mean = jnp.mean(weighted * row_data, axis=-1, keepdims=True)
    grad_rows = scaling * weighted - row_data * scaling * scaling * scaling * inner_mean
    grad_gain = jnp.sum(grad_norm * row_data * scaling, axis=0, keepdims=True)
    return (grad_rows, grad_gain)


def front_kernel(
    seq_count, tables, x_ref, gain_ref, w_ref, pair_ref, n_ref, qkv_ref, hash_ref,
    pack_ref, sum_ref, snd, rcv, psnd, prcv,
):
    me, sib, far, _, core = places()
    seq = lax.axis_index("seq")
    near = seq + 1 - 2 * lax.rem(seq, 2)
    parity, place, half = lax.rem(seq, 2), seq // 2, seq_count // 2
    level = [lax.rem(seq + 2 * j, seq_count) for j in range(1, half)]
    greet([(seq, sib), (seq, far), (near, me)] + [(s, me) for s in level])
    rows = x_ref.shape[0]
    size = rows // STEPS

    pack_ref[parity, place, me] = pair_ref[core]
    mine = pack_ref.at[parity, place, me]
    stage_sib = push(pair_ref.at[1 - core], mine, psnd.at[0], prcv.at[0], (seq, sib))
    stage_sib.start()
    both = pack_ref.at[parity, place, pl.ds(me - core, 2)]
    stage_far = push(both, both, psnd.at[1], prcv.at[1], (seq, far))
    four = pack_ref.at[parity, place]
    stage_level = [
        push(four, four, psnd.at[2 + j], prcv.at[2 + j], (s, me)) for j, s in enumerate(level)
    ]
    plane = pack_ref.at[parity]
    stage_near = push(plane, plane, psnd.at[half + 1], prcv.at[half + 1], (near, me))

    def own(kind, k, to, block):
        part = n_ref.at[block, chunk(k, size)]
        return push(part, part, snd.at[kind, k], rcv.at[kind, k], (seq, to))

    for k in range(STEPS):
        part = slice(k * size, (k + 1) * size)
        normed, _ = norm_rows(x_ref[part].astype(F32), gain_ref[...])
        n_ref[me, part] = normed.astype(BF)
        if k == 0:
            stage_sib.wait_recv()
            stage_far.start()
        own(1, k, far, me).start()
        own(0, k, sib, me).start()

    def project(block):
        def body(k, carry):
            part = chunk(k, rows // 2)
            qkv_ref[block, part] = dot(n_ref[block, part], w_ref[...]).astype(BF)
            return carry

        lax.fori_loop(0, 2, body, 0)

    project(me)
    stage_far.wait_recv()
    for copy in stage_level:
        copy.start()
    for k in range(STEPS):
        own(0, k, sib, me).wait_recv()
    project(sib)
    own(1, 0, far, me).wait_recv()
    own(2, 0, sib, far).start()
    for copy in stage_level:
        copy.wait_recv()
    stage_near.start()

    sum_ref[...] = jnp.zeros_like(sum_ref)
    high_rows = sum_ref.shape[1]
    first = seq * (high_rows * LANES)

    def sums(which):
        def body(n, carry):
            table, block = n // (half * 4), lax.rem(n, half * 4)
            pairs = pack_ref.at[which, block // 4, lax.rem(block, 4)]
            ids = pairs[pl.ds(table, 1)].astype(jnp.int32) - first
            weights = pairs[pl.ds(table + tables, 1)]
            high = lax.broadcasted_iota(jnp.int32, (high_rows, rows), 0) == (ids >> 8)
            low = lax.broadcasted_iota(jnp.int32, (LANES, rows), 0) == (ids & (LANES - 1))
            high = jnp.where(high, 1.0, 0.0).astype(BF)
            low = jnp.where(low, weights, 0.0).astype(BF)
            sum_ref[table] += dot_nt(high, low)
            return carry

        lax.fori_loop(0, tables * half * 4, body, 0)

    sums(parity)
    for k in range(1, STEPS):
        own(1, k, far, me).wait_recv()
        own(2, k, sib, far).start()
    stage_near.wait_recv()
    sums(1 - parity)
    hash_ref[...] = sum_ref[...].astype(BF)
    project(far)
    for k in range(STEPS):
        own(2, k, sib, far).wait_recv()
    project(lax.rem(sib + 2, 4))
    for k in range(STEPS):
        for kind in range(3):
            own(kind, k, sib, me).wait_send()
    stage_sib.wait_send()
    stage_far.wait_send()
    for copy in stage_level:
        copy.wait_send()
    stage_near.wait_send()


def front_call(x, gain, w, pairs, high_rows):
    seq_count = lax.axis_size("seq")
    rows, model = x.shape
    tables = 3
    half = seq_count // 2
    dma = pltpu.SemaphoreType.DMA
    return pl.pallas_call(
        functools.partial(front_kernel, seq_count, tables),
        in_specs=[VM] * 4,
        out_specs=[VM] * 3,
        out_shape=[
            jax.ShapeDtypeStruct((4, rows, model), BF),
            jax.ShapeDtypeStruct((4, rows, w.shape[1]), BF),
            jax.ShapeDtypeStruct((tables, high_rows, LANES), BF),
        ],
        scratch_shapes=[
            pltpu.VMEM((2, half, 4, 8, rows), F32),
            pltpu.VMEM((tables, high_rows, LANES), F32),
            dma((3, STEPS)),
            dma((3, STEPS)),
            dma((half + 2,)),
            dma((half + 2,)),
        ],
        compiler_params=params(collective_id=0, has_side_effects=True),
        cost_estimate=cost(30_000_000_000, 10_000_000),
        name="front",
    )(x, gain, w, pairs)


def doc_bounds(sc, places):
    low = jnp.where(places >= sc[2], sc[2], jnp.where(places >= sc[1], sc[1], 0))
    end = jnp.where(places >= sc[2], sc[5], jnp.where(places >= sc[1], sc[4], sc[3]))
    return low, jnp.minimum(places, end - 1)


def head_rows(x, h):
    where = lax.broadcasted_iota(jnp.int32, x.shape, 0) // HEAD_DIM
    return jnp.where(where == h, x, jnp.zeros_like(x))


def head_lanes(x, h):
    where = lax.broadcasted_iota(jnp.int32, x.shape, 1) // HEAD_DIM
    return jnp.where(where == h, x, jnp.zeros_like(x))


def attend_kernel(heads, sc, qkv_ref, heads_ref, lse_ref, vt_ref, qt_ref, acc_ref):
    width = heads * HEAD_DIM
    step = pl.program_id(0)

    @pl.when(step == 0)
    def _():
        for n in range(qkv_ref.shape[0] // QB):
            vt_ref[:, n * QB : (n + 1) * QB] = qkv_ref[n * QB : (n + 1) * QB, 2 * width :].T

    start = pl.multiple_of(step * QB, QB)
    q_t = qkv_ref[pl.ds(start, QB), :width].T * jnp.asarray(HEAD_DIM**-0.5, BF)
    for h in range(heads):
        qt_ref[h] = head_rows(q_t, h)
    acc_ref[...] = jnp.zeros_like(acc_ref)
    places = start + lax.broadcasted_iota(jnp.int32, (1, QB), 1)
    low, high = doc_bounds(sc, places)
    low_first, _ = doc_bounds(sc, start)

    def body(kb, state):
        at = pl.multiple_of(kb * QB, QB)
        keys = qkv_ref[pl.ds(at, QB), width : 2 * width]
        value_t = vt_ref[:, pl.ds(at, QB)]
        spot = at + lax.broadcasted_iota(jnp.int32, (QB, QB), 0)
        allowed = (spot >= low) & (spot <= high)
        fresh = []
        for h in range(heads):
            top, total = state[h]
            scores = jnp.where(allowed, dot(keys, qt_ref[h]), MASKED)
            new_top = jnp.maximum(top, jnp.max(scores, axis=0, keepdims=True))
            fade = jnp.exp(top - new_top)
            probs = jnp.exp(scores - new_top)
            total = total * fade + jnp.sum(probs, axis=0, keepdims=True)
            part = slice(h * HEAD_DIM, (h + 1) * HEAD_DIM)
            acc_ref[part] = acc_ref[part] * fade + dot(value_t[part], probs.astype(BF))
            fresh.append((new_top, total))
        return tuple(fresh)

    begin = tuple(
        (jnp.full((1, QB), MASKED, F32), jnp.zeros((1, QB), F32)) for _ in range(heads)
    )
    state = lax.fori_loop(low_first // QB, start // QB + 1, body, begin)
    lse_ref[...] = jnp.zeros_like(lse_ref)
    for h in range(heads):
        top, total = state[h]
        part = slice(h * HEAD_DIM, (h + 1) * HEAD_DIM)
        acc_ref[part] = acc_ref[part] * (1.0 / total)
        lse_ref[h : h + 1] = top + jnp.log(total)
    heads_ref[...] = acc_ref[...].T.astype(BF)


def attend_call(sc, qkv):
    rows, width = qkv.shape[0], qkv.shape[1] // 3
    heads = width // HEAD_DIM
    return pl.pallas_call(
        functools.partial(attend_kernel, heads),
        grid_spec=pltpu.PrefetchScalarGridSpec(
            num_scalar_prefetch=1,
            grid=(rows // QB,),
            in_specs=[whole(qkv.shape)],
            out_specs=[
                pl.BlockSpec((QB, width), lambda i, sc: (i, 0)),
                pl.BlockSpec((8, QB), lambda i, sc: (0, i)),
            ],
            scratch_shapes=[
                pltpu.VMEM((width, rows), BF),
                pltpu.VMEM((heads, width, QB), BF),
                pltpu.VMEM((width, QB), F32),
            ],
        ),
        out_shape=[
            jax.ShapeDtypeStruct((rows, width), BF),
            jax.ShapeDtypeStruct((8, rows), F32),
        ],
        compiler_params=params(),
        cost_estimate=cost(35_000_000_000, 8_000_000),
        name="attend",
    )(sc, qkv)


def attend_back_kernel(
    heads, sc, grad_ref, wo_ref, qkv_ref, heads_ref, lse_ref, mixed_ref,
    kt_ref, qt_ref, gt_ref, qs_ref, gs_ref, dqt_ref, dk_ref, dv_ref,
):
    width = heads * HEAD_DIM
    step = pl.program_id(0)
    rows = qkv_ref.shape[0]

    @pl.when(step == 0)
    def _():
        for n in range(rows // QB):
            kt_ref[:, n * QB : (n + 1) * QB] = qkv_ref[n * QB : (n + 1) * QB, width : 2 * width].T
        dk_ref[...] = jnp.zeros_like(dk_ref)
        dv_ref[...] = jnp.zeros_like(dv_ref)

    start = pl.multiple_of(step * QB, QB)
    grad = dot(grad_ref[...], wo_ref[...]).astype(BF)
    grad_t = grad.T
    out_t = heads_ref[...].T
    product = grad_t.astype(F32) * out_t.astype(F32)
    query = qkv_ref[pl.ds(start, QB), :width] * jnp.asarray(HEAD_DIM**-0.5, BF)
    q_t = query.T
    inner = []
    for h in range(heads):
        part = slice(h * HEAD_DIM, (h + 1) * HEAD_DIM)
        inner.append(jnp.sum(product[part], axis=0, keepdims=True))
        qt_ref[h] = head_rows(q_t, h)
        gt_ref[h] = head_rows(grad_t, h)
        qs_ref[h * QB : (h + 1) * QB] = head_lanes(query, h)
        gs_ref[h * QB : (h + 1) * QB] = head_lanes(grad, h)
    dqt_ref[...] = jnp.zeros_like(dqt_ref)
    places = start + lax.broadcasted_iota(jnp.int32, (1, QB), 1)
    low, high = doc_bounds(sc, places)
    low_first, _ = doc_bounds(sc, start)

    def body(kb, carry):
        at = pl.multiple_of(kb * QB, QB)
        keys = qkv_ref[pl.ds(at, QB), width : 2 * width]
        values = qkv_ref[pl.ds(at, QB), 2 * width :]
        spot = at + lax.broadcasted_iota(jnp.int32, (QB, QB), 0)
        allowed = (spot >= low) & (spot <= high)
        all_probs, all_grads = [], []
        for h in range(heads):
            part = slice(h * HEAD_DIM, (h + 1) * HEAD_DIM)
            scores = jnp.where(allowed, dot(keys, qt_ref[h]), MASKED)
            probs = jnp.exp(scores - lse_ref[h : h + 1])
            grad_probs = dot(values, gt_ref[h])
            grad_scores = (probs * (grad_probs - inner[h])).astype(BF)
            all_probs.append(probs.astype(BF))
            all_grads.append(grad_scores)
            dqt_ref[part] += dot(kt_ref[part, pl.ds(at, QB)], grad_scores)
        dv_ref[pl.ds(at, QB)] += dot(jnp.concatenate(all_probs, axis=1), gs_ref[...])
        dk_ref[pl.ds(at, QB)] += dot(jnp.concatenate(all_grads, axis=1), qs_ref[...])
        return carry

    lax.fori_loop(low_first // QB, start // QB + 1, body, 0)
    dq = (dqt_ref[...] * HEAD_DIM**-0.5).T.astype(BF)
    mixed_ref[pl.ds(start, QB), :width] = dq

    @pl.when(step == pl.num_programs(0) - 1)
    def _():
        mixed_ref[:, width : 2 * width] = dk_ref[...].astype(BF)
        mixed_ref[:, 2 * width :] = dv_ref[...].astype(BF)


def attend_back_call(sc, grad, wo, qkv, heads_out, lse):
    rows, width = qkv.shape[0], qkv.shape[1] // 3
    heads = width // HEAD_DIM
    model = wo.shape[0]
    return pl.pallas_call(
        functools.partial(attend_back_kernel, heads),
        grid_spec=pltpu.PrefetchScalarGridSpec(
            num_scalar_prefetch=1,
            grid=(rows // QB,),
            in_specs=[
                pl.BlockSpec((QB, model), lambda i, sc: (i, 0)),
                whole(wo.shape),
                whole(qkv.shape),
                pl.BlockSpec((QB, width), lambda i, sc: (i, 0)),
                pl.BlockSpec((8, QB), lambda i, sc: (0, i)),
            ],
            out_specs=whole((rows, 3 * width)),
            scratch_shapes=[
                pltpu.VMEM((width, rows), BF),
                pltpu.VMEM((heads, width, QB), BF),
                pltpu.VMEM((heads, width, QB), BF),
                pltpu.VMEM((heads * QB, width), BF),
                pltpu.VMEM((heads * QB, width), BF),
                pltpu.VMEM((width, QB), F32),
                pltpu.VMEM((rows, width), F32),
                pltpu.VMEM((rows, width), F32),
            ],
        ),
        out_shape=jax.ShapeDtypeStruct((rows, 3 * width), BF),
        compiler_params=params(),
        cost_estimate=cost(45_000_000_000, 12_000_000),
        name="attend_back",
    )(sc, grad, wo, qkv, heads_out, lse)


def middle_kernel(
    seq_count, heads_ref, wo_ref, x_ref, gain_ref, c0, c1, c2, c3, wg_ref, wu_ref, wd_ref,
    rest_ref, fardown_ref, grad_ref, gain_out, branch_ref,
    keep_ref, got_ref,
    n_ref, act_ref, gg_ref, gu_ref, g0_ref, g1s_ref, g1r_ref, d0_ref, d1s_ref, d1r_ref,
    d3s_ref, d3r_ref, as_ref, ar_ref, ys_ref, yr_ref, bs_ref, br_ref, gb_ref, dw_ref,
    snd, rcv, xsnd, xrcv, loc, wloc,
):
    me, sib, far, farsib, core = places()
    seq = lax.axis_index("seq")
    near = seq + 1 - 2 * lax.rem(seq, 2)
    greet([(seq, sib), (seq, far), (near, me)])
    rows, model = x_ref.shape
    size = rows // STEPS
    half = seq_count // 2
    units = keep_ref.shape[-1]

    def copy(kind, k, src, dst, to):
        return push(
            src.at[chunk(k, size)], dst.at[chunk(k, size)], snd.at[kind, k], rcv.at[kind, k], (seq, to)
        )

    def block_copy(kind, k, ref, block, to):
        part = ref.at[block, chunk(k, size)]
        return push(part, part, snd.at[kind, k], rcv.at[kind, k], (seq, to))

    proj_a = lambda k: copy(0, k, as_ref, ar_ref, sib)
    proj_y = lambda k: copy(1, k, ys_ref, yr_ref, far)
    proj_b = lambda k: copy(2, k, bs_ref, br_ref, sib)
    two_sib = lambda k: block_copy(3, k, n_ref, me, sib)
    two_far = lambda k: block_copy(4, k, n_ref, me, far)
    two_on = lambda k: block_copy(5, k, n_ref, far, sib)
    back_one = lambda k: copy(6, k, g1s_ref, g1r_ref, sib)
    down_one = lambda k: copy(7, k, d1s_ref, d1r_ref, sib)
    back_a = lambda k: copy(8, k, as_ref, ar_ref, sib)
    back_y = lambda k: copy(9, k, ys_ref, yr_ref, far)
    down_three = lambda k: copy(10, k, d3s_ref, d3r_ref, sib)
    branch_on = lambda k: block_copy(13, k, branch_ref, far, sib)

    def branch_out(kind, k, to):
        return push(
            gb_ref.at[chunk(k, size)], branch_ref.at[me, chunk(k, size)],
            snd.at[kind, k], rcv.at[kind, k], (seq, to),
        )

    def branch_home(k):
        return pltpu.make_async_copy(
            gb_ref.at[chunk(k, size)], branch_ref.at[me, chunk(k, size)], loc.at[k]
        )

    def each(body, count=STEPS):
        lax.fori_loop(0, count, lambda k, c: (body(k), c)[1], 0)

    def project(block, k):
        return dot(heads_ref[block, chunk(k, size)], wo_ref[...])

    def send_three(k):
        as_ref[chunk(k, size)] = project(farsib, k).astype(BF)
        proj_a(k).start()

    def send_two(k):
        part = project(far, k)
        proj_a(k).wait_recv()
        ys_ref[chunk(k, size)] = (part + ar_ref[chunk(k, size)].astype(F32)).astype(BF)
        proj_y(k).start()

    def send_one(k):
        bs_ref[chunk(k, size)] = project(sib, k).astype(BF)
        proj_b(k).start()

    each(send_three)
    each(send_two)
    each(send_one)

    def feed(k, block_a, block_b, ca, cb):
        part = chunk(k, size)
        normed = jnp.concatenate([n_ref[block_a, part], n_ref[block_b, part]], axis=0)
        cot = jnp.concatenate([ca[part], cb[part]], axis=0)
        gate = dot(normed, wg_ref[...])
        up = dot(normed, wu_ref[...])
        sig = jax.nn.sigmoid(gate)
        silu = gate * sig
        act = (silu * up).astype(BF)
        grad_act = dot(cot, wd_ref[...])
        grad_gate = (grad_act * up * sig * (1.0 + gate * (1.0 - sig))).astype(BF)
        grad_up = (grad_act * silu).astype(BF)
        for ref, value in ((act_ref, act), (gg_ref, grad_gate), (gu_ref, grad_up)):
            ref[block_a, part] = value[:size]
            ref[block_b, part] = value[size:]
        back = dot_nt(grad_gate, wg_ref[...]) + dot_nt(grad_up, wu_ref[...])
        return back, dot_nt(act, wd_ref[...])

    def own_chunk(k):
        part = chunk(k, size)
        total = x_ref[part].astype(F32) + project(me, k)
        proj_b(k).wait_recv()
        proj_y(k).wait_recv()
        hidden = total + br_ref[part].astype(F32) + yr_ref[part].astype(F32)
        rest_ref[part] = hidden
        normed, _ = norm_rows(hidden, gain_ref[...])
        n_ref[me, part] = normed.astype(BF)
        two_far(k).start()
        two_sib(k).start()
        two_sib(k).wait_recv()
        back, down = feed(k, me, sib, c0, c1)
        g0_ref[part] = back[:size].astype(BF)
        g1s_ref[part] = back[size:].astype(BF)
        back_one(k).start()
        d0_ref[part] = down[:size].astype(BF)
        d1s_ref[part] = down[size:].astype(BF)
        down_one(k).start()

    each(own_chunk)

    def settle(k):
        proj_a(k).wait_send()
        proj_y(k).wait_send()

    each(settle)

    def far_sum(k):
        part = chunk(k, size)
        back_a(k).wait_recv()
        ys_ref[part] = (ys_ref[part].astype(F32) + ar_ref[part].astype(F32)).astype(BF)
        back_y(k).start()

    def far_chunk(k):
        part = chunk(k, size)
        two_far(k).wait_recv()
        two_on(k).start()

        @pl.when(k > 0)
        def _():
            far_sum(k - 1)

        two_on(k).wait_recv()
        back, down = feed(k, far, farsib, c2, c3)
        as_ref[part] = back[size:].astype(BF)
        back_a(k).start()
        ys_ref[part] = back[:size].astype(BF)
        d3s_ref[part] = down[size:].astype(BF)
        down_three(k).start()
        fardown_ref[part] = down[:size].astype(BF)

    each(far_chunk)
    far_sum(STEPS - 1)

    parity = lax.rem(seq, 2)
    piece = model // seq_count

    def weight_home(w, b):
        return pltpu.make_async_copy(
            dw_ref.at[w, 0, b], keep_ref.at[b, w], wloc.at[w, b]
        )

    def weight_away(w, b):
        return push(
            dw_ref.at[w, 1, b], got_ref.at[b, w], xsnd.at[w, b], xrcv.at[w, b], (near, me)
        )

    def weight_tile(w, k):
        cots = (c0, c1, c2, c3)
        order = (me, sib, far, farsib)
        right = (act_ref, gg_ref, gu_ref)[w]
        span = model // STEPS
        total = None
        for r in range(4):
            cols = chunk(k, span)
            left = cots[r][:, cols] if w == 0 else n_ref[order[r], :, cols]
            term = dot_tn(left, right[order[r]])
            total = term if total is None else total + term
        total = total[:, :units].astype(BF).reshape(span // (2 * piece), 2, piece, units)
        return total

    def weights_step(k):
        per = model // STEPS // (2 * piece)
        for w in range(3):
            tile = weight_tile(w, k)
            for j in range(per):
                b = k * per + j

                @pl.when(parity == 0)
                def _():
                    dw_ref[w, 0, b] = tile[j, 0]
                    dw_ref[w, 1, b] = tile[j, 1]

                @pl.when(parity == 1)
                def _():
                    dw_ref[w, 0, b] = tile[j, 1]
                    dw_ref[w, 1, b] = tile[j, 0]

                weight_home(w, b).start()
                weight_away(w, b).start()

    gain_out[...] = jnp.zeros_like(gain_out)

    def back_chunk(k):
        weights_step(k)
        part = chunk(k, size)
        back_one(k).wait_recv()
        back_y(k).wait_recv()
        grad_norm = g0_ref[part].astype(F32) + g1r_ref[part].astype(F32) + yr_ref[part].astype(F32)
        hidden = rest_ref[part]
        _, scaling = norm_rows(hidden, gain_ref[...])
        grad_rows, grad_gain = norm_back(hidden, scaling, gain_ref[...], grad_norm)
        grad = c0[part].astype(F32) + grad_rows
        grad_ref[part] = grad
        gain_out[...] += grad_gain
        gb_ref[part] = grad.astype(BF)
        branch_out(12, k, far).start()
        branch_out(11, k, sib).start()
        branch_home(k).start()

    each(back_chunk)

    def finish(k):
        part = chunk(k, size)
        down_one(k).wait_recv()
        down_three(k).wait_recv()
        rest_ref[part] += d0_ref[part].astype(F32) + d1r_ref[part].astype(F32)
        fardown_ref[part] = (fardown_ref[part].astype(F32) + d3r_ref[part].astype(F32)).astype(BF)
        branch_out(12, k, far).wait_recv()
        branch_on(k).start()

    each(finish)

    def close(k):
        branch_out(11, k, sib).wait_recv()
        branch_on(k).wait_recv()
        branch_home(k).wait()
        for made in (
            proj_b, two_sib, two_far, two_on, back_one, down_one, back_a, back_y, down_three, branch_on,
        ):
            made(k).wait_send()
        branch_out(11, k, sib).wait_send()
        branch_out(12, k, far).wait_send()

    each(close)

    def close_weights(b):
        for w in range(3):
            weight_home(w, b).wait()
            weight_away(w, b).wait_recv()
            weight_away(w, b).wait_send()

    each(close_weights, half)


def middle_call(heads_out, wo_t, x, gain, cots, weights, units):
    seq_count = lax.axis_size("seq")
    rows, model = x.shape
    half = seq_count // 2
    piece = model // seq_count
    wide = weights[0].shape[1]
    dma = pltpu.SemaphoreType.DMA
    shape = jax.ShapeDtypeStruct
    part = shape((half, 3, piece, units), BF)
    rows_bf = pltpu.VMEM((rows, model), BF)
    return pl.pallas_call(
        functools.partial(middle_kernel, seq_count),
        in_specs=[VM] * 11,
        out_specs=[VM] * 4 + [ANY] * 3,
        out_shape=[
            shape((rows, model), F32),
            shape((rows, model), BF),
            shape((rows, model), F32),
            shape((1, model), F32),
            shape((4, rows, model), BF),
        ]
        + [part] * 2,
        scratch_shapes=[pltpu.VMEM((4, rows, model), BF)]
        + [pltpu.VMEM((4, rows, wide), BF)] * 3
        + [rows_bf] * 15
        + [pltpu.VMEM((3, 2, half, piece, units), BF)]
        + [
            dma((14, STEPS)),
            dma((14, STEPS)),
            dma((3, half)),
            dma((3, half)),
            dma((STEPS,)),
            dma((3, half)),
        ],
        compiler_params=params(collective_id=1, has_side_effects=True),
        cost_estimate=cost(100_000_000_000, 30_000_000),
        name="middle",
    )(heads_out, wo_t, x, gain, *cots, *weights)


def last_kernel(
    seq_count, mixed_ref, w_ref, x_ref, gain_ref, grad_ref, n_ref, heads_ref, branch_ref, gain_in,
    out_ref, wqkv_ref, wout_ref, gains_ref,
    as_ref, ar_ref, ys_ref, yr_ref, bs_ref, br_ref, dw_ref, got_ref, sum_ref, zr_ref, gs_ref, gr_ref,
    snd, rcv, xsnd, xrcv, zsnd, zrcv, gsnd, grcv,
):
    me, sib, far, farsib, core = places()
    seq = lax.axis_index("seq")
    parity, place, half = lax.rem(seq, 2), seq // 2, seq_count // 2
    near = seq + 1 - 2 * parity
    level = [lax.rem(seq + 2 * j, seq_count) for j in range(1, half)]
    greet([(seq, sib), (seq, far), (near, me)] + [(s, me) for s in level])
    rows, model = x_ref.shape
    size = rows // STEPS
    piece = model // seq_count
    wide = mixed_ref.shape[-1]

    def copy(kind, k, src, dst, to):
        return push(
            src.at[chunk(k, size)], dst.at[chunk(k, size)], snd.at[kind, k], rcv.at[kind, k], (seq, to)
        )

    back_a = lambda k: copy(0, k, as_ref, ar_ref, sib)
    back_y = lambda k: copy(1, k, ys_ref, yr_ref, far)
    back_b = lambda k: copy(2, k, bs_ref, br_ref, sib)

    def near_copy(b):
        return push(dw_ref.at[1, b], got_ref.at[b], xsnd.at[b], xrcv.at[b], (near, me))

    def level_copy(j):
        b = lax.rem(place + j, half)
        return push(sum_ref.at[b], zr_ref.at[j], zsnd.at[j], zrcv.at[j], (level[j - 1], me))

    def each(body, count=STEPS):
        lax.fori_loop(0, count, lambda k, c: (body(k), c)[1], 0)

    def project(block, k):
        return dot_nt(mixed_ref[block, chunk(k, size)], w_ref[...])

    def send_three(k):
        as_ref[chunk(k, size)] = project(farsib, k).astype(BF)
        back_a(k).start()

    def send_two(k):
        part = project(far, k)
        back_a(k).wait_recv()
        ys_ref[chunk(k, size)] = (part + ar_ref[chunk(k, size)].astype(F32)).astype(BF)
        back_y(k).start()

    def send_one(k):
        bs_ref[chunk(k, size)] = project(sib, k).astype(BF)
        back_b(k).start()

    span = model // STEPS
    per = span // (2 * piece)

    def weights_step(k):
        cols = chunk(k, span)
        to_qkv, to_out = None, None
        for r in range(4):
            term = dot_tn(n_ref[r, :, cols], mixed_ref[r])
            to_qkv = term if to_qkv is None else to_qkv + term
            term = dot_tn(branch_ref[r, :, cols], heads_ref[r])
            to_out = term if to_out is None else to_out + term
        for ref_at, value in ((slice(0, wide), to_qkv), (slice(wide, None), to_out)):
            tile = value.astype(BF).reshape(per, 2, piece, value.shape[1])
            for j in range(per):
                b = k * per + j

                @pl.when(parity == 0)
                def _():
                    dw_ref[0, b, :, ref_at] = tile[j, 0]
                    dw_ref[1, b, :, ref_at] = tile[j, 1]

                @pl.when(parity == 1)
                def _():
                    dw_ref[0, b, :, ref_at] = tile[j, 1]
                    dw_ref[1, b, :, ref_at] = tile[j, 0]

        for j in range(per):
            near_copy(k * per + j).start()

    each(send_three)
    each(send_two)
    each(weights_step)
    each(send_one)

    gs_ref[...] = jnp.zeros_like(gs_ref)

    def own_chunk(k):
        part = chunk(k, size)
        total = project(me, k)
        x = x_ref[part].astype(F32)
        _, scaling = norm_rows(x, gain_ref[...])
        back_b(k).wait_recv()
        back_y(k).wait_recv()
        grad_norm = total + br_ref[part].astype(F32) + yr_ref[part].astype(F32)
        grad_rows, grad_gain = norm_back(x, scaling, gain_ref[...], grad_norm)
        out_ref[part] = grad_ref[part] + grad_rows
        gs_ref[0, 0:1] += grad_gain

    def near_sum(b):
        near_copy(b).wait_recv()
        sum_ref[b] = (dw_ref[0, b].astype(F32) + got_ref[b].astype(F32)).astype(BF)

    def both(k):
        own_chunk(k)
        for j in range(half // STEPS):
            near_sum(k * (half // STEPS) + j)

    each(both)
    for j in range(1, half):
        level_copy(j).start()

    gs_ref[0, 1:2] = gain_in[...]
    others = [(seq, sib), (seq, far), (near, me)]

    def gain_copy(n, slot, to):
        return push(gs_ref.at[n], gr_ref.at[slot], gsnd.at[slot], grcv.at[slot], to)

    for n, to in enumerate(others):
        gain_copy(n, n, to).start()
        gain_copy(n, n, to).wait_recv()
        gs_ref[n + 1] = gs_ref[n] + gr_ref[n]
    for j in range(1, half):
        gain_copy(3, 2 + j, (level[j - 1], me)).start()
    gains = gs_ref[3]
    for j in range(1, half):
        gain_copy(3, 2 + j, (level[j - 1], me)).wait_recv()
        gains = gains + gr_ref[2 + j]
    gains_ref[...] = gains

    total = sum_ref[place].astype(F32)
    for j in range(1, half):
        level_copy(j).wait_recv()
        total = total + zr_ref[j].astype(F32)
    wqkv_ref[...] = total[:, :wide]
    wout_ref[...] = total[:, wide:]

    def close(k):
        for made in (back_a, back_y, back_b):
            made(k).wait_send()

    each(close)
    each(lambda b: near_copy(b).wait_send(), half)
    for n, to in enumerate(others):
        gain_copy(n, n, to).wait_send()
    for j in range(1, half):
        gain_copy(3, 2 + j, (level[j - 1], me)).wait_send()
        level_copy(j).wait_send()


def last_call(mixed, w, x, gain, grad, normed, heads_out, branch, gain_two):
    seq_count = lax.axis_size("seq")
    rows, model = x.shape
    half = seq_count // 2
    piece = model // seq_count
    wide, width = mixed.shape[-1], heads_out.shape[-1]
    dma = pltpu.SemaphoreType.DMA
    shape = jax.ShapeDtypeStruct
    rows_bf = pltpu.VMEM((rows, model), BF)
    pieces = pltpu.VMEM((half, piece, wide + width), BF)
    return pl.pallas_call(
        functools.partial(last_kernel, seq_count),
        in_specs=[VM] * 9,
        out_specs=[VM] * 4,
        out_shape=[
            shape((rows, model), F32),
            shape((piece, wide), F32),
            shape((piece, width), F32),
            shape((8, model), F32),
        ],
        scratch_shapes=[rows_bf] * 6
        + [pltpu.VMEM((2, half, piece, wide + width), BF), pieces, pieces, pieces]
        + [pltpu.VMEM((4, 8, model), F32), pltpu.VMEM((half + 2, 8, model), F32)]
        + [
            dma((3, STEPS)),
            dma((3, STEPS)),
            dma((half,)),
            dma((half,)),
            dma((half,)),
            dma((half,)),
            dma((half + 2,)),
            dma((half + 2,)),
        ],
        compiler_params=params(collective_id=2, has_side_effects=True),
        cost_estimate=cost(60_000_000_000, 30_000_000),
        name="last",
    )(mixed, w, x, gain, grad, normed, heads_out, branch, gain_two)


def spread_kernel(sc, em_ref, om_ref, es_ref, os_ref, out_ref, flat_ref):
    mine, places = em_ref.shape[1], em_ref.shape[2]
    odd = (pl.program_id(0) ^ sc[1]) % 2

    def put(m_ref, s_ref):
        for k in range(mine):
            for ref, first in ((m_ref, sc[0] * mine), (s_ref, (1 - sc[0]) * mine)):
                at = pl.multiple_of((first + k) * places, 8)
                flat_ref[pl.ds(at, places)] = ref[0, k].astype(F32)

    @pl.when(odd == 0)
    def _():
        put(em_ref, es_ref)

    @pl.when(odd == 1)
    def _():
        put(om_ref, os_ref)

    def body(n, carry):
        for u in range(8):
            row = n * 8 + u
            out_ref[:, pl.ds(pl.multiple_of(row * LANES, LANES), LANES)] = jnp.concatenate(
                [flat_ref[pl.ds(k * places + row, 1), :] for k in range(2 * mine)], axis=0
            )
        return carry

    lax.fori_loop(0, places // 8, body, 0)


def spread_call(even_mine, odd_mine, even_sib, odd_sib, core, seq, hash_rows):
    halves, mine, places, lanes = even_mine.shape
    piece = pl.BlockSpec((1, mine, places, lanes), lambda i, sc: ((i ^ sc[1]) // 2, 0, 0, 0))
    return pl.pallas_call(
        spread_kernel,
        grid_spec=pltpu.PrefetchScalarGridSpec(
            num_scalar_prefetch=1,
            grid=(2 * halves,),
            in_specs=[piece] * 4,
            out_specs=pl.BlockSpec((2 * mine, places * lanes), lambda i, sc: (0, i)),
            scratch_shapes=[pltpu.VMEM((2 * mine * places, lanes), F32)],
        ),
        out_shape=jax.ShapeDtypeStruct((2 * mine, hash_rows), F32),
        compiler_params=params(),
        cost_estimate=cost(1_000_000, 24_000_000),
        name="hash_spread",
    )(jnp.stack([core, seq]).astype(jnp.int32), even_mine, odd_mine, even_sib, odd_sib)


def spread_tables(mine, core, seq):
    seq_count = lax.axis_size("seq")
    even = jnp.stack([mine] + [flip(mine, "seq", 2 * j) for j in range(1, seq_count // 2)])
    odd = flip(even, "seq", 1)
    return spread_call(
        even, odd, flip(even, "tp", 1), flip(odd, "tp", 1), core, seq, HASH_ROWS
    )


def shards(
    latents_in,
    gain_one,
    w_qkv,
    w_out,
    gain_two,
    w_gate,
    w_up,
    w_down,
    cotangent,
    doc_lengths,
    valid_lengths,
    hash_ids,
    hash_weights,
):
    local_rows, model_width = latents_in.shape
    local_width = w_qkv.shape[2]
    group_rows = 4 * local_rows
    units = w_gate.shape[1]
    rank = lax.axis_index("tp")
    seq = lax.axis_index("seq")
    core = rank % 2
    seq_count = lax.axis_size("seq")
    lengths, valid = doc_lengths[0], valid_lengths[0]
    start_one = lengths[0]
    start_two = lengths[0] + lengths[1]
    sc = jnp.stack(
        [rank, start_one, start_two, valid[0], start_one + valid[1], start_two + valid[2]]
    ).astype(jnp.int32)
    gain_one, gain_two = gain_one[None], gain_two[None]

    tables = hash_ids.shape[0] // 2
    blank = jnp.zeros((8 - 2 * tables, local_rows), F32)
    pairs = jnp.stack(
        [
            jnp.concatenate(
                [
                    hash_ids[c * tables : (c + 1) * tables].astype(F32),
                    hash_weights[c * tables : (c + 1) * tables],
                    blank,
                ]
            )
            for c in range(2)
        ]
    )
    per_seq = -(-HASH_ROWS // seq_count)
    high_rows = -(-per_seq // (LANES * 8)) * 8

    qkv_weight = w_qkv.reshape(model_width, 3 * local_width)
    normed, qkv, sums = front_call(latents_in, gain_one, qkv_weight, pairs, high_rows)
    sums, cotangent_late = lax.optimization_barrier((sums, cotangent))
    qkv = qkv.reshape(group_rows, 3 * local_width)
    heads_out, lse = attend_call(sc, qkv)
    cot_far = flip(cotangent_late, "tp", 2)
    cots = [cotangent, flip(cotangent_late, "tp", 1), cot_far, flip(cot_far, "tp", 1)]

    pad = -units % 256
    weights = [jnp.pad(w, ((0, 0), (0, pad))) for w in (w_gate, w_up, w_down)]
    heads_four = heads_out.reshape(4, local_rows, local_width)
    rest, far_down, grad_hidden, gain_two_part, branch, keep, got = middle_call(
        heads_four, w_out.T, latents_in, gain_two, cots, weights, units
    )
    down_far = flip(far_down, "tp", 2)
    half_sum = (keep.astype(F32) + got.astype(F32)).astype(BF)
    place = seq // 2
    pieces = [
        lax.dynamic_index_in_dim(half_sum, place ^ j, 0, keepdims=False)
        for j in range(seq_count // 2)
    ]
    arrived = [flip(pieces[j], "seq", 2 * j) for j in range(1, seq_count // 2)]
    mixed = attend_back_call(
        sc, branch.reshape(group_rows, model_width), w_out, qkv, heads_out, lse
    )
    grad_latents, qkv_total, out_total, gains = last_call(
        mixed.reshape(4, local_rows, -1), qkv_weight, latents_in, gain_one, grad_hidden,
        normed, heads_four, branch, gain_two_part,
    )
    qkv_total = qkv_total.reshape(-1, 3, local_width)
    total = pieces[0].astype(F32)
    for piece in arrived:
        total = total + piece.astype(F32)
    latents_out = (rest + down_far.astype(F32)).astype(BF)
    hash_counts = spread_tables(sums, core, seq)
    return (
        latents_out,
        grad_latents,
        gains[0],
        qkv_total,
        out_total,
        gains[1],
        total[1],
        total[2],
        total[0],
        hash_counts,
    )


def solution(mesh):
    in_specs = (
        P(("seq", "tp"), None),
        P(),
        P(None, None, "tp"),
        P(None, "tp"),
        P(),
        P(None, "tp"),
        P(None, "tp"),
        P(None, "tp"),
        P(("seq", "tp"), None),
        P("seq", None),
        P("seq", None),
        P(None, ("seq", "tp")),
        P(None, ("seq", "tp")),
    )
    out_specs = (
        P(("seq", "tp"), None),
        P(("seq", "tp"), None),
        P(),
        P("seq", None, "tp"),
        P("seq", "tp"),
        P(),
        P("seq", "tp"),
        P("seq", "tp"),
        P("seq", "tp"),
        P(),
    )
    return jax.shard_map(shards, mesh=mesh, in_specs=in_specs, out_specs=out_specs, check_vma=False)
```

```python
import functools

import jax
import jax.numpy as jnp
from jax import lax
from jax.experimental import pallas as pl
from jax.experimental.pallas import tpu as pltpu
from jax.sharding import PartitionSpec as P

HEAD_DIM = 64
HASH_ROWS = 500002
EPSILON = 1e-05
MASKED = -1e30
BF = jnp.bfloat16
F32 = jnp.float32
QB = 256
LANES = 256
STEPS = 4
VMEM_BYTES = 60 * 1024 * 1024
MESH = pl.DeviceIdType.MESH


def flip(x, axis, bits):
    count = lax.axis_size(axis)
    return lax.ppermute(x, axis, [(i, i ^ bits) for i in range(count)])


def dot(a, b):
    return lax.dot_general(a, b, (((1,), (0,)), ((), ())), preferred_element_type=F32)


def dot_nt(a, b):
    return lax.dot_general(a, b, (((1,), (1,)), ((), ())), preferred_element_type=F32)


def dot_tn(a, b):
    return lax.dot_general(a, b, (((0,), (0,)), ((), ())), preferred_element_type=F32)


def cost(flops, moved):
    return pl.CostEstimate(flops=flops, bytes_accessed=moved, transcendentals=0)


def params(**more):
    return pltpu.CompilerParams(vmem_limit_bytes=VMEM_BYTES, **more)


def whole(shape):
    return pl.BlockSpec(shape, lambda i, sc: (0,) * len(shape))


VM = pl.BlockSpec(memory_space=pltpu.VMEM)
ANY = pl.BlockSpec(memory_space=pl.ANY)


def places():
    me = lax.axis_index("tp")
    core = lax.rem(me, 2)
    sib = me + 1 - 2 * core
    far = lax.rem(me + 2, 4)
    return me, sib, far, lax.rem(sib + 2, 4), core


def push(src, dst, send, recv, where):
    return pltpu.make_async_remote_copy(
        src_ref=src,
        dst_ref=dst,
        send_sem=send,
        recv_sem=recv,
        device_id={"seq": where[0], "tp": where[1]},
        device_id_type=MESH,
    )


def greet(others):
    barrier = pltpu.get_barrier_semaphore()
    for seq, tp in others:
        pl.semaphore_signal(
            barrier, inc=1, device_id={"seq": seq, "tp": tp}, device_id_type=MESH
        )
    pl.semaphore_wait(barrier, len(others))


def each(body, count):
    lax.fori_loop(0, count, lambda k, c: (body(k), c)[1], 0)


def chunk(k, size):
    return pl.ds(pl.multiple_of(k * size, size), size)


def norm_rows(row_data, gain):
    scaling = lax.rsqrt(jnp.mean(row_data * row_data, axis=-1, keepdims=True) + EPSILON)
    return (row_data * scaling * gain, scaling)


def norm_back(row_data, scaling, gain, grad_norm):
    weighted = grad_norm * gain
    inner_mean = jnp.mean(weighted * row_data, axis=-1, keepdims=True)
    grad_rows = scaling * weighted - row_data * scaling * scaling * scaling * inner_mean
    grad_gain = jnp.sum(grad_norm * row_data * scaling, axis=0, keepdims=True)
    return (grad_rows, grad_gain)


def front_kernel(
    seq_count, tables, x_ref, gain_ref, w_ref, pair_ref, n_out, qkv_out, hash_ref,
    n_ref, qkv_ref, pack_ref, sum_ref, snd, rcv, psnd, prcv, loc,
):
    me, sib, far, farsib, core = places()
    seq = lax.axis_index("seq")
    near = seq + 1 - 2 * lax.rem(seq, 2)
    parity, place, half = lax.rem(seq, 2), seq // 2, seq_count // 2
    level = [lax.rem(seq + 2 * j, seq_count) for j in range(1, half)]
    greet([(seq, sib), (seq, far), (near, me)] + [(s, me) for s in level])
    rows = x_ref.shape[0]
    size = rows // STEPS

    pack_ref[parity, place, me] = pair_ref[core]
    mine = pack_ref.at[parity, place, me]
    stage_sib = push(pair_ref.at[1 - core], mine, psnd.at[0], prcv.at[0], (seq, sib))
    stage_sib.start()
    both = pack_ref.at[parity, place, pl.ds(me - core, 2)]
    stage_far = push(both, both, psnd.at[1], prcv.at[1], (seq, far))
    four = pack_ref.at[parity, place]
    stage_level = [
        push(four, four, psnd.at[2 + j], prcv.at[2 + j], (s, me)) for j, s in enumerate(level)
    ]
    plane = pack_ref.at[parity]
    stage_near = push(plane, plane, psnd.at[half + 1], prcv.at[half + 1], (near, me))

    def own(kind, k, to, block):
        part = n_ref.at[block, chunk(k, size)]
        return push(part, part, snd.at[kind, k], rcv.at[kind, k], (seq, to))

    for k in range(STEPS):
        part = slice(k * size, (k + 1) * size)
        normed, _ = norm_rows(x_ref[part].astype(F32), gain_ref[...])
        n_ref[me, part] = normed.astype(BF)
        if k == 0:
            stage_sib.wait_recv()
            stage_far.start()
        own(1, k, far, me).start()
        own(0, k, sib, me).start()

    width = w_ref.shape[2]

    def project(block, k, length):
        part = chunk(k, length)
        for c in range(3):
            qkv_ref[block, part, c * width : (c + 1) * width] = dot(
                n_ref[block, part], w_ref[c]
            ).astype(BF)

    def homes(block):
        return [
            pltpu.make_async_copy(n_ref.at[block], n_out.at[block], loc.at[0, block]),
            pltpu.make_async_copy(qkv_ref.at[block], qkv_out.at[block], loc.at[1, block]),
        ]

    each(lambda k: project(me, k, rows // 2), 2)
    for copy in homes(me):
        copy.start()
    stage_far.wait_recv()
    for copy in stage_level:
        copy.start()
    for k in range(STEPS):
        own(0, k, sib, me).wait_recv()
    each(lambda k: project(sib, k, rows // 2), 2)
    for copy in homes(sib):
        copy.start()

    def far_chunk(k):
        own(1, k, far, me).wait_recv()
        own(2, k, sib, far).start()
        project(far, k, size)

    def farsib_chunk(k):
        own(2, k, sib, far).wait_recv()
        project(farsib, k, size)

    far_chunk(0)
    for copy in stage_level:
        copy.wait_recv()
    stage_near.start()

    sum_ref[...] = jnp.zeros_like(sum_ref)
    high_rows = sum_ref.shape[1]
    first = seq * (high_rows * LANES)

    def sums(which):
        def body(b):
            for table in range(tables):
                line = lambda row: jnp.concatenate(
                    [pack_ref[which, b, t, row : row + 1] for t in range(4)], axis=1
                )
                ids = line(table).astype(jnp.int32) - first
                weights = line(table + tables)
                high = lax.broadcasted_iota(jnp.int32, (high_rows, 4 * rows), 0) == (ids >> 8)
                low = lax.broadcasted_iota(jnp.int32, (LANES, 4 * rows), 0) == (ids & (LANES - 1))
                high = jnp.where(high, 1.0, 0.0).astype(BF)
                low = jnp.where(low, weights, 0.0).astype(BF)
                sum_ref[table] += dot_nt(high, low)

        each(body, half)

    sums(parity)
    each(lambda k: far_chunk(k + 1), STEPS - 2)
    each(farsib_chunk, STEPS - 1)
    stage_near.wait_recv()
    sums(1 - parity)
    far_chunk(STEPS - 1)
    for copy in homes(far):
        copy.start()
    hash_ref[...] = sum_ref[...].astype(BF)
    farsib_chunk(STEPS - 1)
    for copy in homes(farsib):
        copy.start()
    for k in range(STEPS):
        for kind in range(3):
            own(kind, k, sib, me).wait_send()
    stage_sib.wait_send()
    stage_far.wait_send()
    for copy in stage_level:
        copy.wait_send()
    stage_near.wait_send()
    for block in (me, sib, far, farsib):
        for copy in homes(block):
            copy.wait()


def front_call(x, gain, w, pairs, high_rows):
    seq_count = lax.axis_size("seq")
    rows, model = x.shape
    width = w.shape[0] * w.shape[2]
    tables = 3
    half = seq_count // 2
    dma = pltpu.SemaphoreType.DMA
    return pl.pallas_call(
        functools.partial(front_kernel, seq_count, tables),
        in_specs=[VM] * 4,
        out_specs=[ANY] * 2 + [VM],
        out_shape=[
            jax.ShapeDtypeStruct((4, rows, model), BF),
            jax.ShapeDtypeStruct((4, rows, width), BF),
            jax.ShapeDtypeStruct((tables, high_rows, LANES), BF),
        ],
        scratch_shapes=[
            pltpu.VMEM((4, rows, model), BF),
            pltpu.VMEM((4, rows, width), BF),
            pltpu.VMEM((2, half, 4, 8, rows), F32),
            pltpu.VMEM((tables, high_rows, LANES), F32),
            dma((3, STEPS)),
            dma((3, STEPS)),
            dma((half + 2,)),
            dma((half + 2,)),
            dma((2, 4)),
        ],
        compiler_params=params(collective_id=0, has_side_effects=True),
        cost_estimate=cost(1_000_000, 1_000_000),
        name="front",
    )(x, gain, w, pairs)


def doc_bounds(sc, places):
    low = jnp.where(places >= sc[2], sc[2], jnp.where(places >= sc[1], sc[1], 0))
    end = jnp.where(places >= sc[2], sc[5], jnp.where(places >= sc[1], sc[4], sc[3]))
    return low, jnp.minimum(places, end - 1)


def head_rows(x, h):
    where = lax.broadcasted_iota(jnp.int32, x.shape, 0) // HEAD_DIM
    return jnp.where(where == h, x, jnp.zeros_like(x))


def attend_kernel(heads, sc, qkv_ref, heads_ref, lse_ref, vt_ref, qt_ref, acc_ref, score_ref):
    width = heads * HEAD_DIM
    step = pl.program_id(0)

    @pl.when(step == 0)
    def _():
        for n in range(qkv_ref.shape[0] // QB):
            vt_ref[:, n * QB : (n + 1) * QB] = qkv_ref[n * QB : (n + 1) * QB, 2 * width :].T

    start = pl.multiple_of(step * QB, QB)
    q_t = qkv_ref[pl.ds(start, QB), :width].T * jnp.asarray(HEAD_DIM**-0.5, BF)
    for h in range(heads):
        qt_ref[:, h * QB : (h + 1) * QB] = head_rows(q_t, h)
    acc_ref[...] = jnp.zeros_like(acc_ref)
    places = start + lax.broadcasted_iota(jnp.int32, (1, QB), 1)
    low, high = doc_bounds(sc, places)
    low_first, _ = doc_bounds(sc, start)

    def body(kb, state):
        at = pl.multiple_of(kb * QB, QB)
        keys = qkv_ref[pl.ds(at, QB), width : 2 * width]
        value_t = vt_ref[:, pl.ds(at, QB)]
        spot = at + lax.broadcasted_iota(jnp.int32, (QB, QB), 0)
        allowed = (spot >= low) & (spot <= high)
        score_ref[...] = dot(keys, qt_ref[...])
        fresh = []
        for h in range(heads):
            top, total = state[h]
            scores = jnp.where(allowed, score_ref[:, h * QB : (h + 1) * QB], MASKED)
            new_top = jnp.maximum(top, jnp.max(scores, axis=0, keepdims=True))
            fade = jnp.exp(top - new_top)
            probs = jnp.exp(scores - new_top)
            total = total * fade + jnp.sum(probs, axis=0, keepdims=True)
            part = slice(h * HEAD_DIM, (h + 1) * HEAD_DIM)
            acc_ref[part] = acc_ref[part] * fade + dot(value_t[part], probs.astype(BF))
            fresh.append((new_top, total))
        return tuple(fresh)

    begin = tuple(
        (jnp.full((1, QB), MASKED, F32), jnp.zeros((1, QB), F32)) for _ in range(heads)
    )
    state = lax.fori_loop(low_first // QB, start // QB + 1, body, begin)
    lse_ref[...] = jnp.zeros_like(lse_ref)
    for h in range(heads):
        top, total = state[h]
        part = slice(h * HEAD_DIM, (h + 1) * HEAD_DIM)
        acc_ref[part] = acc_ref[part] * (1.0 / total)
        lse_ref[h : h + 1] = top + jnp.log(total)
    heads_ref[...] = acc_ref[...].T.astype(BF)


def attend_call(sc, qkv):
    rows, width = qkv.shape[0], qkv.shape[1] // 3
    heads = width // HEAD_DIM
    return pl.pallas_call(
        functools.partial(attend_kernel, heads),
        grid_spec=pltpu.PrefetchScalarGridSpec(
            num_scalar_prefetch=1,
            grid=(rows // QB,),
            in_specs=[whole(qkv.shape)],
            out_specs=[
                pl.BlockSpec((QB, width), lambda i, sc: (i, 0)),
                pl.BlockSpec((8, QB), lambda i, sc: (0, i)),
            ],
            scratch_shapes=[
                pltpu.VMEM((width, rows), BF),
                pltpu.VMEM((width, heads * QB), BF),
                pltpu.VMEM((width, QB), F32),
                pltpu.VMEM((QB, heads * QB), F32),
            ],
        ),
        out_shape=[
            jax.ShapeDtypeStruct((rows, width), BF),
            jax.ShapeDtypeStruct((8, rows), F32),
        ],
        compiler_params=params(),
        cost_estimate=cost(60_000_000_000, 8_000_000),
        name="attend",
    )(sc, qkv)


def attend_back_kernel(
    heads, sc, grad_ref, wo_ref, qkv_ref, heads_ref, lse_ref, mixed_ref,
    kt_ref, qt_ref, gt_ref, qs_ref, gs_ref, dqt_ref, dk_ref, dv_ref, score_ref, prob_ref,
):
    width = heads * HEAD_DIM
    step = pl.program_id(0)
    rows = qkv_ref.shape[0]

    @pl.when(step == 0)
    def _():
        for n in range(rows // QB):
            kt_ref[:, n * QB : (n + 1) * QB] = qkv_ref[n * QB : (n + 1) * QB, width : 2 * width].T
        dk_ref[...] = jnp.zeros_like(dk_ref)
        dv_ref[...] = jnp.zeros_like(dv_ref)

    start = pl.multiple_of(step * QB, QB)
    grad = dot(grad_ref[...], wo_ref[...]).astype(BF)
    grad_t = grad.T
    out_t = heads_ref[...].T
    product = grad_t.astype(F32) * out_t.astype(F32)
    query = qkv_ref[pl.ds(start, QB), :width] * jnp.asarray(HEAD_DIM**-0.5, BF)
    q_t = query.T
    inner = []
    for h in range(heads):
        part = slice(h * HEAD_DIM, (h + 1) * HEAD_DIM)
        inner.append(jnp.sum(product[part], axis=0, keepdims=True))
        qt_ref[:, h * QB : (h + 1) * QB] = head_rows(q_t, h)
        gt_ref[:, h * QB : (h + 1) * QB] = head_rows(grad_t, h)
    qs_ref[...] = q_t
    gs_ref[...] = grad_t
    dqt_ref[...] = jnp.zeros_like(dqt_ref)
    places = start + lax.broadcasted_iota(jnp.int32, (1, QB), 1)
    low, high = doc_bounds(sc, places)
    low_first, _ = doc_bounds(sc, start)

    def body(kb, carry):
        at = pl.multiple_of(kb * QB, QB)
        keys = qkv_ref[pl.ds(at, QB), width : 2 * width]
        values = qkv_ref[pl.ds(at, QB), 2 * width :]
        spot = at + lax.broadcasted_iota(jnp.int32, (QB, QB), 0)
        allowed = (spot >= low) & (spot <= high)
        score_ref[...] = dot(keys, qt_ref[...])
        prob_ref[...] = dot(values, gt_ref[...])
        for h in range(heads):
            part = slice(h * HEAD_DIM, (h + 1) * HEAD_DIM)
            lanes = slice(h * QB, (h + 1) * QB)
            scores = jnp.where(allowed, score_ref[:, lanes], MASKED)
            probs = jnp.exp(scores - lse_ref[h : h + 1])
            grad_scores = (probs * (prob_ref[:, lanes] - inner[h])).astype(BF)
            dqt_ref[part] += dot(kt_ref[part, pl.ds(at, QB)], grad_scores)
            dv_ref[part, pl.ds(at, QB)] += dot_nt(gs_ref[part], probs.astype(BF))
            dk_ref[part, pl.ds(at, QB)] += dot_nt(qs_ref[part], grad_scores)
        return carry

    lax.fori_loop(low_first // QB, start // QB + 1, body, 0)
    dq = (dqt_ref[...] * HEAD_DIM**-0.5).T.astype(BF)
    mixed_ref[pl.ds(start, QB), :width] = dq

    @pl.when(step == pl.num_programs(0) - 1)
    def _():
        for n in range(rows // QB):
            part = slice(n * QB, (n + 1) * QB)
            mixed_ref[part, width : 2 * width] = dk_ref[:, part].T.astype(BF)
            mixed_ref[part, 2 * width :] = dv_ref[:, part].T.astype(BF)


def attend_back_call(sc, grad, wo, qkv, heads_out, lse):
    rows, width = qkv.shape[0], qkv.shape[1] // 3
    heads = width // HEAD_DIM
    model = wo.shape[0]
    return pl.pallas_call(
        functools.partial(attend_back_kernel, heads),
        grid_spec=pltpu.PrefetchScalarGridSpec(
            num_scalar_prefetch=1,
            grid=(rows // QB,),
            in_specs=[
                pl.BlockSpec((QB, model), lambda i, sc: (i, 0)),
                whole(wo.shape),
                whole(qkv.shape),
                pl.BlockSpec((QB, width), lambda i, sc: (i, 0)),
                pl.BlockSpec((8, QB), lambda i, sc: (0, i)),
            ],
            out_specs=whole((rows, 3 * width)),
            scratch_shapes=[
                pltpu.VMEM((width, rows), BF),
                pltpu.VMEM((width, heads * QB), BF),
                pltpu.VMEM((width, heads * QB), BF),
                pltpu.VMEM((width, QB), BF),
                pltpu.VMEM((width, QB), BF),
                pltpu.VMEM((width, QB), F32),
                pltpu.VMEM((width, rows), F32),
                pltpu.VMEM((width, rows), F32),
                pltpu.VMEM((QB, heads * QB), F32),
                pltpu.VMEM((QB, heads * QB), F32),
            ],
        ),
        out_shape=jax.ShapeDtypeStruct((rows, 3 * width), BF),
        compiler_params=params(),
        cost_estimate=cost(90_000_000_000, 12_000_000),
        name="attend_back",
    )(sc, grad, wo, qkv, heads_out, lse)


def middle_kernel(
    seq_count, heads_ref, wo_ref, x_ref, gain_ref, c0, c2, wg_in, wu_in, wd_in, table_in, *refs
):
    half = seq_count // 2
    rest_ref, fardown_ref, grad_ref, gain_out, keep_out, send_out, branch_ref, table_ref = refs[:8]
    piece_refs, refs = refs[8 : 8 + half], refs[8 + half :]
    (
        c1, c3, n_ref, wg_ref, wu_ref, wd_ref, act_ref, gg_ref, gu_ref,
        g0_ref, g1s_ref, g1r_ref, d0_ref, d1s_ref, d1r_ref,
        as_ref, ar_ref, ys_ref, yr_ref, bs_ref, br_ref, gb_ref,
        stay_ref, away_ref, got_ref, up_ref, upgot_ref,
        snd, rcv, xsnd, xrcv, zsnd, zrcv, tsnd, trcv, loc, wloc,
    ) = refs
    me, sib, far, farsib, core = places()
    seq = lax.axis_index("seq")
    parity, place = lax.rem(seq, 2), seq // 2
    near = seq + 1 - 2 * parity
    level = [lax.rem(seq + 2 * j, seq_count) for j in range(1, half)]

    loads = [
        pltpu.make_async_copy(w_in, w_ref.at[: w_in.shape[0]], wloc.at[n])
        for n, (w_in, w_ref) in enumerate(((wg_in, wg_ref), (wu_in, wu_ref), (wd_in, wd_ref)))
    ]
    for load in loads:
        load.start()
    greet([(seq, sib), (seq, far), (near, me)] + [(s, me) for s in level])
    rows, model = x_ref.shape
    size = rows // STEPS
    units = wg_in.shape[0]
    long = rows // 2
    kinds = iter(range(100))

    def maker(src, dst, to, length=size):
        kind = next(kinds)

        def made(k):
            part = chunk(k, length)
            return push(src.at[part], dst.at[part], snd.at[kind, k], rcv.at[kind, k], (seq, to))

        return made

    proj_a = maker(as_ref, ar_ref, sib)
    proj_y = maker(ys_ref, yr_ref, far)
    proj_b = maker(bs_ref, br_ref, sib)
    two_sib = maker(n_ref.at[me], n_ref.at[me], sib)
    two_far = maker(n_ref.at[me], n_ref.at[me], far)
    two_on = maker(n_ref.at[far], n_ref.at[far], sib)
    back_one = maker(g1s_ref, g1r_ref, sib, long)
    down_one = maker(d1s_ref, d1r_ref, sib, long)
    back_a = maker(as_ref, ar_ref, sib, long)
    back_y = maker(ys_ref, yr_ref, far)
    down_three = maker(bs_ref, br_ref, sib, long)
    branch_sib = maker(gb_ref, branch_ref.at[me], sib)
    branch_far = maker(gb_ref, branch_ref.at[me], far)
    branch_on = maker(branch_ref.at[far], branch_ref.at[far], sib)
    cot_one = maker(c0, c1, sib, long)
    cot_three = maker(c2, c3, sib, long)

    def branch_home(k):
        part = chunk(k, size)
        return pltpu.make_async_copy(gb_ref.at[part], branch_ref.at[me, part], loc.at[k])

    table_home = pltpu.make_async_copy(table_in, table_ref.at[parity, place, core], wloc.at[3])

    def table_level(j):
        return push(
            table_in, table_ref.at[parity, place, core], tsnd.at[0, j], trcv.at[0, j], (level[j - 1], me)
        )

    def table_near(j):
        spot = table_ref.at[parity, lax.rem(place + half - j, half), core]
        return push(table_in if j == 0 else spot, spot, tsnd.at[1, j], trcv.at[1, j], (near, me))

    def table_sib(same, j):
        which = parity if same else 1 - parity
        spot = table_ref.at[which, lax.rem(place + half - j, half), core]
        kind = 2 if same else 3
        src = table_in if same and j == 0 else spot
        return push(src, spot, tsnd.at[kind, j], trcv.at[kind, j], (seq, sib))

    table_home.start()
    for j in range(1, half):
        table_level(j).start()
    table_near(0).start()
    table_sib(True, 0).start()
    for k in range(2):
        cot_one(k).start()
        cot_three(k).start()

    def project(block, k):
        return dot_nt(heads_ref[block, chunk(k, size)], wo_ref[...])

    def send_three(k):
        as_ref[chunk(k, size)] = project(farsib, k).astype(BF)
        proj_a(k).start()

    def send_two(k):
        part = project(far, k)
        proj_a(k).wait_recv()
        ys_ref[chunk(k, size)] = (part + ar_ref[chunk(k, size)].astype(F32)).astype(BF)
        proj_y(k).start()

    def send_one(k):
        bs_ref[chunk(k, size)] = project(sib, k).astype(BF)
        proj_b(k).start()

    each(send_three, STEPS)
    each(send_two, STEPS)
    each(send_one, STEPS)
    wide = act_ref.shape[0]
    if wide > units:
        for ref in (act_ref, gg_ref, gu_ref, wg_ref, wu_ref, wd_ref):
            ref[units:] = jnp.zeros((wide - units, ref.shape[1]), BF)
    for load in loads:
        load.wait()
    for k in range(2):
        cot_one(k).wait_recv()
        cot_three(k).wait_recv()

    def feed(m, block_a, block_b, ca, cb):
        part = chunk(m, long)
        normed = jnp.concatenate([n_ref[block_a, part], n_ref[block_b, part]], axis=0)
        cot = jnp.concatenate([ca[part], cb[part]], axis=0)
        gate = dot_nt(wg_ref[:units], normed)
        up = dot_nt(wu_ref[:units], normed)
        sig = jax.nn.sigmoid(gate)
        silu = gate * sig
        act = (silu * up).astype(BF)
        grad_act = dot_nt(wd_ref[:units], cot)
        grad_gate = (grad_act * up * sig * (1.0 + gate * (1.0 - sig))).astype(BF)
        grad_up = (grad_act * silu).astype(BF)
        lanes = [
            pl.ds(pl.multiple_of(block * rows + m * long, long), long) for block in (block_a, block_b)
        ]
        for ref, value in ((act_ref, act), (gg_ref, grad_gate), (gu_ref, grad_up)):
            ref[:units, lanes[0]] = value[:, :long]
            ref[:units, lanes[1]] = value[:, long:]
        pair = lambda ref: jnp.concatenate([ref[:, lanes[0]], ref[:, lanes[1]]], axis=1)
        back = dot_tn(pair(gg_ref), wg_ref[...]) + dot_tn(pair(gu_ref), wu_ref[...])
        return back, dot_tn(pair(act_ref), wd_ref[...])

    def own_chunk(k):
        part = chunk(k, size)
        total = x_ref[part].astype(F32) + project(me, k)
        proj_b(k).wait_recv()
        proj_y(k).wait_recv()
        hidden = total + br_ref[part].astype(F32) + yr_ref[part].astype(F32)
        rest_ref[part] = hidden
        normed, _ = norm_rows(hidden, gain_ref[...])
        n_ref[me, part] = normed.astype(BF)
        two_far(k).start()
        two_sib(k).start()

    def own_half(m):
        own_chunk(2 * m)
        own_chunk(2 * m + 1)
        two_sib(2 * m).wait_recv()
        two_sib(2 * m + 1).wait_recv()
        part = chunk(m, long)
        back, down = feed(m, me, sib, c0, c1)
        g0_ref[part] = back[:long].astype(BF)
        g1s_ref[part] = back[long:].astype(BF)
        back_one(m).start()
        d0_ref[part] = down[:long].astype(BF)
        d1s_ref[part] = down[long:].astype(BF)
        down_one(m).start()

    each(own_half, 2)
    for j in range(1, half):
        table_level(j).wait_recv()
        table_near(j).start()
        table_sib(True, j).start()

    def settle(k):
        proj_a(k).wait_send()
        proj_y(k).wait_send()
        proj_b(k).wait_send()

    each(settle, STEPS)

    def far_sum(k):
        part = chunk(k, size)
        ys_ref[part] = (ys_ref[part].astype(F32) + ar_ref[part].astype(F32)).astype(BF)
        back_y(k).start()

    def far_half(m):
        for k in (2 * m, 2 * m + 1):
            two_far(k).wait_recv()
            two_on(k).start()
        for k in (2 * m, 2 * m + 1):
            two_on(k).wait_recv()
        part = chunk(m, long)
        back, down = feed(m, far, farsib, c2, c3)
        as_ref[part] = back[long:].astype(BF)
        back_a(m).start()
        ys_ref[part] = back[:long].astype(BF)
        bs_ref[part] = down[long:].astype(BF)
        down_three(m).start()
        fardown_ref[part] = down[:long].astype(BF)
        back_a(m).wait_recv()
        far_sum(2 * m)
        far_sum(2 * m + 1)

    each(far_half, 2)
    for j in range(half):
        table_near(j).wait_recv()
        table_sib(False, j).start()

    piece = model // seq_count
    span = model // STEPS
    per = half // STEPS
    upright = piece % 128 == 0

    def weight_away(w, b):
        return push(
            away_ref.at[w, b], got_ref.at[w, b], xsnd.at[w, b], xrcv.at[w, b], (near, me)
        )

    def up_away(j):
        b = lax.rem(place + j, half)
        return push(
            up_ref.at[b], upgot_ref.at[j - 1], zsnd.at[j], zrcv.at[j],
            (lax.rem(seq + 2 * j, seq_count), me),
        )

    def weight_tile(w, k):
        cots = (c0, c1, c2, c3)
        order = (me, sib, far, farsib)
        left = (act_ref, gg_ref, gu_ref)[w]
        total = None
        for r in range(4):
            cols = chunk(k, span)
            right = cots[r][:, cols] if w == 0 else n_ref[order[r], :, cols]
            lanes = pl.ds(pl.multiple_of(order[r] * rows, rows), rows)
            term = dot(left[:units, lanes], right)
            total = term if total is None else total + term
        return total.astype(BF)

    def weights_step(kk):
        k = lax.rem(place // per + 1 + kk, STEPS)
        for w in range(3):
            tile = weight_tile(w, k)
            tile = tile if upright else tile.T
            for n in range(per):
                b = k * per + n
                take = lambda i: slice(i * piece, (i + 1) * piece)
                even = tile[:, take(2 * n)] if upright else tile[take(2 * n)]
                odd = tile[:, take(2 * n + 1)] if upright else tile[take(2 * n + 1)]
                if w == 2:
                    up_ref[b, 0] = even
                    up_ref[b, 1] = odd

                    @pl.when(b != place)
                    def _():
                        up_away(lax.rem(b + half - place, half)).start()
                else:

                    @pl.when(parity == 0)
                    def _():
                        stay_ref[w, b] = even
                        away_ref[w, b] = odd

                    @pl.when(parity == 1)
                    def _():
                        stay_ref[w, b] = odd
                        away_ref[w, b] = even

                    weight_away(w, b).start()

    gain_out[...] = jnp.zeros_like(gain_out)

    def back_chunk(k):
        weights_step(k)
        part = chunk(k, size)
        back_y(k).wait_recv()
        grad_norm = g0_ref[part].astype(F32) + g1r_ref[part].astype(F32) + yr_ref[part].astype(F32)
        hidden = rest_ref[part]
        _, scaling = norm_rows(hidden, gain_ref[...])
        grad_rows, grad_gain = norm_back(hidden, scaling, gain_ref[...], grad_norm)
        grad = c0[part].astype(F32) + grad_rows
        grad_ref[part] = grad
        gain_out[...] += grad_gain
        gb_ref[part] = grad.astype(BF)
        branch_far(k).start()
        branch_sib(k).start()
        branch_home(k).start()

    for m in range(2):
        back_one(m).wait_recv()
    each(back_chunk, STEPS)

    for m in range(2):
        down_one(m).wait_recv()
        down_three(m).wait_recv()

    def finish(k):
        part = chunk(k, size)
        rest_ref[part] += d0_ref[part].astype(F32) + d1r_ref[part].astype(F32)
        fardown_ref[part] = (fardown_ref[part].astype(F32) + br_ref[part].astype(F32)).astype(BF)
        branch_far(k).wait_recv()
        branch_on(k).start()

    each(finish, STEPS)

    for j in range(half):
        b = lax.rem(place + j, half)
        for w in range(2):
            weight_away(w, b).wait_recv()
            piece_refs[j][w] = (stay_ref[w, b].astype(F32) + got_ref[w, b].astype(F32)).astype(BF)

    def up_sum(which):
        total = up_ref[place, which].astype(F32)
        for j in range(1, half):
            total = total + upgot_ref[j - 1, which].astype(F32)
        return total.astype(BF)

    for j in range(1, half):
        up_away(j).wait_recv()
    keep_out[...] = up_sum(parity)
    send_out[...] = up_sum(1 - parity)

    def close(k):
        branch_sib(k).wait_recv()
        branch_on(k).wait_recv()
        branch_home(k).wait()
        for made in (two_sib, two_far, two_on, back_y, branch_sib, branch_far, branch_on):
            made(k).wait_send()

    each(close, STEPS)
    for m in range(2):
        for made in (back_one, down_one, back_a, down_three, cot_one, cot_three):
            made(m).wait_send()
    table_home.wait()
    for j in range(half):
        table_sib(True, j).wait_recv()
        table_sib(False, j).wait_recv()
        table_near(j).wait_send()
        table_sib(True, j).wait_send()
        table_sib(False, j).wait_send()
        for w in range(2):
            weight_away(w, j).wait_send()
    for j in range(1, half):
        table_level(j).wait_send()
        up_away(j).wait_send()


def middle_call(heads_out, wo, x, gain, cot, cot_far, weights, tables):
    seq_count = lax.axis_size("seq")
    rows, model = x.shape
    half = seq_count // 2
    piece = model // seq_count
    units = weights[0].shape[0]
    wide = units + -units % 256
    block = (units, piece) if piece % 128 == 0 else (piece, units)
    dma = pltpu.SemaphoreType.DMA
    shape = jax.ShapeDtypeStruct
    vm = pltpu.VMEM
    rows_bf = vm((rows, model), BF)
    return pl.pallas_call(
        functools.partial(middle_kernel, seq_count),
        in_specs=[VM] * 6 + [ANY] * 4,
        out_specs=[VM] * 6 + [ANY] * 2 + [VM] * half,
        out_shape=[
            shape((rows, model), F32),
            shape((rows, model), BF),
            shape((rows, model), F32),
            shape((1, model), F32),
            shape(block, BF),
            shape(block, BF),
            shape((4, rows, model), BF),
            shape((2, half, 2) + tables.shape, BF),
        ]
        + [shape((2,) + block, BF)] * half,
        scratch_shapes=[rows_bf, rows_bf, vm((4, rows, model), BF)]
        + [vm((wide, model), BF)] * 3
        + [vm((wide, 4 * rows), BF)] * 3
        + [rows_bf] * 13
        + [vm((2, half) + block, BF)] * 3
        + [vm((half, 2) + block, BF), vm((half - 1, 2) + block, BF)]
        + [dma((16, STEPS))] * 2
        + [dma((2, half))] * 2
        + [dma((half,))] * 2
        + [dma((4, half))] * 2
        + [dma((STEPS,)), dma((4,))],
        compiler_params=params(collective_id=1, has_side_effects=True),
        cost_estimate=cost(100_000_000_000, 30_000_000),
        name="middle",
    )(heads_out, wo, x, gain, cot, cot_far, *weights, tables)


def last_kernel(
    seq_count, mixed_in, w_in, x_in, gain_ref, grad_in, n_in, heads_in, branch_in, gain_in,
    out_ref, wqkv_ref, wout_ref, gains_ref,
    mixed_ref, w_ref, x_ref, grad_ref, n_ref, heads_ref, branch_ref,
    as_ref, ar_ref, ys_ref, yr_ref, bs_ref, br_ref, dw_ref, got_ref, sum_ref, zr_ref, gs_ref, gr_ref,
    snd, rcv, xsnd, xrcv, zsnd, zrcv, gsnd, grcv, loc,
):
    me, sib, far, farsib, core = places()
    seq = lax.axis_index("seq")
    parity, place, half = lax.rem(seq, 2), seq // 2, seq_count // 2
    near = seq + 1 - 2 * parity
    level = [lax.rem(seq + 2 * j, seq_count) for j in range(1, half)]
    loads = [
        pltpu.make_async_copy(src, dst, loc.at[n])
        for n, (src, dst) in enumerate(
            (
                (mixed_in, mixed_ref), (w_in, w_ref), (n_in, n_ref), (branch_in, branch_ref),
                (heads_in, heads_ref), (x_in, x_ref), (grad_in, grad_ref),
            )
        )
    ]
    for load in loads:
        load.start()
    greet([(seq, sib), (seq, far), (near, me)] + [(s, me) for s in level])
    rows, model = x_ref.shape
    size = rows // STEPS
    piece = model // seq_count
    wide = mixed_ref.shape[-1]

    def copy(kind, k, src, dst, to):
        return push(
            src.at[chunk(k, size)], dst.at[chunk(k, size)], snd.at[kind, k], rcv.at[kind, k], (seq, to)
        )

    back_a = lambda k: copy(0, k, as_ref, ar_ref, sib)
    back_y = lambda k: copy(1, k, ys_ref, yr_ref, far)
    back_b = lambda k: copy(2, k, bs_ref, br_ref, sib)

    def near_copy(b):
        return push(dw_ref.at[1, b], got_ref.at[b], xsnd.at[b], xrcv.at[b], (near, me))

    def level_copy(j):
        b = lax.rem(place + j, half)
        return push(
            sum_ref.at[b], zr_ref.at[j], zsnd.at[j], zrcv.at[j], (lax.rem(seq + 2 * j, seq_count), me)
        )

    width = w_ref.shape[2]

    def project(block, k):
        part = chunk(k, size)
        terms = [
            dot_nt(mixed_ref[block, part, c * width : (c + 1) * width], w_ref[c]) for c in range(3)
        ]
        return terms[0] + terms[1] + terms[2]

    def send_three(k):
        as_ref[chunk(k, size)] = project(farsib, k).astype(BF)
        back_a(k).start()

    def send_two(k):
        part = project(far, k)
        back_a(k).wait_recv()
        ys_ref[chunk(k, size)] = (part + ar_ref[chunk(k, size)].astype(F32)).astype(BF)
        back_y(k).start()

    def send_one(k):
        bs_ref[chunk(k, size)] = project(sib, k).astype(BF)
        back_b(k).start()

    span = model // STEPS
    per = half // STEPS

    def weights_step(kk):
        k = lax.rem(place // per + 1 + kk, STEPS)
        cols = chunk(k, span)
        to_qkv, to_out = None, None
        for r in range(4):
            term = dot_tn(n_ref[r, :, cols], mixed_ref[r])
            to_qkv = term if to_qkv is None else to_qkv + term
            term = dot_tn(branch_ref[r, :, cols], heads_ref[r])
            to_out = term if to_out is None else to_out + term
        for ref_at, value in ((slice(0, wide), to_qkv), (slice(wide, None), to_out)):
            tile = value.astype(BF).reshape(per, 2, piece, value.shape[1])
            for j in range(per):
                b = k * per + j

                @pl.when(parity == 0)
                def _():
                    dw_ref[0, b, :, ref_at] = tile[j, 0]
                    dw_ref[1, b, :, ref_at] = tile[j, 1]

                @pl.when(parity == 1)
                def _():
                    dw_ref[0, b, :, ref_at] = tile[j, 1]
                    dw_ref[1, b, :, ref_at] = tile[j, 0]

        for j in range(per):
            near_copy(k * per + j).start()

    for load in loads[:2]:
        load.wait()
    each(send_three, STEPS)
    each(send_two, STEPS)
    for load in loads[2:5]:
        load.wait()
    each(weights_step, STEPS)
    each(send_one, STEPS)
    for load in loads[5:]:
        load.wait()

    gs_ref[...] = jnp.zeros_like(gs_ref)

    def own_chunk(k):
        part = chunk(k, size)
        total = project(me, k)
        x = x_ref[part].astype(F32)
        _, scaling = norm_rows(x, gain_ref[...])
        back_b(k).wait_recv()
        back_y(k).wait_recv()
        grad_norm = total + br_ref[part].astype(F32) + yr_ref[part].astype(F32)
        grad_rows, grad_gain = norm_back(x, scaling, gain_ref[...], grad_norm)
        out_ref[part] = grad_ref[part] + grad_rows
        gs_ref[0, 0:1] += grad_gain

    def near_sum(b):
        near_copy(b).wait_recv()
        sum_ref[b] = (dw_ref[0, b].astype(F32) + got_ref[b].astype(F32)).astype(BF)

        @pl.when(b != place)
        def _():
            level_copy(lax.rem(b + half - place, half)).start()

    def both(kk):
        k = lax.rem(place // per + 1 + kk, STEPS)
        own_chunk(kk)
        for n in range(per):
            near_sum(k * per + n)

    each(both, STEPS)

    gs_ref[0, 1:2] = gain_in[...]
    others = [(seq, sib), (seq, far), (near, me)]

    def gain_copy(n, slot, to):
        return push(gs_ref.at[n], gr_ref.at[slot], gsnd.at[slot], grcv.at[slot], to)

    for n, to in enumerate(others):
        gain_copy(n, n, to).start()
        gain_copy(n, n, to).wait_recv()
        gs_ref[n + 1] = gs_ref[n] + gr_ref[n]
    for j in range(1, half):
        gain_copy(3, 2 + j, (level[j - 1], me)).start()
    gains = gs_ref[3]
    for j in range(1, half):
        gain_copy(3, 2 + j, (level[j - 1], me)).wait_recv()
        gains = gains + gr_ref[2 + j]
    gains_ref[...] = gains

    total = sum_ref[place].astype(F32)
    for j in range(1, half):
        level_copy(j).wait_recv()
        total = total + zr_ref[j].astype(F32)
    for c in range(3):
        wqkv_ref[c] = total[:, c * width : (c + 1) * width]
    wout_ref[...] = total[:, wide:]

    def close(k):
        for made in (back_a, back_y, back_b):
            made(k).wait_send()

    each(close, STEPS)
    each(lambda b: near_copy(b).wait_send(), half)
    for n, to in enumerate(others):
        gain_copy(n, n, to).wait_send()
    for j in range(1, half):
        gain_copy(3, 2 + j, (level[j - 1], me)).wait_send()
        level_copy(j).wait_send()


def last_call(mixed, w, x, gain, grad, normed, heads_out, branch, gain_two):
    seq_count = lax.axis_size("seq")
    rows, model = x.shape
    half = seq_count // 2
    piece = model // seq_count
    wide, width = mixed.shape[-1], heads_out.shape[-1]
    dma = pltpu.SemaphoreType.DMA
    shape = jax.ShapeDtypeStruct
    rows_bf = pltpu.VMEM((rows, model), BF)
    pieces = pltpu.VMEM((half, piece, wide + width), BF)
    return pl.pallas_call(
        functools.partial(last_kernel, seq_count),
        in_specs=[ANY] * 3 + [VM] + [ANY] * 4 + [VM],
        out_specs=[VM] * 4,
        out_shape=[
            shape((rows, model), F32),
            shape((3, piece, width), F32),
            shape((piece, width), F32),
            shape((8, model), F32),
        ],
        scratch_shapes=[
            pltpu.VMEM(a.shape, a.dtype) for a in (mixed, w, x, grad, normed, heads_out, branch)
        ]
        + [rows_bf] * 6
        + [pltpu.VMEM((2, half, piece, wide + width), BF), pieces, pieces, pieces]
        + [pltpu.VMEM((4, 8, model), F32), pltpu.VMEM((half + 2, 8, model), F32)]
        + [
            dma((3, STEPS)),
            dma((3, STEPS)),
            dma((half,)),
            dma((half,)),
            dma((half,)),
            dma((half,)),
            dma((half + 2,)),
            dma((half + 2,)),
            dma((7,)),
        ],
        compiler_params=params(collective_id=2, has_side_effects=True),
        cost_estimate=cost(1_000_000, 1_000_000),
        name="last",
    )(mixed, w, x, gain, grad, normed, heads_out, branch, gain_two)


def spread_kernel(in_ref, out_ref, flat_ref):
    tables, high_rows = in_ref.shape[2], in_ref.shape[3]
    for n in range(tables):
        for side in range(2):
            flat_ref[side, n * high_rows : (n + 1) * high_rows] = in_ref[
                0, 0, n, :, side * 128 : (side + 1) * 128
            ].astype(F32)

    def body(n, carry):
        for u in range(8):
            row = n * 8 + u
            for side in range(2):
                at = pl.multiple_of(row * LANES + side * 128, 128)
                out_ref[:, pl.ds(at, 128)] = flat_ref[side, pl.ds(row, tables, stride=high_rows)]
        return carry

    lax.fori_loop(0, high_rows // 8, body, 0)


def spread_call(tables, hash_rows):
    parities, half, count, high_rows, lanes = tables.shape
    return pl.pallas_call(
        spread_kernel,
        grid=(parities * half,),
        in_specs=[pl.BlockSpec((1, 1, count, high_rows, lanes), lambda i: (i % 2, i // 2, 0, 0, 0))],
        out_specs=pl.BlockSpec((count, high_rows * lanes), lambda i: (0, i)),
        out_shape=jax.ShapeDtypeStruct((count, hash_rows), F32),
        scratch_shapes=[pltpu.VMEM((2, count * high_rows, 128), F32)],
        compiler_params=params(),
        cost_estimate=cost(1_000_000, 24_000_000),
        name="hash_spread",
    )(tables)


def shards(
    latents_in,
    gain_one,
    w_qkv,
    w_out,
    gain_two,
    w_gate,
    w_up,
    w_down,
    cotangent,
    doc_lengths,
    valid_lengths,
    hash_ids,
    hash_weights,
):
    local_rows, model_width = latents_in.shape
    local_width = w_qkv.shape[2]
    group_rows = 4 * local_rows
    units = w_gate.shape[1]
    rank = lax.axis_index("tp")
    seq = lax.axis_index("seq")
    core = rank % 2
    seq_count = lax.axis_size("seq")
    lengths, valid = doc_lengths[0], valid_lengths[0]
    start_one = lengths[0]
    start_two = lengths[0] + lengths[1]
    sc = jnp.stack(
        [rank, start_one, start_two, valid[0], start_one + valid[1], start_two + valid[2]]
    ).astype(jnp.int32)
    gain_one, gain_two = gain_one[None], gain_two[None]

    tables = hash_ids.shape[0] // 2
    blank = jnp.zeros((8 - 2 * tables, local_rows), F32)
    pairs = jnp.stack(
        [
            jnp.concatenate(
                [
                    hash_ids[c * tables : (c + 1) * tables].astype(F32),
                    hash_weights[c * tables : (c + 1) * tables],
                    blank,
                ]
            )
            for c in range(2)
        ]
    )
    per_seq = -(-HASH_ROWS // seq_count)
    high_rows = -(-per_seq // (LANES * 8)) * 8

    qkv_weight = w_qkv.transpose(1, 0, 2)
    normed, qkv, sums = front_call(latents_in, gain_one, qkv_weight, pairs, high_rows)
    qkv, cotangent_late = lax.optimization_barrier((qkv, cotangent))
    qkv = qkv.reshape(group_rows, 3 * local_width)
    cot_far = flip(cotangent_late, "tp", 2)
    heads_out, lse = attend_call(sc, qkv)
    heads_four = heads_out.reshape(4, local_rows, local_width)
    (
        rest, far_down, grad_hidden, gain_two_part, up_keep, up_send, branch, hash_parts, *pieces
    ) = middle_call(
        heads_four, w_out, latents_in, gain_two, cotangent, cot_far,
        (w_gate.T, w_up.T, w_down.T), sums,
    )
    down_far = flip(far_down, "tp", 2)
    up_got = flip(up_send, "seq", 1)
    arrived = [
        lax.ppermute(pieces[j], "seq", [(s, (s + 2 * j) % seq_count) for s in range(seq_count)])
        for j in range(1, seq_count // 2)
    ]
    mixed = attend_back_call(
        sc, branch.reshape(group_rows, model_width), w_out, qkv, heads_out, lse
    )
    mixed, up_got, arrived, down_far = lax.optimization_barrier((mixed, up_got, arrived, down_far))
    hash_parts = hash_parts.reshape(2, seq_count // 2, 2 * tables, high_rows, LANES)
    hash_counts = spread_call(hash_parts, HASH_ROWS)
    grad_latents, qkv_total, out_total, gains = last_call(
        mixed.reshape(4, local_rows, -1), qkv_weight, latents_in, gain_one, grad_hidden,
        normed, heads_four, branch, gain_two_part,
    )
    total = pieces[0].astype(F32)
    for piece in arrived:
        total = total + piece.astype(F32)
    up_total = up_keep.astype(F32) + up_got.astype(F32)
    latents_out = (rest + down_far.astype(F32)).astype(BF)
    upright = lambda w: w.T if w.shape[0] == units else w
    return (
        latents_out,
        grad_latents,
        gains[0],
        qkv_total.transpose(1, 0, 2),
        out_total,
        gains[1],
        upright(total[1]),
        upright(up_total),
        upright(total[0]),
        hash_counts,
    )


def solution(mesh):
    in_specs = (
        P(("seq", "tp"), None),
        P(),
        P(None, None, "tp"),
        P(None, "tp"),
        P(),
        P(None, "tp"),
        P(None, "tp"),
        P(None, "tp"),
        P(("seq", "tp"), None),
        P("seq", None),
        P("seq", None),
        P(None, ("seq", "tp")),
        P(None, ("seq", "tp")),
    )
    out_specs = (
        P(("seq", "tp"), None),
        P(("seq", "tp"), None),
        P(),
        P("seq", None, "tp"),
        P("seq", "tp"),
        P(),
        P("seq", "tp"),
        P("seq", "tp"),
        P("seq", "tp"),
        P(),
    )
    return jax.shard_map(shards, mesh=mesh, in_specs=in_specs, out_specs=out_specs, check_vma=False)
```

```python
import functools

import jax
import jax.numpy as jnp
from jax import lax
from jax.experimental import pallas as pl
from jax.experimental.pallas import tpu as pltpu
from jax.sharding import PartitionSpec as P

HEAD_DIM = 64
HASH_ROWS = 500002
EPSILON = 1e-05
MASKED = -1e30
BF = jnp.bfloat16
F32 = jnp.float32
QB = 256
LANES = 256
STEPS = 4
VMEM_BYTES = 60 * 1024 * 1024
MESH = pl.DeviceIdType.MESH


def flip(x, axis, bits):
    count = lax.axis_size(axis)
    return lax.ppermute(x, axis, [(i, i ^ bits) for i in range(count)])


def dot(a, b):
    return lax.dot_general(a, b, (((1,), (0,)), ((), ())), preferred_element_type=F32)


def dot_nt(a, b):
    return lax.dot_general(a, b, (((1,), (1,)), ((), ())), preferred_element_type=F32)


def dot_tn(a, b):
    return lax.dot_general(a, b, (((0,), (0,)), ((), ())), preferred_element_type=F32)


def cost(flops, moved):
    return pl.CostEstimate(flops=flops, bytes_accessed=moved, transcendentals=0)


def params(**more):
    return pltpu.CompilerParams(vmem_limit_bytes=VMEM_BYTES, **more)


def whole(shape):
    return pl.BlockSpec(shape, lambda i, *sc: (0,) * len(shape))


VM = pl.BlockSpec(memory_space=pltpu.VMEM)
ANY = pl.BlockSpec(memory_space=pl.ANY)


def places():
    me = lax.axis_index("tp")
    core = lax.rem(me, 2)
    sib = me + 1 - 2 * core
    far = lax.rem(me + 2, 4)
    return me, sib, far, lax.rem(sib + 2, 4), core


def push(src, dst, send, recv, where):
    return pltpu.make_async_remote_copy(
        src_ref=src,
        dst_ref=dst,
        send_sem=send,
        recv_sem=recv,
        device_id={"seq": where[0], "tp": where[1]},
        device_id_type=MESH,
    )


def greet(others):
    barrier = pltpu.get_barrier_semaphore()
    for seq, tp in others:
        pl.semaphore_signal(
            barrier, inc=1, device_id={"seq": seq, "tp": tp}, device_id_type=MESH
        )
    pl.semaphore_wait(barrier, len(others))


def each(body, count):
    lax.fori_loop(0, count, lambda k, c: (body(k), c)[1], 0)


def chunk(k, size):
    return pl.ds(pl.multiple_of(k * size, size), size)


def norm_rows(row_data, gain):
    scaling = lax.rsqrt(jnp.mean(row_data * row_data, axis=-1, keepdims=True) + EPSILON)
    return (row_data * scaling * gain, scaling)


def norm_back(row_data, scaling, gain, grad_norm):
    weighted = grad_norm * gain
    inner_mean = jnp.mean(weighted * row_data, axis=-1, keepdims=True)
    grad_rows = scaling * weighted - row_data * scaling * scaling * scaling * inner_mean
    grad_gain = jnp.sum(grad_norm * row_data * scaling, axis=0, keepdims=True)
    return (grad_rows, grad_gain)


def front_kernel(
    seq_count, x_ref, gain_ref, w_ref, ids_ref, weights_ref, wo_ref, n_out, qkv_out, hash_ref, out_out,
    out_ref, n_ref, qkv_ref, pair_ref, pack_ref, sum_ref, snd, rcv, psnd, prcv, osnd, orcv, loc,
):
    me, sib, far, farsib, core = places()
    seq = lax.axis_index("seq")
    near = seq + 1 - 2 * lax.rem(seq, 2)
    parity, place, half = lax.rem(seq, 2), seq // 2, seq_count // 2
    level = [lax.rem(seq + 2 * j, seq_count) for j in range(1, half)]
    greet([(seq, sib), (seq, far), (near, me)] + [(s, me) for s in level])
    rows = x_ref.shape[0]
    size = rows // STEPS
    tables = ids_ref.shape[0] // 2

    def pairs(low):
        ids = jnp.where(core == low, ids_ref[:tables], ids_ref[tables:]).astype(F32)
        weights = jnp.where(core == low, weights_ref[:tables], weights_ref[tables:])
        return jnp.concatenate([ids, weights, jnp.zeros((8 - 2 * tables, rows), F32)], axis=0)

    pack_ref[parity, place, me] = pairs(0)
    pair_ref[...] = pairs(1)
    mine = pack_ref.at[parity, place, me]
    stage_sib = push(pair_ref, mine, psnd.at[0], prcv.at[0], (seq, sib))
    stage_sib.start()
    both = pack_ref.at[parity, place, pl.ds(me - core, 2)]
    stage_far = push(both, both, psnd.at[1], prcv.at[1], (seq, far))
    four = pack_ref.at[parity, place]
    stage_level = [
        push(four, four, psnd.at[2 + j], prcv.at[2 + j], (s, me)) for j, s in enumerate(level)
    ]
    plane = pack_ref.at[parity]
    stage_near = push(plane, plane, psnd.at[half + 1], prcv.at[half + 1], (near, me))

    out_ref[me] = wo_ref[...]
    eighth = out_ref.at[me, place, parity]
    out_far = push(eighth, eighth, osnd.at[0], orcv.at[0], (seq, far))
    got_eighth = out_ref.at[far, place, parity]
    out_level = [
        push(got_eighth, got_eighth, osnd.at[2 + j], orcv.at[2 + j], (s, me))
        for j, s in enumerate(level)
    ]
    got_plane = out_ref.at[far, :, parity]
    out_near = push(got_plane, got_plane, osnd.at[half + 1], orcv.at[half + 1], (near, me))
    out_sib = push(out_ref.at[me], out_ref.at[me], osnd.at[1], orcv.at[1], (seq, sib))
    out_on = push(out_ref.at[far], out_ref.at[far], osnd.at[half + 2], orcv.at[half + 2], (seq, sib))

    def own(kind, k, to, block):
        part = n_ref.at[block, chunk(k, size)]
        return push(part, part, snd.at[kind, k], rcv.at[kind, k], (seq, to))

    for k in range(STEPS):
        part = slice(k * size, (k + 1) * size)
        normed, _ = norm_rows(x_ref[part].astype(F32), gain_ref[...])
        n_ref[me, part] = normed.astype(BF)
        if k == 0:
            stage_sib.wait_recv()
            stage_far.start()
            out_far.start()
            out_sib.start()
        own(1, k, far, me).start()
        own(0, k, sib, me).start()

    width = w_ref.shape[2]

    def project(block, k, length):
        part = chunk(k, length)
        for c in range(3):
            qkv_ref[block, part, c * width : (c + 1) * width] = dot(
                n_ref[block, part], w_ref[c]
            ).astype(BF)

    def out_home(block):
        return pltpu.make_async_copy(out_ref.at[block], out_out.at[block], loc.at[2, block])

    out_home(me).start()

    def homes(block):
        return [
            pltpu.make_async_copy(n_ref.at[block], n_out.at[block], loc.at[0, block]),
            pltpu.make_async_copy(qkv_ref.at[block], qkv_out.at[block], loc.at[1, block]),
        ]

    each(lambda k: project(me, k, rows // 2), 2)
    for copy in homes(me):
        copy.start()
    stage_far.wait_recv()
    for copy in stage_level:
        copy.start()
    out_far.wait_recv()
    for copy in out_level:
        copy.start()
    for k in range(STEPS):
        own(0, k, sib, me).wait_recv()
    each(lambda k: project(sib, k, rows // 2), 2)
    for copy in homes(sib):
        copy.start()

    def far_chunk(k):
        own(1, k, far, me).wait_recv()
        own(2, k, sib, far).start()
        project(far, k, size)

    def farsib_chunk(k):
        own(2, k, sib, far).wait_recv()
        project(farsib, k, size)

    far_chunk(0)
    for copy in stage_level:
        copy.wait_recv()
    stage_near.start()

    sum_ref[...] = jnp.zeros_like(sum_ref)
    high_rows = sum_ref.shape[1]
    first = seq * (high_rows * LANES)

    def sums(which):
        def body(b):
            for table in range(tables):
                line = lambda row: jnp.concatenate(
                    [pack_ref[which, b, t, row : row + 1] for t in range(4)], axis=1
                )
                ids = line(table).astype(jnp.int32) - first
                weights = line(table + tables)
                high = lax.broadcasted_iota(jnp.int32, (high_rows, 4 * rows), 0) == (ids >> 8)
                low = lax.broadcasted_iota(jnp.int32, (LANES, 4 * rows), 0) == (ids & (LANES - 1))
                high = jnp.where(high, 1.0, 0.0).astype(BF)
                low = jnp.where(low, weights, 0.0).astype(BF)
                sum_ref[table] += dot_nt(high, low)

        each(body, half)

    sums(parity)
    for copy in out_level:
        copy.wait_recv()
    out_near.start()
    each(lambda k: far_chunk(k + 1), STEPS - 2)
    each(farsib_chunk, STEPS - 1)
    stage_near.wait_recv()
    sums(1 - parity)
    out_near.wait_recv()
    out_on.start()
    out_home(far).start()
    out_sib.wait_recv()
    out_home(sib).start()
    far_chunk(STEPS - 1)
    for copy in homes(far):
        copy.start()
    hash_ref[...] = sum_ref[...].astype(BF)
    out_on.wait_recv()
    out_home(farsib).start()
    farsib_chunk(STEPS - 1)
    for copy in homes(farsib):
        copy.start()
    for k in range(STEPS):
        for kind in range(3):
            own(kind, k, sib, me).wait_send()
    stage_sib.wait_send()
    stage_far.wait_send()
    for copy in stage_level:
        copy.wait_send()
    stage_near.wait_send()
    for copy in [out_far, out_near, out_sib, out_on] + out_level:
        copy.wait_send()
    for block in (me, sib, far, farsib):
        out_home(block).wait()
    for block in (me, sib, far, farsib):
        for copy in homes(block):
            copy.wait()


def front_call(x, gain, w, ids, weights, wo, high_rows):
    seq_count = lax.axis_size("seq")
    rows, model = x.shape
    width = w.shape[0] * w.shape[2]
    tables = ids.shape[0] // 2
    half = seq_count // 2
    dma = pltpu.SemaphoreType.DMA
    return pl.pallas_call(
        functools.partial(front_kernel, seq_count),
        in_specs=[VM] * 6,
        out_specs=[ANY] * 2 + [VM, ANY],
        out_shape=[
            jax.ShapeDtypeStruct((4, rows, model), BF),
            jax.ShapeDtypeStruct((4, rows, width), BF),
            jax.ShapeDtypeStruct((tables, high_rows, LANES), BF),
            jax.ShapeDtypeStruct((4,) + wo.shape, BF),
        ],
        scratch_shapes=[
            pltpu.VMEM((4,) + wo.shape, BF),
            pltpu.VMEM((4, rows, model), BF),
            pltpu.VMEM((4, rows, width), BF),
            pltpu.VMEM((8, rows), F32),
            pltpu.VMEM((2, half, 4, 8, rows), F32),
            pltpu.VMEM((tables, high_rows, LANES), F32),
            dma((3, STEPS)),
            dma((3, STEPS)),
            dma((half + 2,)),
            dma((half + 2,)),
            dma((half + 3,)),
            dma((half + 3,)),
            dma((3, 4)),
        ],
        compiler_params=params(collective_id=0, has_side_effects=True),
        cost_estimate=cost(1_000_000, 1_000_000),
        name="front",
    )(x, gain, w, ids, weights, wo)


def doc_bounds(sc, places):
    _, lengths, valid = sc
    one = lengths[0]
    two = one + lengths[1]
    low = jnp.where(places >= two, two, jnp.where(places >= one, one, 0))
    end = jnp.where(
        places >= two, two + valid[2], jnp.where(places >= one, one + valid[1], valid[0])
    )
    return low, jnp.minimum(places, end - 1)


def head_rows(x, h):
    where = lax.broadcasted_iota(jnp.int32, x.shape, 0) // HEAD_DIM
    return jnp.where(where == h, x, jnp.zeros_like(x))


def attend_kernel(heads, rank, lengths, valid, qkv_ref, heads_ref, lse_ref, vt_ref, qt_ref, acc_ref, score_ref):
    sc = (rank, lengths, valid)
    width = heads * HEAD_DIM
    step = pl.program_id(0)

    @pl.when(step == 0)
    def _():
        for n in range(qkv_ref.shape[0] // QB):
            vt_ref[:, n * QB : (n + 1) * QB] = qkv_ref[n * QB : (n + 1) * QB, 2 * width :].T

    start = pl.multiple_of(step * QB, QB)
    q_t = qkv_ref[pl.ds(start, QB), :width].T * jnp.asarray(HEAD_DIM**-0.5, BF)
    for h in range(heads):
        qt_ref[:, h * QB : (h + 1) * QB] = head_rows(q_t, h)
    acc_ref[...] = jnp.zeros_like(acc_ref)
    places = start + lax.broadcasted_iota(jnp.int32, (1, QB), 1)
    low, high = doc_bounds(sc, places)
    low_first, _ = doc_bounds(sc, start)

    def body(kb, state):
        at = pl.multiple_of(kb * QB, QB)
        keys = qkv_ref[pl.ds(at, QB), width : 2 * width]
        value_t = vt_ref[:, pl.ds(at, QB)]
        spot = at + lax.broadcasted_iota(jnp.int32, (QB, QB), 0)
        allowed = (spot >= low) & (spot <= high)
        score_ref[...] = dot(keys, qt_ref[...])
        fresh = []
        for h in range(heads):
            top, total = state[h]
            scores = jnp.where(allowed, score_ref[:, h * QB : (h + 1) * QB], MASKED)
            new_top = jnp.maximum(top, jnp.max(scores, axis=0, keepdims=True))
            fade = jnp.exp(top - new_top)
            probs = jnp.exp(scores - new_top)
            total = total * fade + jnp.sum(probs, axis=0, keepdims=True)
            part = slice(h * HEAD_DIM, (h + 1) * HEAD_DIM)
            acc_ref[part] = acc_ref[part] * fade + dot(value_t[part], probs.astype(BF))
            fresh.append((new_top, total))
        return tuple(fresh)

    begin = tuple(
        (jnp.full((1, QB), MASKED, F32), jnp.zeros((1, QB), F32)) for _ in range(heads)
    )
    state = lax.fori_loop(low_first // QB, start // QB + 1, body, begin)
    lse_ref[...] = jnp.zeros_like(lse_ref)
    for h in range(heads):
        top, total = state[h]
        part = slice(h * HEAD_DIM, (h + 1) * HEAD_DIM)
        acc_ref[part] = acc_ref[part] * (1.0 / total)
        lse_ref[h : h + 1] = top + jnp.log(total)
    heads_ref[...] = acc_ref[...].T.astype(BF)


def attend_call(sc, qkv):
    rows, width = qkv.shape[0], qkv.shape[1] // 3
    heads = width // HEAD_DIM
    return pl.pallas_call(
        functools.partial(attend_kernel, heads),
        grid_spec=pltpu.PrefetchScalarGridSpec(
            num_scalar_prefetch=3,
            grid=(rows // QB,),
            in_specs=[whole(qkv.shape)],
            out_specs=[
                pl.BlockSpec((QB, width), lambda i, *sc: (i, 0)),
                pl.BlockSpec((8, QB), lambda i, *sc: (0, i)),
            ],
            scratch_shapes=[
                pltpu.VMEM((width, rows), BF),
                pltpu.VMEM((width, heads * QB), BF),
                pltpu.VMEM((width, QB), F32),
                pltpu.VMEM((QB, heads * QB), F32),
            ],
        ),
        out_shape=[
            jax.ShapeDtypeStruct((rows, width), BF),
            jax.ShapeDtypeStruct((8, rows), F32),
        ],
        compiler_params=params(),
        cost_estimate=cost(60_000_000_000, 8_000_000),
        name="attend",
    )(*sc, qkv)


def spread(table_ref, out_ref, flat_ref):
    parities, levels, tables, high_rows, _ = table_ref.shape
    for piece in range(parities * levels):
        p, q = piece % parities, piece // parities
        for n in range(tables):
            for side in range(2):
                flat_ref[side, n * high_rows : (n + 1) * high_rows] = table_ref[
                    p, q, n, :, side * 128 : (side + 1) * 128
                ].astype(F32)

        def body(n, carry):
            for u in range(8):
                row = n * 8 + u
                for side in range(2):
                    at = pl.multiple_of((piece * high_rows + row) * LANES + side * 128, 128)
                    out_ref[:, pl.ds(at, 128)] = flat_ref[side, pl.ds(row, tables, stride=high_rows)]
            return carry

        lax.fori_loop(0, high_rows // 8, body, 0)


def attend_back_kernel(
    heads, rank, lengths, valid, grad_ref, qkv_ref, heads_ref, lse_ref, table_ref, mixed_ref, spread_ref,
    kt_ref, qt_ref, gt_ref, qs_ref, gs_ref, dqt_ref, dk_ref, dv_ref, score_ref, prob_ref, flat_ref,
):
    sc = (rank, lengths, valid)
    width = heads * HEAD_DIM
    step = pl.program_id(0)
    rows = qkv_ref.shape[0]

    @pl.when(step == 0)
    def _():
        for n in range(rows // QB):
            kt_ref[:, n * QB : (n + 1) * QB] = qkv_ref[n * QB : (n + 1) * QB, width : 2 * width].T
        dk_ref[...] = jnp.zeros_like(dk_ref)
        dv_ref[...] = jnp.zeros_like(dv_ref)

    start = pl.multiple_of(step * QB, QB)
    grad = grad_ref[...]
    grad_t = grad.T
    out_t = heads_ref[...].T
    product = grad_t.astype(F32) * out_t.astype(F32)
    query = qkv_ref[pl.ds(start, QB), :width] * jnp.asarray(HEAD_DIM**-0.5, BF)
    q_t = query.T
    inner = []
    for h in range(heads):
        part = slice(h * HEAD_DIM, (h + 1) * HEAD_DIM)
        inner.append(jnp.sum(product[part], axis=0, keepdims=True))
        qt_ref[:, h * QB : (h + 1) * QB] = head_rows(q_t, h)
        gt_ref[:, h * QB : (h + 1) * QB] = head_rows(grad_t, h)
    qs_ref[...] = q_t
    gs_ref[...] = grad_t
    dqt_ref[...] = jnp.zeros_like(dqt_ref)
    places = start + lax.broadcasted_iota(jnp.int32, (1, QB), 1)
    low, high = doc_bounds(sc, places)
    low_first, _ = doc_bounds(sc, start)

    def body(kb, carry):
        at = pl.multiple_of(kb * QB, QB)
        keys = qkv_ref[pl.ds(at, QB), width : 2 * width]
        values = qkv_ref[pl.ds(at, QB), 2 * width :]
        spot = at + lax.broadcasted_iota(jnp.int32, (QB, QB), 0)
        allowed = (spot >= low) & (spot <= high)
        score_ref[...] = dot(keys, qt_ref[...])
        prob_ref[...] = dot(values, gt_ref[...])
        for h in range(heads):
            part = slice(h * HEAD_DIM, (h + 1) * HEAD_DIM)
            lanes = slice(h * QB, (h + 1) * QB)
            scores = jnp.where(allowed, score_ref[:, lanes], MASKED)
            probs = jnp.exp(scores - lse_ref[h : h + 1])
            grad_scores = (probs * (prob_ref[:, lanes] - inner[h])).astype(BF)
            dqt_ref[part] += dot(kt_ref[part, pl.ds(at, QB)], grad_scores)
            dv_ref[part, pl.ds(at, QB)] += dot_nt(gs_ref[part], probs.astype(BF))
            dk_ref[part, pl.ds(at, QB)] += dot_nt(qs_ref[part], grad_scores)
        return carry

    lax.fori_loop(low_first // QB, start // QB + 1, body, 0)
    spread(table_ref, spread_ref, flat_ref)
    dq = (dqt_ref[...] * HEAD_DIM**-0.5).T.astype(BF)
    mixed_ref[pl.ds(start, QB), :width] = dq

    @pl.when(step == pl.num_programs(0) - 1)
    def _():
        for n in range(rows // QB):
            part = slice(n * QB, (n + 1) * QB)
            mixed_ref[part, width : 2 * width] = dk_ref[:, part].T.astype(BF)
            mixed_ref[part, 2 * width :] = dv_ref[:, part].T.astype(BF)


def attend_back_call(sc, grad, qkv, heads_out, lse, tables, hash_rows):
    rows, width = qkv.shape[0], qkv.shape[1] // 3
    heads = width // HEAD_DIM
    parities, levels, count, high_rows, lanes = tables.shape
    per = parities * levels // (rows // QB)
    if per == 1:
        table_spec = pl.BlockSpec(
            (1, 1, count, high_rows, lanes), lambda i, *sc: (i % 2, i // 2, 0, 0, 0)
        )
    else:
        table_spec = pl.BlockSpec(
            (2, per // 2, count, high_rows, lanes), lambda i, *sc: (0, i, 0, 0, 0)
        )
    return pl.pallas_call(
        functools.partial(attend_back_kernel, heads),
        grid_spec=pltpu.PrefetchScalarGridSpec(
            num_scalar_prefetch=3,
            grid=(rows // QB,),
            in_specs=[
                pl.BlockSpec((QB, width), lambda i, *sc: (i, 0)),
                whole(qkv.shape),
                pl.BlockSpec((QB, width), lambda i, *sc: (i, 0)),
                pl.BlockSpec((8, QB), lambda i, *sc: (0, i)),
                table_spec,
            ],
            out_specs=[
                whole((rows, 3 * width)),
                pl.BlockSpec((count, per * high_rows * lanes), lambda i, *sc: (0, i)),
            ],
            scratch_shapes=[
                pltpu.VMEM((width, rows), BF),
                pltpu.VMEM((width, heads * QB), BF),
                pltpu.VMEM((width, heads * QB), BF),
                pltpu.VMEM((width, QB), BF),
                pltpu.VMEM((width, QB), BF),
                pltpu.VMEM((width, QB), F32),
                pltpu.VMEM((width, rows), F32),
                pltpu.VMEM((width, rows), F32),
                pltpu.VMEM((QB, heads * QB), F32),
                pltpu.VMEM((QB, heads * QB), F32),
                pltpu.VMEM((2, count * high_rows, 128), F32),
            ],
        ),
        out_shape=[
            jax.ShapeDtypeStruct((rows, 3 * width), BF),
            jax.ShapeDtypeStruct((count, hash_rows), F32),
        ],
        compiler_params=params(),
        cost_estimate=cost(90_000_000_000, 12_000_000),
        name="attend_back",
    )(*sc, grad, qkv, heads_out, lse, tables)


def middle_kernel(
    seq_count, heads_ref, wo_in, x_in, gain_ref, c0_in, c2_in, wg_in, wu_in, wd_in, *refs
):
    half = seq_count // 2
    early = half // 2 + 1
    table_ins, refs = refs[:early], refs[early:]
    rest_out, fardown_out, grad_out, gain_out, keep_out, send_out = refs[:6]
    ostay_out, oaway_out, gh_out, table_ref = refs[6:10]
    piece_refs, refs = refs[10 : 10 + half], refs[10 + half :]
    (
        rest_ref, grad_ref, wo_ref, c0, c1, c2, c3, x_ref,
        ps_ref, pr_ref, py_ref, n_ref, wg_ref, wu_ref, wd_ref, act_ref, gg_ref, gu_ref,
        g0_ref, g1s_ref, g1r_ref, d0_ref, d1s_ref, d1r_ref,
        ys_ref, yr_ref, all_ref, gh_ref,
        stay_ref, away_ref, got_ref, up_ref, upgot_ref,
        snd, rcv, xsnd, xrcv, zsnd, zrcv, tsnd, trcv, psnd, prcv, loc, wloc, hloc,
    ) = refs
    fardown_ref, gb_ref, ar_ref, br_ref = x_ref, d0_ref, g1r_ref, d1r_ref
    me, sib, far, farsib, core = places()
    seq = lax.axis_index("seq")
    parity, place = lax.rem(seq, 2), seq // 2
    near = seq + 1 - 2 * parity
    level = [lax.rem(seq + 2 * j, seq_count) for j in range(1, half)]

    loads = [
        pltpu.make_async_copy(w_in, w_ref.at[: w_in.shape[0]], wloc.at[n])
        for n, (w_in, w_ref) in enumerate(((wg_in, wg_ref), (wu_in, wu_ref), (wd_in, wd_ref)))
    ]
    pairs = ((wo_in, wo_ref), (x_in, x_ref), (c0_in, c0), (c2_in, c2), (heads_ref.at[me], all_ref.at[me]))
    first = [
        pltpu.make_async_copy(src, dst, wloc.at[4 + n]) for n, (src, dst) in enumerate(pairs)
    ]
    for load in first + loads:
        load.start()
    greet([(seq, sib), (seq, far), (seq, farsib), (near, me)] + [(s, me) for s in level])
    rows, model = x_in.shape
    size = rows // STEPS
    units = wg_in.shape[0]
    long = rows // 2
    kinds = iter(range(100))

    def maker(src, dst, to, length=size):
        kind = next(kinds)

        def made(k):
            part = chunk(k, length)
            return push(src.at[part], dst.at[part], snd.at[kind, k], rcv.at[kind, k], (seq, to))

        return made

    head_copies = [
        maker(heads_ref.at[to], all_ref.at[me], to) for to in (far, farsib, sib)
    ]
    grad_copies = [maker(gh_ref.at[to], gh_out.at[me], to) for to in (far, farsib, sib)]
    two_sib = maker(n_ref.at[me], n_ref.at[me], sib)
    two_far = maker(n_ref.at[me], n_ref.at[me], far)
    two_on = maker(n_ref.at[far], n_ref.at[far], sib)
    back_one = maker(g1s_ref, g1r_ref, sib, long)
    down_one = maker(d1s_ref, d1r_ref, sib, long)
    back_a = maker(g1s_ref, ar_ref, sib, long)
    back_y = maker(ys_ref, yr_ref, far)
    down_three = maker(d1s_ref, br_ref, sib, long)
    cot_one = maker(c0_in, c1, sib, long)
    cot_three = maker(c2_in, c3, sib, long)

    def grad_home(k):
        part = chunk(k, size)
        return pltpu.make_async_copy(gh_ref.at[me, part], gh_out.at[me, part], loc.at[0, k])

    def table_spot(which, j):
        return table_ref.at[which, lax.rem(place + half - j, half), core]

    def table_home(j):
        return pltpu.make_async_copy(table_ins[j], table_spot(parity, j), hloc.at[j])

    def table_level(j):
        return push(
            table_ins[0], table_ref.at[parity, place, core], tsnd.at[0, j], trcv.at[0, j], (level[j - 1], me)
        )

    def table_near(j):
        spot = table_spot(parity, j)
        return push(table_ins[j] if j < early else spot, spot, tsnd.at[1, j], trcv.at[1, j], (near, me))

    def table_sib(same, j):
        spot = table_spot(parity if same else 1 - parity, j)
        kind = 2 if same else 3
        src = table_ins[j] if same and j < early else spot
        return push(src, spot, tsnd.at[kind, j], trcv.at[kind, j], (seq, sib))

    for k in range(STEPS):
        for made in head_copies:
            made(k).start()
    for j in range(early, half):
        table_level(j).start()
    for j in range(early):
        table_home(j).start()
        table_near(j).start()
        table_sib(True, j).start()
    for k in range(2):
        cot_one(k).start()
        cot_three(k).start()

    wide = act_ref.shape[0]
    if wide > units:
        for ref in (act_ref, gg_ref, gu_ref, wg_ref, wu_ref, wd_ref):
            ref[units:] = jnp.zeros((wide - units, ref.shape[1]), BF)
    for load in first + loads:
        load.wait()
    for k in range(2):
        cot_one(k).wait_recv()
        cot_three(k).wait_recv()

    def feed(m, block_a, block_b, ca, cb):
        part = chunk(m, long)
        normed = jnp.concatenate([n_ref[block_a, part], n_ref[block_b, part]], axis=0)
        cot = jnp.concatenate([ca[part], cb[part]], axis=0)
        gate = dot_nt(wg_ref[:units], normed)
        up = dot_nt(wu_ref[:units], normed)
        sig = jax.nn.sigmoid(gate)
        silu = gate * sig
        act = (silu * up).astype(BF)
        grad_act = dot_nt(wd_ref[:units], cot)
        grad_gate = (grad_act * up * sig * (1.0 + gate * (1.0 - sig))).astype(BF)
        grad_up = (grad_act * silu).astype(BF)
        lanes = [
            pl.ds(pl.multiple_of(block * rows + m * long, long), long) for block in (block_a, block_b)
        ]
        for ref, value in ((act_ref, act), (gg_ref, grad_gate), (gu_ref, grad_up)):
            ref[:units, lanes[0]] = value[:, :long]
            ref[:units, lanes[1]] = value[:, long:]
        pair = lambda ref: jnp.concatenate([ref[:, lanes[0]], ref[:, lanes[1]]], axis=1)
        back = dot_tn(pair(gg_ref), wg_ref[...]) + dot_tn(pair(gu_ref), wu_ref[...])
        return back, dot_tn(pair(act_ref), wd_ref[...])

    def own_chunk(k):
        part = chunk(k, size)
        hidden = x_ref[part].astype(F32) + dot_nt(all_ref[me, part], wo_ref[me])
        for made in head_copies:
            made(k).wait_recv()
        for block in (sib, far, farsib):
            hidden = hidden + dot_nt(all_ref[block, part], wo_ref[block])
        rest_ref[part] = hidden
        normed, _ = norm_rows(hidden, gain_ref[...])
        n_ref[me, part] = normed.astype(BF)
        two_far(k).start()
        two_sib(k).start()

    def own_half(m):
        own_chunk(2 * m)
        own_chunk(2 * m + 1)
        two_sib(2 * m).wait_recv()
        two_sib(2 * m + 1).wait_recv()
        part = chunk(m, long)
        back, down = feed(m, me, sib, c0, c1)
        g0_ref[part] = back[:long].astype(BF)
        g1s_ref[part] = back[long:].astype(BF)
        back_one(m).start()
        d0_ref[part] = down[:long].astype(BF)
        d1s_ref[part] = down[long:].astype(BF)
        down_one(m).start()

    each(own_half, 2)
    for j in range(early, half):
        table_level(j).wait_recv()
        table_near(j).start()
        table_sib(True, j).start()

    def far_sum(k):
        part = chunk(k, size)
        ys_ref[part] = (ys_ref[part].astype(F32) + ar_ref[part].astype(F32)).astype(BF)
        back_y(k).start()

    def far_half(m):
        part = chunk(m, long)
        back_one(m).wait_recv()
        g0_ref[part] = (g0_ref[part].astype(F32) + g1r_ref[part].astype(F32)).astype(BF)
        down_one(m).wait_recv()
        d0_ref[part] = (d0_ref[part].astype(F32) + d1r_ref[part].astype(F32)).astype(BF)
        for k in (2 * m, 2 * m + 1):
            two_far(k).wait_recv()
            two_on(k).start()
        for k in (2 * m, 2 * m + 1):
            two_on(k).wait_recv()
        back, down = feed(m, far, farsib, c2, c3)
        back_one(m).wait_send()
        g1s_ref[part] = back[long:].astype(BF)
        back_a(m).start()
        ys_ref[part] = back[:long].astype(BF)
        down_one(m).wait_send()
        d1s_ref[part] = down[long:].astype(BF)
        down_three(m).start()
        fardown_ref[part] = down[:long].astype(BF)
        back_a(m).wait_recv()
        far_sum(2 * m)
        far_sum(2 * m + 1)

    each(far_half, 2)

    piece = model // seq_count
    span = model // STEPS
    per = half // STEPS
    upright = piece % 128 == 0

    def weight_away(w, b):
        return push(
            away_ref.at[w, b], got_ref.at[w, b], xsnd.at[w, b], xrcv.at[w, b], (near, me)
        )

    def up_away(j):
        b = lax.rem(place + j, half)
        return push(
            up_ref.at[b], upgot_ref.at[j - 1], zsnd.at[j], zrcv.at[j],
            (lax.rem(seq + 2 * j, seq_count), me),
        )

    def weight_tile(w, k):
        cots = (c0, c1, c2, c3)
        order = (me, sib, far, farsib)
        left = (act_ref, gg_ref, gu_ref)[w]
        total = None
        for r in range(4):
            cols = chunk(k, span)
            right = cots[r][:, cols] if w == 0 else n_ref[order[r], :, cols]
            lanes = pl.ds(pl.multiple_of(order[r] * rows, rows), rows)
            term = dot(left[:units, lanes], right)
            total = term if total is None else total + term
        return total.astype(BF)

    def weights_step(kk):
        k = lax.rem(place // per + 1 + kk, STEPS)
        for w in range(3):
            tile = weight_tile(w, k)
            tile = tile if upright else tile.T
            for n in range(per):
                b = k * per + n
                take = lambda i: slice(i * piece, (i + 1) * piece)
                even = tile[:, take(2 * n)] if upright else tile[take(2 * n)]
                odd = tile[:, take(2 * n + 1)] if upright else tile[take(2 * n + 1)]
                if w == 2:
                    up_ref[b, 0] = even
                    up_ref[b, 1] = odd

                    @pl.when(b != place)
                    def _():
                        up_away(lax.rem(b + half - place, half)).start()
                else:

                    @pl.when(parity == 0)
                    def _():
                        stay_ref[w, b] = even
                        away_ref[w, b] = odd

                    @pl.when(parity == 1)
                    def _():
                        stay_ref[w, b] = odd
                        away_ref[w, b] = even

                    weight_away(w, b).start()

    gain_out[...] = jnp.zeros_like(gain_out)

    def leave(k, n, ref, out):
        part = chunk(k, size)
        return pltpu.make_async_copy(ref.at[part], out.at[part], loc.at[1 + n, k])

    def back_chunk(k):
        weights_step(k)
        part = chunk(k, size)
        back_y(k).wait_recv()
        grad_norm = g0_ref[part].astype(F32) + yr_ref[part].astype(F32)
        hidden = rest_ref[part]
        _, scaling = norm_rows(hidden, gain_ref[...])
        grad_rows, grad_gain = norm_back(hidden, scaling, gain_ref[...], grad_norm)
        grad = c0[part].astype(F32) + grad_rows
        grad_ref[part] = grad
        leave(k, 0, grad_ref, grad_out).start()
        rest_ref[part] = hidden + d0_ref[part].astype(F32)
        leave(k, 1, rest_ref, rest_out).start()
        fardown_ref[part] = (fardown_ref[part].astype(F32) + br_ref[part].astype(F32)).astype(BF)
        leave(k, 2, fardown_ref, fardown_out).start()
        gain_out[...] += grad_gain
        gb_ref[part] = grad.astype(BF)
        low = grad.astype(BF)
        for block in (far, farsib, sib, me):
            gh_ref[block, part] = dot(low, wo_ref[block]).astype(BF)
        for made in grad_copies:
            made(k).start()
        grad_home(k).start()

    for m in range(2):
        down_three(m).wait_recv()
    each(back_chunk, STEPS)
    for j in range(half):
        table_near(j).wait_recv()
        table_sib(False, j).start()

    def out_part(block):
        return dot_tn(gb_ref[...], all_ref[block])

    def out_sib(n):
        return push(ps_ref.at[n], pr_ref.at[n], psnd.at[n], prcv.at[n], (seq, sib))

    out_far = push(ps_ref.at[0], py_ref, psnd.at[2], prcv.at[2], (seq, far))
    for n, block in enumerate((farsib, sib)):
        ps_ref[n] = out_part(block).astype(BF)
        out_sib(n).start()
    total = out_part(far)
    out_sib(0).wait_recv()
    out_sib(0).wait_send()
    ps_ref[0] = (total + pr_ref[0].astype(F32)).astype(BF)
    out_far.start()
    total = out_part(me)
    out_sib(1).wait_recv()
    total = total + pr_ref[1].astype(F32)
    out_far.wait_recv()
    pr_ref[0] = (total + py_ref[...].astype(F32)).astype(BF)
    for j in range(half):
        b = lax.rem(place + j, half)
        take = lambda which: pl.ds(pl.multiple_of((2 * b + which) * piece, piece), piece)
        ostay_out[j] = pr_ref[0, take(parity)]
        oaway_out[j] = pr_ref[0, take(1 - parity)]

    for j in range(half):
        b = lax.rem(place + j, half)
        for w in range(2):
            weight_away(w, b).wait_recv()
            piece_refs[j][w] = (stay_ref[w, b].astype(F32) + got_ref[w, b].astype(F32)).astype(BF)

    def up_sum(which):
        total = up_ref[place, which].astype(F32)
        for j in range(1, half):
            total = total + upgot_ref[j - 1, which].astype(F32)
        return total.astype(BF)

    for j in range(1, half):
        up_away(j).wait_recv()
    keep_out[...] = up_sum(parity)
    send_out[...] = up_sum(1 - parity)

    def close(k):
        grad_home(k).wait()
        leave(k, 0, grad_ref, grad_out).wait()
        leave(k, 1, rest_ref, rest_out).wait()
        leave(k, 2, fardown_ref, fardown_out).wait()
        for made in grad_copies:
            made(k).wait_recv()
        for made in [two_sib, two_far, two_on, back_y] + head_copies + grad_copies:
            made(k).wait_send()

    each(close, STEPS)
    for m in range(2):
        for made in (back_a, down_three, cot_one, cot_three):
            made(m).wait_send()
    for copy in (out_sib(1), out_far):
        copy.wait_send()
    for j in range(early):
        table_home(j).wait()
    for j in range(half):
        table_sib(True, j).wait_recv()
        table_sib(False, j).wait_recv()
        table_near(j).wait_send()
        table_sib(True, j).wait_send()
        table_sib(False, j).wait_send()
        for w in range(2):
            weight_away(w, j).wait_send()
    for j in range(early, half):
        table_level(j).wait_send()
    for j in range(1, half):
        up_away(j).wait_send()


def middle_call(heads_out, wo, x, gain, cot, cot_far, weights, tables):
    seq_count = lax.axis_size("seq")
    rows, model = x.shape
    half = seq_count // 2
    piece = model // seq_count
    units = weights[0].shape[0]
    wide = units + -units % 256
    block = (units, piece) if piece % 128 == 0 else (piece, units)
    dma = pltpu.SemaphoreType.DMA
    shape = jax.ShapeDtypeStruct
    vm = pltpu.VMEM
    rows_bf = vm((rows, model), BF)
    return pl.pallas_call(
        functools.partial(middle_kernel, seq_count),
        in_specs=[ANY] * 3 + [VM] + [ANY] * (5 + len(tables)),
        out_specs=[ANY] * 3 + [VM] * 5 + [ANY] * 2 + [VM] * half,
        out_shape=[
            shape((rows, model), F32),
            shape((rows, model), BF),
            shape((rows, model), F32),
            shape((1, model), F32),
            shape(block, BF),
            shape(block, BF),
            shape((half, piece, heads_out.shape[2]), BF),
            shape((half, piece, heads_out.shape[2]), BF),
            shape(heads_out.shape, BF),
            shape((2, half, 2) + tables[0].shape, BF),
        ]
        + [shape((2,) + block, BF)] * half,
        scratch_shapes=[vm((rows, model), F32)] * 2
        + [vm(wo.shape, BF)]
        + [rows_bf] * 5
        + [vm((2,) + wo.shape[1:], BF), vm((2,) + wo.shape[1:], BF), vm(wo.shape[1:], BF)]
        + [vm((4, rows, model), BF)]
        + [vm((wide, model), BF)] * 3
        + [vm((wide, 4 * rows), BF)] * 3
        + [rows_bf] * 8
        + [vm(heads_out.shape, BF)] * 2
        + [vm((2, half) + block, BF)] * 3
        + [vm((half, 2) + block, BF), vm((half - 1, 2) + block, BF)]
        + [dma((20, STEPS))] * 2
        + [dma((2, half))] * 2
        + [dma((half,))] * 2
        + [dma((4, half))] * 2
        + [dma((3,))] * 2
        + [dma((4, STEPS)), dma((9,)), dma((half // 2 + 1,))],
        compiler_params=params(collective_id=1, has_side_effects=True),
        cost_estimate=cost(100_000_000_000, 30_000_000),
        name="middle",
    )(heads_out, wo, x, gain, cot, cot_far, *weights, *tables)


def last_kernel(
    seq_count, mixed_in, w_in, x_in, gain_ref, grad_in, n_in, gain_in,
    out_out, wqkv_ref, gains_ref,
    mixed_ref, w_ref, x_ref, grad_ref, n_ref,
    as_ref, ar_ref, ys_ref, yr_ref, bs_ref, br_ref, dw_ref, got_ref, sum_ref, zr_ref, gs_ref, gr_ref,
    snd, rcv, xsnd, xrcv, zsnd, zrcv, gsnd, grcv, loc,
):
    me, sib, far, farsib, core = places()
    seq = lax.axis_index("seq")
    parity, place, half = lax.rem(seq, 2), seq // 2, seq_count // 2
    near = seq + 1 - 2 * parity
    level = [lax.rem(seq + 2 * j, seq_count) for j in range(1, half)]
    loads = [
        pltpu.make_async_copy(src, dst, loc.at[n])
        for n, (src, dst) in enumerate(
            (
                (mixed_in, mixed_ref), (w_in, w_ref), (n_in, n_ref), (x_in, x_ref), (grad_in, grad_ref),
            )
        )
    ]
    for load in loads:
        load.start()
    greet([(seq, sib), (seq, far), (near, me)] + [(s, me) for s in level])
    rows, model = x_ref.shape
    size = rows // STEPS
    piece = model // seq_count
    wide = mixed_ref.shape[-1]

    def copy(kind, k, src, dst, to):
        return push(
            src.at[chunk(k, size)], dst.at[chunk(k, size)], snd.at[kind, k], rcv.at[kind, k], (seq, to)
        )

    back_a = lambda k: copy(0, k, as_ref, ar_ref, sib)
    back_y = lambda k: copy(1, k, ys_ref, yr_ref, far)
    back_b = lambda k: copy(2, k, bs_ref, br_ref, sib)

    def near_copy(b):
        return push(dw_ref.at[1, b], got_ref.at[b], xsnd.at[b], xrcv.at[b], (near, me))

    def level_copy(j):
        b = lax.rem(place + j, half)
        return push(
            sum_ref.at[b], zr_ref.at[j], zsnd.at[j], zrcv.at[j], (lax.rem(seq + 2 * j, seq_count), me)
        )

    width = w_ref.shape[2]

    def project(block, k):
        part = chunk(k, size)
        terms = [
            dot_nt(mixed_ref[block, part, c * width : (c + 1) * width], w_ref[c]) for c in range(3)
        ]
        return terms[0] + terms[1] + terms[2]

    def send_three(k):
        as_ref[chunk(k, size)] = project(farsib, k).astype(BF)
        back_a(k).start()

    def send_two(k):
        part = project(far, k)
        back_a(k).wait_recv()
        ys_ref[chunk(k, size)] = (part + ar_ref[chunk(k, size)].astype(F32)).astype(BF)
        back_y(k).start()

    def send_one(k):
        bs_ref[chunk(k, size)] = project(sib, k).astype(BF)
        back_b(k).start()

    span = model // STEPS
    per = half // STEPS

    def weights_step(kk):
        k = lax.rem(place // per + 1 + kk, STEPS)
        cols = chunk(k, span)
        total = None
        for r in range(4):
            term = dot_tn(n_ref[r, :, cols], mixed_ref[r])
            total = term if total is None else total + term
        tile = total.astype(BF).reshape(per, 2, piece, wide)
        for j in range(per):
            b = k * per + j

            @pl.when(parity == 0)
            def _():
                dw_ref[0, b] = tile[j, 0]
                dw_ref[1, b] = tile[j, 1]

            @pl.when(parity == 1)
            def _():
                dw_ref[0, b] = tile[j, 1]
                dw_ref[1, b] = tile[j, 0]

        for j in range(per):
            near_copy(k * per + j).start()

    for load in loads[:2]:
        load.wait()
    each(send_three, STEPS)
    loads[2].wait()
    weights_step(0)
    each(send_two, STEPS)
    each(lambda k: weights_step(k + 1), STEPS - 1)
    each(send_one, STEPS)
    for load in loads[3:]:
        load.wait()

    gs_ref[...] = jnp.zeros_like(gs_ref)

    def leave(k):
        part = chunk(k, size)
        return pltpu.make_async_copy(grad_ref.at[part], out_out.at[part], loc.at[5 + k])

    def own_chunk(k):
        part = chunk(k, size)
        total = project(me, k)
        x = x_ref[part].astype(F32)
        _, scaling = norm_rows(x, gain_ref[...])
        back_b(k).wait_recv()
        back_y(k).wait_recv()
        grad_norm = total + br_ref[part].astype(F32) + yr_ref[part].astype(F32)
        grad_rows, grad_gain = norm_back(x, scaling, gain_ref[...], grad_norm)
        grad_ref[part] = grad_ref[part] + grad_rows
        leave(k).start()
        gs_ref[0, 0:1] += grad_gain

    def near_sum(b):
        near_copy(b).wait_recv()
        sum_ref[b] = (dw_ref[0, b].astype(F32) + got_ref[b].astype(F32)).astype(BF)

        @pl.when(b != place)
        def _():
            level_copy(lax.rem(b + half - place, half)).start()

    def both(kk):
        k = lax.rem(place // per + 1 + kk, STEPS)
        own_chunk(kk)
        for n in range(per):
            near_sum(k * per + n)

    each(both, STEPS)

    gs_ref[0, 1:2] = gain_in[...]
    others = [(seq, sib), (seq, far), (near, me)]

    def gain_copy(n, slot, to):
        return push(gs_ref.at[n], gr_ref.at[slot], gsnd.at[slot], grcv.at[slot], to)

    for n, to in enumerate(others):
        gain_copy(n, n, to).start()
        gain_copy(n, n, to).wait_recv()
        gs_ref[n + 1] = gs_ref[n] + gr_ref[n]
    for j in range(1, half):
        gain_copy(3, 2 + j, (level[j - 1], me)).start()
    gains = gs_ref[3]
    for j in range(1, half):
        gain_copy(3, 2 + j, (level[j - 1], me)).wait_recv()
        gains = gains + gr_ref[2 + j]
    gains_ref[...] = gains

    total = sum_ref[place].astype(F32)
    for j in range(1, half):
        level_copy(j).wait_recv()
        total = total + zr_ref[j].astype(F32)
    for c in range(3):
        wqkv_ref[c] = total[:, c * width : (c + 1) * width]

    def close(k):
        for made in (back_a, back_y, back_b):
            made(k).wait_send()

    each(close, STEPS)
    each(lambda k: leave(k).wait(), STEPS)
    each(lambda b: near_copy(b).wait_send(), half)
    for n, to in enumerate(others):
        gain_copy(n, n, to).wait_send()
    for j in range(1, half):
        gain_copy(3, 2 + j, (level[j - 1], me)).wait_send()
        level_copy(j).wait_send()


def last_call(mixed, w, x, gain, grad, normed, gain_two):
    seq_count = lax.axis_size("seq")
    rows, model = x.shape
    half = seq_count // 2
    piece = model // seq_count
    wide, width = mixed.shape[-1], w.shape[-1]
    dma = pltpu.SemaphoreType.DMA
    shape = jax.ShapeDtypeStruct
    rows_bf = pltpu.VMEM((rows, model), BF)
    pieces = pltpu.VMEM((half, piece, wide), BF)
    return pl.pallas_call(
        functools.partial(last_kernel, seq_count),
        in_specs=[ANY] * 3 + [VM] + [ANY] * 2 + [VM],
        out_specs=[ANY] + [VM] * 2,
        out_shape=[
            shape((rows, model), F32),
            shape((3, piece, width), F32),
            shape((8, model), F32),
        ],
        scratch_shapes=[
            pltpu.VMEM(a.shape, a.dtype) for a in (mixed, w, x, grad, normed)
        ]
        + [rows_bf] * 6
        + [pltpu.VMEM((2, half, piece, wide), BF), pieces, pieces, pieces]
        + [pltpu.VMEM((4, 8, model), F32), pltpu.VMEM((half + 2, 8, model), F32)]
        + [
            dma((3, STEPS)),
            dma((3, STEPS)),
            dma((half,)),
            dma((half,)),
            dma((half,)),
            dma((half,)),
            dma((half + 2,)),
            dma((half + 2,)),
            dma((5 + STEPS,)),
        ],
        compiler_params=params(collective_id=2, has_side_effects=True),
        cost_estimate=cost(90_000_000_000, 30_000_000),
        name="last",
    )(mixed, w, x, gain, grad, normed, gain_two)


def shards(
    latents_in,
    gain_one,
    w_qkv,
    w_out,
    gain_two,
    w_gate,
    w_up,
    w_down,
    cotangent,
    doc_lengths,
    valid_lengths,
    hash_ids,
    hash_weights,
):
    local_rows, model_width = latents_in.shape
    local_width = w_qkv.shape[2]
    group_rows = 4 * local_rows
    units = w_gate.shape[1]
    rank = lax.axis_index("tp")
    seq_count = lax.axis_size("seq")
    sc = (jnp.full((1,), rank, jnp.int32), doc_lengths.reshape(-1), valid_lengths.reshape(-1))
    gain_one, gain_two = gain_one[None], gain_two[None]

    per_seq = -(-HASH_ROWS // seq_count)
    high_rows = -(-per_seq // (LANES * 8)) * 8

    qkv_weight = w_qkv.transpose(1, 0, 2)
    piece = model_width // seq_count
    wo_four = w_out.reshape(seq_count // 2, 2, piece, local_width)
    normed, qkv, sums, wo_all = front_call(
        latents_in, gain_one, qkv_weight, hash_ids, hash_weights, wo_four, high_rows
    )
    wo_all = wo_all.reshape(4, model_width, local_width)
    qkv, cotangent_late = lax.optimization_barrier((qkv, cotangent))

    def level_flip(x, j):
        return lax.ppermute(x, "seq", [(s, (s + 2 * j) % seq_count) for s in range(seq_count)])

    table_parts = [sums] + [level_flip(sums, j) for j in range(1, seq_count // 4 + 1)]
    qkv = qkv.reshape(group_rows, 3 * local_width)
    cot_far = flip(cotangent_late, "tp", 2)
    heads_out, lse = attend_call(sc, qkv)
    heads_four = heads_out.reshape(4, local_rows, local_width)
    (
        rest, far_down, grad_hidden, gain_two_part, up_keep, up_send, out_stay, out_away,
        grad_heads, hash_parts, *pieces,
    ) = middle_call(
        heads_four, wo_all, latents_in, gain_two, cotangent, cot_far,
        (w_gate.T, w_up.T, w_down.T), table_parts,
    )
    out_got = flip(out_away, "seq", 1)
    down_far = flip(far_down, "tp", 2)
    up_got = flip(up_send, "seq", 1)
    arrived = [level_flip(pieces[j], j) for j in range(1, seq_count // 2)]
    hash_parts = hash_parts.reshape(2, seq_count // 2, hash_ids.shape[0], high_rows, LANES)
    mixed, hash_counts = attend_back_call(
        sc, grad_heads.reshape(group_rows, local_width), qkv, heads_out, lse, hash_parts, HASH_ROWS
    )
    mixed, up_got, arrived, down_far, out_got = lax.optimization_barrier(
        (mixed, up_got, arrived, down_far, out_got)
    )
    out_half = [
        (out_stay[j].astype(F32) + out_got[j].astype(F32)).astype(BF) for j in range(seq_count // 2)
    ]
    mixed, out_half = lax.optimization_barrier((mixed, out_half))
    out_total = out_half[0].astype(F32)
    for j in range(1, seq_count // 2):
        out_total = out_total + level_flip(out_half[j], j).astype(F32)
    grad_latents, qkv_total, gains = last_call(
        mixed.reshape(4, local_rows, -1), qkv_weight, latents_in, gain_one, grad_hidden,
        normed, gain_two_part,
    )
    total = pieces[0].astype(F32)
    for piece in arrived:
        total = total + piece.astype(F32)
    up_total = up_keep.astype(F32) + up_got.astype(F32)
    latents_out = (rest + down_far.astype(F32)).astype(BF)
    upright = lambda w: w.T if w.shape[0] == units else w
    return (
        latents_out,
        grad_latents,
        gains[0],
        qkv_total.transpose(1, 0, 2),
        out_total,
        gains[1],
        upright(total[1]),
        upright(up_total),
        upright(total[0]),
        hash_counts,
    )


def solution(mesh):
    in_specs = (
        P(("seq", "tp"), None),
        P(),
        P(None, None, "tp"),
        P(None, "tp"),
        P(),
        P(None, "tp"),
        P(None, "tp"),
        P(None, "tp"),
        P(("seq", "tp"), None),
        P("seq", None),
        P("seq", None),
        P(None, ("seq", "tp")),
        P(None, ("seq", "tp")),
    )
    out_specs = (
        P(("seq", "tp"), None),
        P(("seq", "tp"), None),
        P(),
        P("seq", None, "tp"),
        P("seq", "tp"),
        P(),
        P("seq", "tp"),
        P("seq", "tp"),
        P("seq", "tp"),
        P(),
    )
    return jax.shard_map(shards, mesh=mesh, in_specs=in_specs, out_specs=out_specs, check_vma=False)
```

```python
import functools

import jax
import jax.numpy as jnp
from jax import lax
from jax.experimental import pallas as pl
from jax.experimental.pallas import tpu as pltpu
from jax.sharding import PartitionSpec as P

HEAD_DIM = 64
HASH_ROWS = 500002
EPSILON = 1e-05
MASKED = -1e30
BF = jnp.bfloat16
F32 = jnp.float32
QB = 256
LANES = 256
STEPS = 4
VMEM_BYTES = 60 * 1024 * 1024
MESH = pl.DeviceIdType.MESH


def flip(x, axis, bits):
    count = lax.axis_size(axis)
    return lax.ppermute(x, axis, [(i, i ^ bits) for i in range(count)])


def dot(a, b):
    return lax.dot_general(a, b, (((1,), (0,)), ((), ())), preferred_element_type=F32)


def dot_nt(a, b):
    return lax.dot_general(a, b, (((1,), (1,)), ((), ())), preferred_element_type=F32)


def dot_tn(a, b):
    return lax.dot_general(a, b, (((0,), (0,)), ((), ())), preferred_element_type=F32)


def cost(flops, moved):
    return pl.CostEstimate(flops=flops, bytes_accessed=moved, transcendentals=0)


def params(**more):
    return pltpu.CompilerParams(vmem_limit_bytes=VMEM_BYTES, **more)


def whole(shape):
    return pl.BlockSpec(shape, lambda i, *sc: (0,) * len(shape))


VM = pl.BlockSpec(memory_space=pltpu.VMEM)
ANY = pl.BlockSpec(memory_space=pl.ANY)


def places():
    me = lax.axis_index("tp")
    core = lax.rem(me, 2)
    sib = me + 1 - 2 * core
    far = lax.rem(me + 2, 4)
    return me, sib, far, lax.rem(sib + 2, 4), core


def push(src, dst, send, recv, where):
    return pltpu.make_async_remote_copy(
        src_ref=src,
        dst_ref=dst,
        send_sem=send,
        recv_sem=recv,
        device_id={"seq": where[0], "tp": where[1]},
        device_id_type=MESH,
    )


def greet(others):
    barrier = pltpu.get_barrier_semaphore()
    for seq, tp in others:
        pl.semaphore_signal(
            barrier, inc=1, device_id={"seq": seq, "tp": tp}, device_id_type=MESH
        )
    pl.semaphore_wait(barrier, len(others))


def each(body, count):
    lax.fori_loop(0, count, lambda k, c: (body(k), c)[1], 0)


def chunk(k, size):
    return pl.ds(pl.multiple_of(k * size, size), size)


def norm_rows(row_data, gain):
    scaling = lax.rsqrt(jnp.mean(row_data * row_data, axis=-1, keepdims=True) + EPSILON)
    return (row_data * scaling * gain, scaling)


def norm_back(row_data, scaling, gain, grad_norm):
    weighted = grad_norm * gain
    inner_mean = jnp.mean(weighted * row_data, axis=-1, keepdims=True)
    grad_rows = scaling * weighted - row_data * scaling * scaling * scaling * inner_mean
    grad_gain = jnp.sum(grad_norm * row_data * scaling, axis=0, keepdims=True)
    return (grad_rows, grad_gain)


def front_kernel(
    seq_count, x_ref, gain_ref, w_ref, ids_ref, weights_ref, wo_ref, n_out, qkv_out, hash_ref, out_out,
    out_ref, n_ref, qkv_ref, pair_ref, pack_ref, sum_ref, snd, rcv, psnd, prcv, osnd, orcv, loc,
):
    me, sib, far, farsib, core = places()
    seq = lax.axis_index("seq")
    near = seq + 1 - 2 * lax.rem(seq, 2)
    parity, place, half = lax.rem(seq, 2), seq // 2, seq_count // 2
    level = [lax.rem(seq + 2 * j, seq_count) for j in range(1, half)]
    greet([(seq, sib), (seq, far), (near, me)] + [(s, me) for s in level])
    rows = x_ref.shape[0]
    size = rows // STEPS
    tables = ids_ref.shape[0] // 2

    def pairs(low):
        ids = jnp.where(core == low, ids_ref[:tables], ids_ref[tables:]).astype(F32)
        weights = jnp.where(core == low, weights_ref[:tables], weights_ref[tables:])
        return jnp.concatenate([ids, weights, jnp.zeros((8 - 2 * tables, rows), F32)], axis=0)

    pack_ref[parity, place, me] = pairs(0)
    pair_ref[...] = pairs(1)
    mine = pack_ref.at[parity, place, me]
    stage_sib = push(pair_ref, mine, psnd.at[0], prcv.at[0], (seq, sib))
    stage_sib.start()
    both = pack_ref.at[parity, place, pl.ds(me - core, 2)]
    stage_far = push(both, both, psnd.at[1], prcv.at[1], (seq, far))
    four = pack_ref.at[parity, place]
    stage_level = [
        push(four, four, psnd.at[2 + j], prcv.at[2 + j], (s, me)) for j, s in enumerate(level)
    ]
    plane = pack_ref.at[parity]
    stage_near = push(plane, plane, psnd.at[half + 1], prcv.at[half + 1], (near, me))

    out_ref[me] = wo_ref[...]
    eighth = out_ref.at[me, place, parity]
    out_far = push(eighth, eighth, osnd.at[0], orcv.at[0], (seq, far))
    got_eighth = out_ref.at[far, place, parity]
    out_level = [
        push(got_eighth, got_eighth, osnd.at[2 + j], orcv.at[2 + j], (s, me))
        for j, s in enumerate(level)
    ]
    got_plane = out_ref.at[far, :, parity]
    out_near = push(got_plane, got_plane, osnd.at[half + 1], orcv.at[half + 1], (near, me))
    out_sib = push(out_ref.at[me], out_ref.at[me], osnd.at[1], orcv.at[1], (seq, sib))
    out_on = push(out_ref.at[far], out_ref.at[far], osnd.at[half + 2], orcv.at[half + 2], (seq, sib))

    def own(kind, k, to, block):
        part = n_ref.at[block, chunk(k, size)]
        return push(part, part, snd.at[kind, k], rcv.at[kind, k], (seq, to))

    for k in range(STEPS):
        part = slice(k * size, (k + 1) * size)
        normed, _ = norm_rows(x_ref[part].astype(F32), gain_ref[...])
        n_ref[me, part] = normed.astype(BF)
        if k == 0:
            stage_sib.wait_recv()
            stage_far.start()
            out_far.start()
            out_sib.start()
        own(1, k, far, me).start()
        own(0, k, sib, me).start()

    width = w_ref.shape[2]

    def project(block, k, length):
        part = chunk(k, length)
        for c in range(3):
            qkv_ref[block, part, c * width : (c + 1) * width] = dot(
                n_ref[block, part], w_ref[c]
            ).astype(BF)

    def out_home(block):
        return pltpu.make_async_copy(out_ref.at[block], out_out.at[block], loc.at[2, block])

    out_home(me).start()

    def homes(block):
        return [
            pltpu.make_async_copy(n_ref.at[block], n_out.at[block], loc.at[0, block]),
            pltpu.make_async_copy(qkv_ref.at[block], qkv_out.at[block], loc.at[1, block]),
        ]

    each(lambda k: project(me, k, rows // 2), 2)
    for copy in homes(me):
        copy.start()
    stage_far.wait_recv()
    for copy in stage_level:
        copy.start()
    out_far.wait_recv()
    for copy in out_level:
        copy.start()
    for k in range(STEPS):
        own(0, k, sib, me).wait_recv()
    each(lambda k: project(sib, k, rows // 2), 2)
    for copy in homes(sib):
        copy.start()

    def far_chunk(k):
        own(1, k, far, me).wait_recv()
        own(2, k, sib, far).start()
        project(far, k, size)

    def farsib_chunk(k):
        own(2, k, sib, far).wait_recv()
        project(farsib, k, size)

    far_chunk(0)
    for copy in stage_level:
        copy.wait_recv()
    stage_near.start()

    sum_ref[...] = jnp.zeros_like(sum_ref)
    high_rows = sum_ref.shape[1]
    first = seq * (high_rows * LANES)

    def sums(which):
        def body(b):
            for table in range(tables):
                line = lambda row: jnp.concatenate(
                    [pack_ref[which, b, t, row : row + 1] for t in range(4)], axis=1
                )
                ids = line(table).astype(jnp.int32) - first
                weights = line(table + tables)
                high = lax.broadcasted_iota(jnp.int32, (high_rows, 4 * rows), 0) == (ids >> 8)
                low = lax.broadcasted_iota(jnp.int32, (LANES, 4 * rows), 0) == (ids & (LANES - 1))
                high = jnp.where(high, 1.0, 0.0).astype(BF)
                low = jnp.where(low, weights, 0.0).astype(BF)
                sum_ref[table] += dot_nt(high, low)

        each(body, half)

    sums(parity)
    for copy in out_level:
        copy.wait_recv()
    out_near.start()
    each(lambda k: far_chunk(k + 1), STEPS - 2)
    each(farsib_chunk, STEPS - 1)
    stage_near.wait_recv()
    sums(1 - parity)
    out_near.wait_recv()
    out_on.start()
    out_home(far).start()
    out_sib.wait_recv()
    out_home(sib).start()
    far_chunk(STEPS - 1)
    for copy in homes(far):
        copy.start()
    hash_ref[...] = sum_ref[...].astype(BF)
    out_on.wait_recv()
    out_home(farsib).start()
    farsib_chunk(STEPS - 1)
    for copy in homes(farsib):
        copy.start()
    for k in range(STEPS):
        for kind in range(3):
            own(kind, k, sib, me).wait_send()
    stage_sib.wait_send()
    stage_far.wait_send()
    for copy in stage_level:
        copy.wait_send()
    stage_near.wait_send()
    for copy in [out_far, out_near, out_sib, out_on] + out_level:
        copy.wait_send()
    for block in (me, sib, far, farsib):
        out_home(block).wait()
    for block in (me, sib, far, farsib):
        for copy in homes(block):
            copy.wait()


def front_call(x, gain, w, ids, weights, wo, high_rows):
    seq_count = lax.axis_size("seq")
    rows, model = x.shape
    width = w.shape[0] * w.shape[2]
    tables = ids.shape[0] // 2
    half = seq_count // 2
    dma = pltpu.SemaphoreType.DMA
    return pl.pallas_call(
        functools.partial(front_kernel, seq_count),
        in_specs=[VM] * 6,
        out_specs=[ANY] * 2 + [VM, ANY],
        out_shape=[
            jax.ShapeDtypeStruct((4, rows, model), BF),
            jax.ShapeDtypeStruct((4, rows, width), BF),
            jax.ShapeDtypeStruct((tables, high_rows, LANES), BF),
            jax.ShapeDtypeStruct((4,) + wo.shape, BF),
        ],
        scratch_shapes=[
            pltpu.VMEM((4,) + wo.shape, BF),
            pltpu.VMEM((4, rows, model), BF),
            pltpu.VMEM((4, rows, width), BF),
            pltpu.VMEM((8, rows), F32),
            pltpu.VMEM((2, half, 4, 8, rows), F32),
            pltpu.VMEM((tables, high_rows, LANES), F32),
            dma((3, STEPS)),
            dma((3, STEPS)),
            dma((half + 2,)),
            dma((half + 2,)),
            dma((half + 3,)),
            dma((half + 3,)),
            dma((3, 4)),
        ],
        compiler_params=params(collective_id=0, has_side_effects=True),
        cost_estimate=cost(1_000_000, 1_000_000),
        name="front",
    )(x, gain, w, ids, weights, wo)


def doc_bounds(sc, places):
    _, lengths, valid = sc
    one = lengths[0]
    two = one + lengths[1]
    low = jnp.where(places >= two, two, jnp.where(places >= one, one, 0))
    end = jnp.where(
        places >= two, two + valid[2], jnp.where(places >= one, one + valid[1], valid[0])
    )
    return low, jnp.minimum(places, end - 1)


def head_rows(x, h):
    where = lax.broadcasted_iota(jnp.int32, x.shape, 0) // HEAD_DIM
    return jnp.where(where == h, x, jnp.zeros_like(x))


def attend_kernel(heads, rank, lengths, valid, qkv_ref, heads_ref, lse_ref, vt_ref, qt_ref, acc_ref, score_ref):
    sc = (rank, lengths, valid)
    width = heads * HEAD_DIM
    step = pl.program_id(0)

    @pl.when(step == 0)
    def _():
        for n in range(qkv_ref.shape[0] // QB):
            vt_ref[:, n * QB : (n + 1) * QB] = qkv_ref[n * QB : (n + 1) * QB, 2 * width :].T

    start = pl.multiple_of(step * QB, QB)
    q_t = qkv_ref[pl.ds(start, QB), :width].T * jnp.asarray(HEAD_DIM**-0.5, BF)
    for h in range(heads):
        qt_ref[:, h * QB : (h + 1) * QB] = head_rows(q_t, h)
    acc_ref[...] = jnp.zeros_like(acc_ref)
    places = start + lax.broadcasted_iota(jnp.int32, (1, QB), 1)
    low, high = doc_bounds(sc, places)
    low_first, _ = doc_bounds(sc, start)

    def body(kb, state):
        at = pl.multiple_of(kb * QB, QB)
        keys = qkv_ref[pl.ds(at, QB), width : 2 * width]
        value_t = vt_ref[:, pl.ds(at, QB)]
        spot = at + lax.broadcasted_iota(jnp.int32, (QB, QB), 0)
        allowed = (spot >= low) & (spot <= high)
        score_ref[...] = dot(keys, qt_ref[...])
        fresh = []
        for h in range(heads):
            top, total = state[h]
            scores = jnp.where(allowed, score_ref[:, h * QB : (h + 1) * QB], MASKED)
            new_top = jnp.maximum(top, jnp.max(scores, axis=0, keepdims=True))
            fade = jnp.exp(top - new_top)
            probs = jnp.exp(scores - new_top)
            total = total * fade + jnp.sum(probs, axis=0, keepdims=True)
            part = slice(h * HEAD_DIM, (h + 1) * HEAD_DIM)
            acc_ref[part] = acc_ref[part] * fade + dot(value_t[part], probs.astype(BF))
            fresh.append((new_top, total))
        return tuple(fresh)

    begin = tuple(
        (jnp.full((1, QB), MASKED, F32), jnp.zeros((1, QB), F32)) for _ in range(heads)
    )
    state = lax.fori_loop(low_first // QB, start // QB + 1, body, begin)
    lse_ref[...] = jnp.zeros_like(lse_ref)
    for h in range(heads):
        top, total = state[h]
        part = slice(h * HEAD_DIM, (h + 1) * HEAD_DIM)
        acc_ref[part] = acc_ref[part] * (1.0 / total)
        lse_ref[h : h + 1] = top + jnp.log(total)
    heads_ref[...] = acc_ref[...].T.astype(BF)


def attend_call(sc, qkv):
    rows, width = qkv.shape[0], qkv.shape[1] // 3
    heads = width // HEAD_DIM
    return pl.pallas_call(
        functools.partial(attend_kernel, heads),
        grid_spec=pltpu.PrefetchScalarGridSpec(
            num_scalar_prefetch=3,
            grid=(rows // QB,),
            in_specs=[whole(qkv.shape)],
            out_specs=[
                pl.BlockSpec((QB, width), lambda i, *sc: (i, 0)),
                pl.BlockSpec((8, QB), lambda i, *sc: (0, i)),
            ],
            scratch_shapes=[
                pltpu.VMEM((width, rows), BF),
                pltpu.VMEM((width, heads * QB), BF),
                pltpu.VMEM((width, QB), F32),
                pltpu.VMEM((QB, heads * QB), F32),
            ],
        ),
        out_shape=[
            jax.ShapeDtypeStruct((rows, width), BF),
            jax.ShapeDtypeStruct((8, rows), F32),
        ],
        compiler_params=params(),
        cost_estimate=cost(60_000_000_000, 8_000_000),
        name="attend",
    )(*sc, qkv)


def spread(table_ref, out_ref, flat_ref):
    parities, levels, tables, high_rows, _ = table_ref.shape
    for piece in range(parities * levels):
        p, q = piece % parities, piece // parities
        for n in range(tables):
            for side in range(2):
                flat_ref[side, n * high_rows : (n + 1) * high_rows] = table_ref[
                    p, q, n, :, side * 128 : (side + 1) * 128
                ].astype(F32)

        def body(n, carry):
            for u in range(8):
                row = n * 8 + u
                for side in range(2):
                    at = pl.multiple_of((piece * high_rows + row) * LANES + side * 128, 128)
                    out_ref[:, pl.ds(at, 128)] = flat_ref[side, pl.ds(row, tables, stride=high_rows)]
            return carry

        lax.fori_loop(0, high_rows // 8, body, 0)


def attend_back_kernel(
    heads, rank, lengths, valid, grad_ref, qkv_ref, heads_ref, lse_ref, table_ref, mixed_ref, spread_ref,
    kt_ref, qt_ref, gt_ref, qs_ref, gs_ref, dqt_ref, dk_ref, dv_ref, score_ref, prob_ref, flat_ref,
):
    sc = (rank, lengths, valid)
    width = heads * HEAD_DIM
    step = pl.program_id(0)
    rows = qkv_ref.shape[0]

    @pl.when(step == 0)
    def _():
        for n in range(rows // QB):
            kt_ref[:, n * QB : (n + 1) * QB] = qkv_ref[n * QB : (n + 1) * QB, width : 2 * width].T
        dk_ref[...] = jnp.zeros_like(dk_ref)
        dv_ref[...] = jnp.zeros_like(dv_ref)

    start = pl.multiple_of(step * QB, QB)
    grad = grad_ref[...]
    grad_t = grad.T
    out_t = heads_ref[...].T
    product = grad_t.astype(F32) * out_t.astype(F32)
    query = qkv_ref[pl.ds(start, QB), :width] * jnp.asarray(HEAD_DIM**-0.5, BF)
    q_t = query.T
    inner = []
    for h in range(heads):
        part = slice(h * HEAD_DIM, (h + 1) * HEAD_DIM)
        inner.append(jnp.sum(product[part], axis=0, keepdims=True))
        qt_ref[:, h * QB : (h + 1) * QB] = head_rows(q_t, h)
        gt_ref[:, h * QB : (h + 1) * QB] = head_rows(grad_t, h)
    qs_ref[...] = q_t
    gs_ref[...] = grad_t
    dqt_ref[...] = jnp.zeros_like(dqt_ref)
    places = start + lax.broadcasted_iota(jnp.int32, (1, QB), 1)
    low, high = doc_bounds(sc, places)
    low_first, _ = doc_bounds(sc, start)

    def body(kb, carry):
        at = pl.multiple_of(kb * QB, QB)
        keys = qkv_ref[pl.ds(at, QB), width : 2 * width]
        values = qkv_ref[pl.ds(at, QB), 2 * width :]
        spot = at + lax.broadcasted_iota(jnp.int32, (QB, QB), 0)
        allowed = (spot >= low) & (spot <= high)
        score_ref[...] = dot(keys, qt_ref[...])
        prob_ref[...] = dot(values, gt_ref[...])
        for h in range(heads):
            part = slice(h * HEAD_DIM, (h + 1) * HEAD_DIM)
            lanes = slice(h * QB, (h + 1) * QB)
            scores = jnp.where(allowed, score_ref[:, lanes], MASKED)
            probs = jnp.exp(scores - lse_ref[h : h + 1])
            grad_scores = (probs * (prob_ref[:, lanes] - inner[h])).astype(BF)
            dqt_ref[part] += dot(kt_ref[part, pl.ds(at, QB)], grad_scores)
            dv_ref[part, pl.ds(at, QB)] += dot_nt(gs_ref[part], probs.astype(BF))
            dk_ref[part, pl.ds(at, QB)] += dot_nt(qs_ref[part], grad_scores)
        return carry

    lax.fori_loop(low_first // QB, start // QB + 1, body, 0)
    spread(table_ref, spread_ref, flat_ref)
    dq = (dqt_ref[...] * HEAD_DIM**-0.5).T.astype(BF)
    mixed_ref[pl.ds(start, QB), :width] = dq

    @pl.when(step == pl.num_programs(0) - 1)
    def _():
        for n in range(rows // QB):
            part = slice(n * QB, (n + 1) * QB)
            mixed_ref[part, width : 2 * width] = dk_ref[:, part].T.astype(BF)
            mixed_ref[part, 2 * width :] = dv_ref[:, part].T.astype(BF)


def attend_back_call(sc, grad, qkv, heads_out, lse, tables, hash_rows):
    rows, width = qkv.shape[0], qkv.shape[1] // 3
    heads = width // HEAD_DIM
    parities, levels, count, high_rows, lanes = tables.shape
    per = parities * levels // (rows // QB)
    if per == 1:
        table_spec = pl.BlockSpec(
            (1, 1, count, high_rows, lanes), lambda i, *sc: (i % 2, i // 2, 0, 0, 0)
        )
    else:
        table_spec = pl.BlockSpec(
            (2, per // 2, count, high_rows, lanes), lambda i, *sc: (0, i, 0, 0, 0)
        )
    return pl.pallas_call(
        functools.partial(attend_back_kernel, heads),
        grid_spec=pltpu.PrefetchScalarGridSpec(
            num_scalar_prefetch=3,
            grid=(rows // QB,),
            in_specs=[
                pl.BlockSpec((QB, width), lambda i, *sc: (i, 0)),
                whole(qkv.shape),
                pl.BlockSpec((QB, width), lambda i, *sc: (i, 0)),
                pl.BlockSpec((8, QB), lambda i, *sc: (0, i)),
                table_spec,
            ],
            out_specs=[
                whole((rows, 3 * width)),
                pl.BlockSpec((count, per * high_rows * lanes), lambda i, *sc: (0, i)),
            ],
            scratch_shapes=[
                pltpu.VMEM((width, rows), BF),
                pltpu.VMEM((width, heads * QB), BF),
                pltpu.VMEM((width, heads * QB), BF),
                pltpu.VMEM((width, QB), BF),
                pltpu.VMEM((width, QB), BF),
                pltpu.VMEM((width, QB), F32),
                pltpu.VMEM((width, rows), F32),
                pltpu.VMEM((width, rows), F32),
                pltpu.VMEM((QB, heads * QB), F32),
                pltpu.VMEM((QB, heads * QB), F32),
                pltpu.VMEM((2, count * high_rows, 128), F32),
            ],
        ),
        out_shape=[
            jax.ShapeDtypeStruct((rows, 3 * width), BF),
            jax.ShapeDtypeStruct((count, hash_rows), F32),
        ],
        compiler_params=params(),
        cost_estimate=cost(90_000_000_000, 12_000_000),
        name="attend_back",
    )(*sc, grad, qkv, heads_out, lse, tables)


def middle_kernel(
    seq_count, heads_ref, wo_in, x_in, gain_ref, c0_in, c2_in, wg_in, wu_in, wd_in, *refs
):
    half = seq_count // 2
    early = half // 2 + 1
    table_ins, refs = refs[:early], refs[early:]
    rest_out, fardown_out, grad_out, gain_out, keep_out, send_out = refs[:6]
    osums, gh_out, table_ref = refs[6:10], refs[10], refs[11]
    piece_refs, refs = refs[12 : 12 + half], refs[12 + half :]
    (
        rest_ref, grad_ref, wo_ref, c0, c1, c2, c3, x_ref,
        ps_ref, pr_ref, ofar_ref, n_ref, wg_ref, wu_ref, wd_ref, act_ref, gg_ref, gu_ref,
        g0_ref, g1s_ref, g1r_ref, d0_ref, d1s_ref, d1r_ref,
        ys_ref, yr_ref, all_ref, gh_ref,
        stay_ref, away_ref, got_ref, up_ref, upgot_ref,
        snd, rcv, xsnd, xrcv, zsnd, zrcv, tsnd, trcv, psnd, prcv, loc, wloc, hloc,
    ) = refs
    fardown_ref, gb_ref, ar_ref, br_ref = x_ref, d0_ref, g1r_ref, d1r_ref
    me, sib, far, farsib, core = places()
    seq = lax.axis_index("seq")
    parity, place = lax.rem(seq, 2), seq // 2
    near = seq + 1 - 2 * parity
    level = [lax.rem(seq + 2 * j, seq_count) for j in range(1, half)]

    loads = [
        pltpu.make_async_copy(w_in, w_ref.at[: w_in.shape[0]], wloc.at[n])
        for n, (w_in, w_ref) in enumerate(((wg_in, wg_ref), (wu_in, wu_ref), (wd_in, wd_ref)))
    ]
    pairs = ((wo_in, wo_ref), (x_in, x_ref), (c0_in, c0), (c2_in, c2), (heads_ref.at[me], all_ref.at[me]))
    first = [
        pltpu.make_async_copy(src, dst, wloc.at[4 + n]) for n, (src, dst) in enumerate(pairs)
    ]
    for load in first + loads:
        load.start()
    greet([(seq, sib), (seq, far), (seq, farsib), (near, me)] + [(s, me) for s in level])
    rows, model = x_in.shape
    size = rows // STEPS
    units = wg_in.shape[0]
    long = rows // 2
    kinds = iter(range(100))

    def maker(src, dst, to, length=size):
        kind = next(kinds)

        def made(k):
            part = chunk(k, length)
            return push(src.at[part], dst.at[part], snd.at[kind, k], rcv.at[kind, k], (seq, to))

        return made

    head_copies = [
        maker(heads_ref.at[to], all_ref.at[me], to) for to in (far, farsib, sib)
    ]
    grad_copies = [maker(gh_ref.at[to], gh_out.at[me], to) for to in (far, farsib, sib)]
    two_sib = maker(n_ref.at[me], n_ref.at[me], sib)
    two_far = maker(n_ref.at[me], n_ref.at[me], far)
    two_on = maker(n_ref.at[far], n_ref.at[far], sib)
    back_one = maker(g1s_ref, g1r_ref, sib, long)
    down_one = maker(d1s_ref, d1r_ref, sib, long)
    back_a = maker(g1s_ref, ar_ref, sib, long)
    back_y = maker(ys_ref, yr_ref, far)
    down_three = maker(d1s_ref, br_ref, sib, long)
    cot_one = maker(c0_in, c1, sib, long)
    cot_three = maker(c2_in, c3, sib, long)

    def grad_home(k):
        part = chunk(k, size)
        return pltpu.make_async_copy(gh_ref.at[me, part], gh_out.at[me, part], loc.at[0, k])

    def table_spot(which, j):
        return table_ref.at[which, lax.rem(place + half - j, half), core]

    def table_home(j):
        return pltpu.make_async_copy(table_ins[j], table_spot(parity, j), hloc.at[j])

    def table_level(j):
        return push(
            table_ins[0], table_ref.at[parity, place, core], tsnd.at[0, j], trcv.at[0, j], (level[j - 1], me)
        )

    def table_near(j):
        spot = table_spot(parity, j)
        return push(table_ins[j] if j < early else spot, spot, tsnd.at[1, j], trcv.at[1, j], (near, me))

    def table_sib(same, j):
        spot = table_spot(parity if same else 1 - parity, j)
        kind = 2 if same else 3
        src = table_ins[j] if same and j < early else spot
        return push(src, spot, tsnd.at[kind, j], trcv.at[kind, j], (seq, sib))

    for k in range(STEPS):
        for made in head_copies:
            made(k).start()
    for j in range(early, half):
        table_level(j).start()
    for j in range(early):
        table_home(j).start()
        table_near(j).start()
        table_sib(True, j).start()
    for k in range(2):
        cot_one(k).start()
        cot_three(k).start()

    wide = act_ref.shape[0]
    if wide > units:
        for ref in (act_ref, gg_ref, gu_ref, wg_ref, wu_ref, wd_ref):
            ref[units:] = jnp.zeros((wide - units, ref.shape[1]), BF)
    for load in first + loads:
        load.wait()
    for k in range(2):
        cot_one(k).wait_recv()
        cot_three(k).wait_recv()

    def feed(m, block_a, block_b, ca, cb):
        part = chunk(m, long)
        normed = jnp.concatenate([n_ref[block_a, part], n_ref[block_b, part]], axis=0)
        cot = jnp.concatenate([ca[part], cb[part]], axis=0)
        gate = dot_nt(wg_ref[:units], normed)
        up = dot_nt(wu_ref[:units], normed)
        sig = jax.nn.sigmoid(gate)
        silu = gate * sig
        act = (silu * up).astype(BF)
        grad_act = dot_nt(wd_ref[:units], cot)
        grad_gate = (grad_act * up * sig * (1.0 + gate * (1.0 - sig))).astype(BF)
        grad_up = (grad_act * silu).astype(BF)
        lanes = [
            pl.ds(pl.multiple_of(block * rows + m * long, long), long) for block in (block_a, block_b)
        ]
        for ref, value in ((act_ref, act), (gg_ref, grad_gate), (gu_ref, grad_up)):
            ref[:units, lanes[0]] = value[:, :long]
            ref[:units, lanes[1]] = value[:, long:]
        pair = lambda ref: jnp.concatenate([ref[:, lanes[0]], ref[:, lanes[1]]], axis=1)
        back = dot_tn(pair(gg_ref), wg_ref[...]) + dot_tn(pair(gu_ref), wu_ref[...])
        return back, dot_tn(pair(act_ref), wd_ref[...])

    def own_chunk(k):
        part = chunk(k, size)
        hidden = x_ref[part].astype(F32) + dot_nt(all_ref[me, part], wo_ref[me])
        for made in head_copies:
            made(k).wait_recv()
        for block in (sib, far, farsib):
            hidden = hidden + dot_nt(all_ref[block, part], wo_ref[block])
        rest_ref[part] = hidden
        normed, _ = norm_rows(hidden, gain_ref[...])
        n_ref[me, part] = normed.astype(BF)
        two_far(k).start()
        two_sib(k).start()

    def own_half(m):
        own_chunk(2 * m)
        own_chunk(2 * m + 1)
        two_sib(2 * m).wait_recv()
        two_sib(2 * m + 1).wait_recv()
        part = chunk(m, long)
        back, down = feed(m, me, sib, c0, c1)
        g0_ref[part] = back[:long].astype(BF)
        g1s_ref[part] = back[long:].astype(BF)
        back_one(m).start()
        d0_ref[part] = down[:long].astype(BF)
        d1s_ref[part] = down[long:].astype(BF)
        down_one(m).start()

    piece = model // seq_count
    span = model // STEPS
    per = half // STEPS
    upright = piece % 128 == 0

    def weight_away(w, b):
        return push(
            away_ref.at[w, b], got_ref.at[w, b], xsnd.at[w, b], xrcv.at[w, b], (near, me)
        )

    def up_away(j):
        b = lax.rem(place + j, half)
        return push(
            up_ref.at[b], upgot_ref.at[j - 1], zsnd.at[j], zrcv.at[j],
            (lax.rem(seq + 2 * j, seq_count), me),
        )

    def weight_tile(w, k, blocks):
        cots = (c0, c1, c2, c3)
        order = (me, sib, far, farsib)
        left = (act_ref, gg_ref, gu_ref)[w]
        total = None
        for r in blocks:
            cols = chunk(k, span)
            right = cots[r][:, cols] if w == 0 else n_ref[order[r], :, cols]
            lanes = pl.ds(pl.multiple_of(order[r] * rows, rows), rows)
            term = dot(left[:units, lanes], right)
            total = term if total is None else total + term
        return total

    def weights_step(kk):
        k = lax.rem(place // per + 1 + kk, STEPS)
        for w in range(3):
            tile = weight_tile(w, k, range(4))
            tile = tile if upright else tile.T

            def put(ref, value):
                ref[...] = value.astype(BF)

            for n in range(per):
                b = k * per + n
                take = lambda i: slice(i * piece, (i + 1) * piece)
                even = tile[:, take(2 * n)] if upright else tile[take(2 * n)]
                odd = tile[:, take(2 * n + 1)] if upright else tile[take(2 * n + 1)]
                if w == 2:
                    put(up_ref.at[b, 0], even)
                    put(up_ref.at[b, 1], odd)

                    @pl.when(b != place)
                    def _():
                        up_away(lax.rem(b + half - place, half)).start()

                else:

                    @pl.when(parity == 0)
                    def _():
                        put(stay_ref.at[w, b], even)
                        put(away_ref.at[w, b], odd)

                    @pl.when(parity == 1)
                    def _():
                        put(stay_ref.at[w, b], odd)
                        put(away_ref.at[w, b], even)

                    weight_away(w, b).start()

    each(own_half, 2)
    for j in range(early, half):
        table_level(j).wait_recv()
        table_near(j).start()
        table_sib(True, j).start()

    def far_sum(k):
        part = chunk(k, size)
        ys_ref[part] = (ys_ref[part].astype(F32) + ar_ref[part].astype(F32)).astype(BF)
        back_y(k).start()

    def far_half(m):
        part = chunk(m, long)
        back_one(m).wait_recv()
        g0_ref[part] = (g0_ref[part].astype(F32) + g1r_ref[part].astype(F32)).astype(BF)
        down_one(m).wait_recv()
        d0_ref[part] = (d0_ref[part].astype(F32) + d1r_ref[part].astype(F32)).astype(BF)
        for k in (2 * m, 2 * m + 1):
            two_far(k).wait_recv()
            two_on(k).start()
        for k in (2 * m, 2 * m + 1):
            two_on(k).wait_recv()
        back, down = feed(m, far, farsib, c2, c3)
        back_one(m).wait_send()
        g1s_ref[part] = back[long:].astype(BF)
        back_a(m).start()
        ys_ref[part] = back[:long].astype(BF)
        down_one(m).wait_send()
        d1s_ref[part] = down[long:].astype(BF)
        down_three(m).start()
        fardown_ref[part] = down[:long].astype(BF)
        back_a(m).wait_recv()
        far_sum(2 * m)
        far_sum(2 * m + 1)

    each(far_half, 2)

    gain_out[...] = jnp.zeros_like(gain_out)

    def leave(k, n, ref, out):
        part = chunk(k, size)
        return pltpu.make_async_copy(ref.at[part], out.at[part], loc.at[1 + n, k])

    def back_chunk(k):
        weights_step(k)
        part = chunk(k, size)
        back_y(k).wait_recv()
        grad_norm = g0_ref[part].astype(F32) + yr_ref[part].astype(F32)
        hidden = rest_ref[part]
        _, scaling = norm_rows(hidden, gain_ref[...])
        grad_rows, grad_gain = norm_back(hidden, scaling, gain_ref[...], grad_norm)
        grad = c0[part].astype(F32) + grad_rows
        grad_ref[part] = grad
        leave(k, 0, grad_ref, grad_out).start()
        rest_ref[part] = hidden + d0_ref[part].astype(F32)
        leave(k, 1, rest_ref, rest_out).start()
        fardown_ref[part] = (fardown_ref[part].astype(F32) + br_ref[part].astype(F32)).astype(BF)
        leave(k, 2, fardown_ref, fardown_out).start()
        gain_out[...] += grad_gain
        gb_ref[part] = grad.astype(BF)
        low = grad.astype(BF)
        for block in (far, farsib, sib, me):
            gh_ref[block, part] = dot(low, wo_ref[block]).astype(BF)
        for made in grad_copies:
            made(k).start()
        grad_home(k).start()

    for m in range(2):
        down_three(m).wait_recv()
    each(back_chunk, STEPS)
    for j in range(half):
        table_near(j).wait_recv()
        table_sib(False, j).start()

    def out_part(block):
        return dot_tn(all_ref[block], gb_ref[...])

    def out_sib(n):
        return push(ps_ref.at[n], pr_ref.at[n], psnd.at[n], prcv.at[n], (seq, sib))

    for n, block in enumerate((farsib, sib)):
        ps_ref[n] = out_part(block).astype(BF)
        out_sib(n).start()
    full_ref = wo_ref.at[0]
    width = full_ref.shape[1]
    ofar_home = pltpu.make_async_copy(ofar_ref, fardown_out.at[rows:], wloc.at[3])
    for n, (block, outs) in enumerate(((far, osums[2:]), (me, osums[:2]))):
        total = out_part(block)
        out_sib(n).wait_recv()
        full_ref[...] = (total + pr_ref[n].astype(F32)).astype(BF).T
        for j in range(half):
            b = lax.rem(place + j, half)
            for side, (which, out) in enumerate(zip((parity, 1 - parity), outs)):
                part = full_ref[pl.ds(pl.multiple_of((2 * b + which) * piece, piece), piece)]
                if n == 0 and side == 0:
                    beside = model // width
                    at, lane = j // beside * piece, j % beside * width
                    ofar_ref[at : at + piece, lane : lane + width] = part
                elif n == 1 and side == 1 and piece == 128:
                    for m in range(width // piece):
                        at = units + (j * (width // piece) + m) * piece
                        send_out[at : at + piece] = part[:, m * piece : (m + 1) * piece]
                else:
                    out[j] = part
        if n == 0:
            ofar_home.start()

    for j in range(half):
        b = lax.rem(place + j, half)
        for w in range(2):
            weight_away(w, b).wait_recv()
            piece_refs[j][w] = (stay_ref[w, b].astype(F32) + got_ref[w, b].astype(F32)).astype(BF)

    def up_sum(which):
        total = up_ref[place, which].astype(F32)
        for j in range(1, half):
            total = total + upgot_ref[j - 1, which].astype(F32)
        return total.astype(BF)

    for j in range(1, half):
        up_away(j).wait_recv()
    keep_out[...] = up_sum(parity)
    if piece == 128:
        send_out[:units] = up_sum(1 - parity)
    else:
        send_out[...] = up_sum(1 - parity)

    def close(k):
        grad_home(k).wait()
        leave(k, 0, grad_ref, grad_out).wait()
        leave(k, 1, rest_ref, rest_out).wait()
        leave(k, 2, fardown_ref, fardown_out).wait()
        for made in grad_copies:
            made(k).wait_recv()
        for made in [two_sib, two_far, two_on, back_y] + head_copies + grad_copies:
            made(k).wait_send()

    each(close, STEPS)
    for m in range(2):
        for made in (back_a, down_three, cot_one, cot_three):
            made(m).wait_send()
    ofar_home.wait()
    for copy in (out_sib(0), out_sib(1)):
        copy.wait_send()
    for j in range(early):
        table_home(j).wait()
    for j in range(half):
        table_sib(True, j).wait_recv()
        table_sib(False, j).wait_recv()
        table_near(j).wait_send()
        table_sib(True, j).wait_send()
        table_sib(False, j).wait_send()
        for w in range(2):
            weight_away(w, j).wait_send()
    for j in range(early, half):
        table_level(j).wait_send()
    for j in range(1, half):
        up_away(j).wait_send()


def middle_call(heads_out, wo, x, gain, cot, cot_far, weights, tables):
    seq_count = lax.axis_size("seq")
    rows, model = x.shape
    half = seq_count // 2
    piece = model // seq_count
    units = weights[0].shape[0]
    wide = units + -units % 256
    block = (units, piece) if piece % 128 == 0 else (piece, units)
    width = heads_out.shape[2]
    tall = half * piece * width // model
    joined = (units + half * width, piece) if piece == 128 else block
    dma = pltpu.SemaphoreType.DMA
    shape = jax.ShapeDtypeStruct
    vm = pltpu.VMEM
    rows_bf = vm((rows, model), BF)
    return pl.pallas_call(
        functools.partial(middle_kernel, seq_count),
        in_specs=[ANY] * 3 + [VM] + [ANY] * (5 + len(tables)),
        out_specs=[ANY] * 3 + [VM] * 7 + [ANY] * 2 + [VM] * half,
        out_shape=[
            shape((rows, model), F32),
            shape((rows + tall, model), BF),
            shape((rows, model), F32),
            shape((1, model), F32),
            shape(block, BF),
            shape(joined, BF),
        ]
        + [shape((half, piece, heads_out.shape[2]), BF)] * 4
        + [
            shape(heads_out.shape, BF),
            shape((2, half, 2) + tables[0].shape, BF),
        ]
        + [shape((2,) + block, BF)] * half,
        scratch_shapes=[vm((rows, model), F32)] * 2
        + [vm(wo.shape, BF)]
        + [rows_bf] * 5
        + [vm((2, wo.shape[2], model), BF)] * 2
        + [vm((tall, model), BF)]
        + [vm((4, rows, model), BF)]
        + [vm((wide, model), BF)] * 3
        + [vm((wide, 4 * rows), BF)] * 3
        + [rows_bf] * 8
        + [vm(heads_out.shape, BF)] * 2
        + [vm((2, half) + block, BF)] * 3
        + [vm((half, 2) + block, BF), vm((half - 1, 2) + block, BF)]
        + [dma((20, STEPS))] * 2
        + [dma((2, half))] * 2
        + [dma((half,))] * 2
        + [dma((4, half))] * 2
        + [dma((2,))] * 2
        + [dma((4, STEPS)), dma((9,)), dma((half // 2 + 1,))],
        compiler_params=params(collective_id=1, has_side_effects=True),
        cost_estimate=cost(100_000_000_000, 30_000_000),
        name="middle",
    )(heads_out, wo, x, gain, cot, cot_far, *weights, *tables)


def last_kernel(
    seq_count, mixed_in, w_in, x_in, gain_ref, grad_in, n_in, o0, o1, o2, o3, gain_in,
    out_out, wqkv_ref, wout_ref, gains_ref,
    mixed_ref, w_ref, x_ref, grad_ref, n_ref, osum_ref, oz_ref,
    as_ref, ar_ref, ys_ref, yr_ref, bs_ref, br_ref, dw_ref, got_ref, sum_ref, zr_ref, gs_ref, gr_ref,
    snd, rcv, xsnd, xrcv, zsnd, zrcv, gsnd, grcv, osnd, orcv, loc,
):
    me, sib, far, farsib, core = places()
    seq = lax.axis_index("seq")
    parity, place, half = lax.rem(seq, 2), seq // 2, seq_count // 2
    near = seq + 1 - 2 * parity
    loads = [
        pltpu.make_async_copy(src, dst, loc.at[n])
        for n, (src, dst) in enumerate(
            (
                (mixed_in, mixed_ref), (n_in, n_ref), (w_in, w_ref), (x_in, x_ref), (grad_in, grad_ref),
            )
        )
    ]
    for load in loads:
        load.start()
    greet(
        [(seq, sib), (seq, far), (seq, farsib)]
        + [(lax.rem(seq + j, seq_count), me) for j in range(1, seq_count)]
    )
    rows, model = x_ref.shape
    size = rows // STEPS
    piece = model // seq_count
    wide = mixed_ref.shape[-1]

    def copy(kind, k, src, dst, to):
        return push(
            src.at[chunk(k, size)], dst.at[chunk(k, size)], snd.at[kind, k], rcv.at[kind, k], (seq, to)
        )

    back_a = lambda k: copy(0, k, as_ref, ar_ref, sib)
    back_y = lambda k: copy(1, k, ys_ref, yr_ref, far)
    back_b = lambda k: copy(2, k, bs_ref, br_ref, sib)

    def near_copy(b):
        return push(dw_ref.at[1, b], got_ref.at[b], xsnd.at[b], xrcv.at[b], (near, me))

    def level_copy(j):
        b = lax.rem(place + j, half)
        return push(
            sum_ref.at[b], zr_ref.at[j], zsnd.at[j], zrcv.at[j], (lax.rem(seq + 2 * j, seq_count), me)
        )

    width = w_ref.shape[2]

    def project(block, k):
        part = chunk(k, size)
        terms = [
            dot_nt(mixed_ref[block, part, c * width : (c + 1) * width], w_ref[c]) for c in range(3)
        ]
        return terms[0] + terms[1] + terms[2]

    def send_three(k):
        as_ref[chunk(k, size)] = project(farsib, k).astype(BF)
        back_a(k).start()

    def send_two(k):
        part = project(far, k)
        back_a(k).wait_recv()
        ys_ref[chunk(k, size)] = (part + ar_ref[chunk(k, size)].astype(F32)).astype(BF)
        back_y(k).start()

    def send_one(k):
        bs_ref[chunk(k, size)] = project(sib, k).astype(BF)
        back_b(k).start()

    span = model // STEPS
    per = half // STEPS

    def weights_step(kk):
        k = lax.rem(place // per + 1 + kk, STEPS)
        cols = chunk(k, span)
        total = None
        for r in range(4):
            term = dot_tn(n_ref[r, :, cols], mixed_ref[r])
            total = term if total is None else total + term
        tile = total.astype(BF).reshape(per, 2, piece, wide)
        for j in range(per):
            b = k * per + j

            @pl.when(parity == 0)
            def _():
                dw_ref[0, b] = tile[j, 0]
                dw_ref[1, b] = tile[j, 1]

            @pl.when(parity == 1)
            def _():
                dw_ref[0, b] = tile[j, 1]
                dw_ref[1, b] = tile[j, 0]

        for j in range(per):
            near_copy(k * per + j).start()

    def out_copy(j):
        return push(
            osum_ref.at[j], oz_ref.at[j], osnd.at[j], orcv.at[j], (lax.rem(seq + 2 * j, seq_count), me)
        )

    def add(j):
        beside = model // width
        at, lane = j // beside * piece, j % beside * width
        parts = [o0[j], o2[at : at + piece, lane : lane + width], o3[j]]
        if piece == 128:
            count = width // piece
            rows_of = lambda m: slice((j * count + m) * piece, (j * count + m + 1) * piece)
            parts.append(jnp.concatenate([o1[rows_of(m)] for m in range(count)], axis=1))
        else:
            parts.append(o1[j])
        return sum(part.astype(F32) for part in parts)

    for j in range(1, half):
        osum_ref[j] = add(j).astype(BF)
        out_copy(j).start()
    for load in loads[:2]:
        load.wait()
    weights_step(0)
    loads[2].wait()
    each(send_three, STEPS)
    weights_step(1)
    each(send_two, STEPS)
    each(lambda k: weights_step(k + 2), STEPS - 2)
    each(send_one, STEPS)
    for load in loads[3:]:
        load.wait()

    gs_ref[...] = jnp.zeros_like(gs_ref)

    def leave(k):
        part = chunk(k, size)
        return pltpu.make_async_copy(grad_ref.at[part], out_out.at[part], loc.at[5 + k])

    def own_chunk(k):
        part = chunk(k, size)
        total = project(me, k)
        x = x_ref[part].astype(F32)
        _, scaling = norm_rows(x, gain_ref[...])
        back_b(k).wait_recv()
        back_y(k).wait_recv()
        grad_norm = total + br_ref[part].astype(F32) + yr_ref[part].astype(F32)
        grad_rows, grad_gain = norm_back(x, scaling, gain_ref[...], grad_norm)
        grad_ref[part] = grad_ref[part] + grad_rows
        leave(k).start()
        gs_ref[0, 0:1] += grad_gain

    def near_sum(b):
        near_copy(b).wait_recv()
        sum_ref[b] = (dw_ref[0, b].astype(F32) + got_ref[b].astype(F32)).astype(BF)

        @pl.when(b != place)
        def _():
            level_copy(lax.rem(b + half - place, half)).start()

    def near_sums(kk):
        k = lax.rem(place // per + 1 + kk, STEPS)
        for n in range(per):
            near_sum(k * per + n)

    near_sums(0)

    def both(kk):
        near_sums(kk + 1)
        own_chunk(kk)

    each(both, STEPS - 1)
    own_chunk(STEPS - 1)

    gs_ref[0, 1:2] = gain_in[...]
    rounds = [
        [(seq, sib), (seq, far), (seq, farsib)],
        [(lax.rem(seq + j, seq_count), me) for j in range(1, seq_count)],
    ]

    def gain_copy(stage, n):
        slot = 3 * stage + n
        return push(gs_ref.at[stage], gr_ref.at[slot], gsnd.at[slot], grcv.at[slot], rounds[stage][n])

    gains = gs_ref[0]
    for stage in range(2):
        for n in range(len(rounds[stage])):
            gain_copy(stage, n).start()
        for n in range(len(rounds[stage])):
            gain_copy(stage, n).wait_recv()
            gains = gains + gr_ref[3 * stage + n]
        if stage == 0:
            gs_ref[1] = gains
    gains_ref[...] = gains

    total = sum_ref[place].astype(F32)
    for j in range(1, half):
        level_copy(j).wait_recv()
        total = total + zr_ref[j].astype(F32)
    for c in range(3):
        wqkv_ref[c] = total[:, c * width : (c + 1) * width]
    out_total = add(0)
    for j in range(1, half):
        out_copy(j).wait_recv()
        out_total = out_total + oz_ref[j].astype(F32)
    wout_ref[...] = out_total

    def close(k):
        for made in (back_a, back_y, back_b):
            made(k).wait_send()

    each(close, STEPS)
    each(lambda k: leave(k).wait(), STEPS)
    each(lambda b: near_copy(b).wait_send(), half)
    for stage in range(2):
        for n in range(len(rounds[stage])):
            gain_copy(stage, n).wait_send()
    for j in range(1, half):
        level_copy(j).wait_send()
        out_copy(j).wait_send()


def last_call(mixed, w, x, gain, grad, normed, outs, gain_two):
    seq_count = lax.axis_size("seq")
    rows, model = x.shape
    half = seq_count // 2
    piece = model // seq_count
    wide, width = mixed.shape[-1], w.shape[-1]
    dma = pltpu.SemaphoreType.DMA
    shape = jax.ShapeDtypeStruct
    rows_bf = pltpu.VMEM((rows, model), BF)
    pieces = pltpu.VMEM((half, piece, wide), BF)
    return pl.pallas_call(
        functools.partial(last_kernel, seq_count),
        in_specs=[ANY] * 3 + [VM] + [ANY] * 2 + [VM] * 5,
        out_specs=[ANY] + [VM] * 3,
        out_shape=[
            shape((rows, model), F32),
            shape((3, piece, width), F32),
            shape((piece, width), F32),
            shape((8, model), F32),
        ],
        scratch_shapes=[
            pltpu.VMEM(a.shape, a.dtype) for a in (mixed, w, x, grad, normed, outs[0], outs[0])
        ]
        + [rows_bf] * 6
        + [pltpu.VMEM((2, half, piece, wide), BF), pieces, pieces, pieces]
        + [pltpu.VMEM((2, 8, model), F32), pltpu.VMEM((seq_count + 2, 8, model), F32)]
        + [
            dma((3, STEPS)),
            dma((3, STEPS)),
            dma((half,)),
            dma((half,)),
            dma((half,)),
            dma((half,)),
            dma((seq_count + 2,)),
            dma((seq_count + 2,)),
            dma((half,)),
            dma((half,)),
            dma((5 + STEPS,)),
        ],
        compiler_params=params(collective_id=2, has_side_effects=True),
        cost_estimate=cost(90_000_000_000, 30_000_000),
        name="last",
    )(mixed, w, x, gain, grad, normed, *outs, gain_two)


def shards(
    latents_in,
    gain_one,
    w_qkv,
    w_out,
    gain_two,
    w_gate,
    w_up,
    w_down,
    cotangent,
    doc_lengths,
    valid_lengths,
    hash_ids,
    hash_weights,
):
    local_rows, model_width = latents_in.shape
    local_width = w_qkv.shape[2]
    group_rows = 4 * local_rows
    units = w_gate.shape[1]
    rank = lax.axis_index("tp")
    seq_count = lax.axis_size("seq")
    sc = (jnp.full((1,), rank, jnp.int32), doc_lengths.reshape(-1), valid_lengths.reshape(-1))
    gain_one, gain_two = gain_one[None], gain_two[None]

    per_seq = -(-HASH_ROWS // seq_count)
    high_rows = -(-per_seq // (LANES * 8)) * 8

    qkv_weight = w_qkv.transpose(1, 0, 2)
    piece = model_width // seq_count
    wo_four = w_out.reshape(seq_count // 2, 2, piece, local_width)
    normed, qkv, sums, wo_all = front_call(
        latents_in, gain_one, qkv_weight, hash_ids, hash_weights, wo_four, high_rows
    )
    wo_all = wo_all.reshape(4, model_width, local_width)
    qkv, cotangent_late = lax.optimization_barrier((qkv, cotangent))

    def level_flip(x, j):
        return lax.ppermute(x, "seq", [(s, (s + 2 * j) % seq_count) for s in range(seq_count)])

    table_parts = [sums] + [level_flip(sums, j) for j in range(1, seq_count // 4 + 1)]
    qkv = qkv.reshape(group_rows, 3 * local_width)
    cot_far = flip(cotangent_late, "tp", 2)
    heads_out, lse = attend_call(sc, qkv)
    heads_four = heads_out.reshape(4, local_rows, local_width)
    (
        rest, far_down, grad_hidden, gain_two_part, up_keep, up_send, out_own, out_near,
        out_far, out_cross, grad_heads, hash_parts, *pieces,
    ) = middle_call(
        heads_four, wo_all, latents_in, gain_two, cotangent, cot_far,
        (w_gate.T, w_up.T, w_down.T), table_parts,
    )
    down_far = flip(far_down, "tp", 2)
    up_got = flip(up_send, "seq", 1)
    cross = [(4 * s + t, 4 * (s ^ 1) + (t ^ 2)) for s in range(seq_count) for t in range(4)]
    out_parts = [
        out_own,
        up_got[units:] if piece == 128 else flip(out_near, "seq", 1),
        down_far[local_rows:],
        lax.ppermute(out_cross, ("seq", "tp"), cross),
    ]
    arrived = [level_flip(pieces[j], j) for j in range(1, seq_count // 2)]
    hash_parts = hash_parts.reshape(2, seq_count // 2, hash_ids.shape[0], high_rows, LANES)
    mixed, hash_counts = attend_back_call(
        sc, grad_heads.reshape(group_rows, local_width), qkv, heads_out, lse, hash_parts, HASH_ROWS
    )
    mixed, up_got, arrived, down_far, out_parts = lax.optimization_barrier(
        (mixed, up_got, arrived, down_far, out_parts)
    )
    grad_latents, qkv_total, out_total, gains = last_call(
        mixed.reshape(4, local_rows, -1), qkv_weight, latents_in, gain_one, grad_hidden,
        normed, out_parts, gain_two_part,
    )
    total = pieces[0].astype(F32)
    for part in arrived:
        total = total + part.astype(F32)
    up_total = up_keep.astype(F32) + (up_got[:units] if piece == 128 else up_got).astype(F32)
    latents_out = (rest + down_far[:local_rows].astype(F32)).astype(BF)
    upright = lambda w: w.T if w.shape[0] == units else w
    return (
        latents_out,
        grad_latents,
        gains[0],
        qkv_total.transpose(1, 0, 2),
        out_total,
        gains[1],
        upright(total[1]),
        upright(up_total),
        upright(total[0]),
        hash_counts,
    )


def solution(mesh):
    in_specs = (
        P(("seq", "tp"), None),
        P(),
        P(None, None, "tp"),
        P(None, "tp"),
        P(),
        P(None, "tp"),
        P(None, "tp"),
        P(None, "tp"),
        P(("seq", "tp"), None),
        P("seq", None),
        P("seq", None),
        P(None, ("seq", "tp")),
        P(None, ("seq", "tp")),
    )
    out_specs = (
        P(("seq", "tp"), None),
        P(("seq", "tp"), None),
        P(),
        P("seq", None, "tp"),
        P("seq", "tp"),
        P(),
        P("seq", "tp"),
        P("seq", "tp"),
        P("seq", "tp"),
        P(),
    )
    return jax.shard_map(shards, mesh=mesh, in_specs=in_specs, out_specs=out_specs, check_vma=False)
```

```python
import functools

import jax
import jax.numpy as jnp
from jax import lax
from jax.experimental import pallas as pl
from jax.experimental.pallas import tpu as pltpu
from jax.sharding import PartitionSpec as P

HEAD_DIM = 64
HASH_ROWS = 500002
EPSILON = 1e-05
MASKED = -1e30
BF = jnp.bfloat16
F32 = jnp.float32
QB = 256
LANES = 256
STEPS = 4
VMEM_BYTES = 60 * 1024 * 1024
MESH = pl.DeviceIdType.MESH


def flip(x, axis, bits):
    count = lax.axis_size(axis)
    return lax.ppermute(x, axis, [(i, i ^ bits) for i in range(count)])


def dot(a, b):
    return lax.dot_general(a, b, (((1,), (0,)), ((), ())), preferred_element_type=F32)


def dot_nt(a, b):
    return lax.dot_general(a, b, (((1,), (1,)), ((), ())), preferred_element_type=F32)


def dot_tn(a, b):
    return lax.dot_general(a, b, (((0,), (0,)), ((), ())), preferred_element_type=F32)


def cost(flops, moved):
    return pl.CostEstimate(flops=flops, bytes_accessed=moved, transcendentals=0)


def params(**more):
    return pltpu.CompilerParams(vmem_limit_bytes=VMEM_BYTES, **more)


def whole(shape):
    return pl.BlockSpec(shape, lambda i, *sc: (0,) * len(shape))


VM = pl.BlockSpec(memory_space=pltpu.VMEM)
ANY = pl.BlockSpec(memory_space=pl.ANY)


def places():
    me = lax.axis_index("tp")
    core = lax.rem(me, 2)
    sib = me + 1 - 2 * core
    far = lax.rem(me + 2, 4)
    return me, sib, far, lax.rem(sib + 2, 4), core


def push(src, dst, send, recv, where):
    return pltpu.make_async_remote_copy(
        src_ref=src,
        dst_ref=dst,
        send_sem=send,
        recv_sem=recv,
        device_id={"seq": where[0], "tp": where[1]},
        device_id_type=MESH,
    )


def greet(others):
    barrier = pltpu.get_barrier_semaphore()
    for seq, tp in others:
        pl.semaphore_signal(
            barrier, inc=1, device_id={"seq": seq, "tp": tp}, device_id_type=MESH
        )
    pl.semaphore_wait(barrier, len(others))


def each(body, count):
    lax.fori_loop(0, count, lambda k, c: (body(k), c)[1], 0)


def chunk(k, size):
    return pl.ds(pl.multiple_of(k * size, size), size)


def norm_rows(row_data, gain):
    scaling = lax.rsqrt(jnp.mean(row_data * row_data, axis=-1, keepdims=True) + EPSILON)
    return (row_data * scaling * gain, scaling)


def norm_back(row_data, scaling, gain, grad_norm):
    weighted = grad_norm * gain
    inner_mean = jnp.mean(weighted * row_data, axis=-1, keepdims=True)
    grad_rows = scaling * weighted - row_data * scaling * scaling * scaling * inner_mean
    grad_gain = jnp.sum(grad_norm * row_data * scaling, axis=0, keepdims=True)
    return (grad_rows, grad_gain)


def front_kernel(
    seq_count, x_ref, gain_ref, w_ref, ids_ref, weights_ref, wo_ref, n_out, qkv_out, hash_ref, out_out,
    out_ref, n_ref, qkv_ref, pair_ref, pack_ref, sum_ref, snd, rcv, psnd, prcv, osnd, orcv, loc,
):
    me, sib, far, farsib, core = places()
    seq = lax.axis_index("seq")
    near = seq + 1 - 2 * lax.rem(seq, 2)
    parity, place, half = lax.rem(seq, 2), seq // 2, seq_count // 2
    level = [lax.rem(seq + 2 * j, seq_count) for j in range(1, half)]
    greet([(seq, sib), (seq, far), (near, me)] + [(s, me) for s in level])
    rows = x_ref.shape[0]
    size = rows // STEPS
    tables = ids_ref.shape[0] // 2

    def pairs(low):
        ids = jnp.where(core == low, ids_ref[:tables], ids_ref[tables:]).astype(F32)
        weights = jnp.where(core == low, weights_ref[:tables], weights_ref[tables:])
        return jnp.concatenate([ids, weights, jnp.zeros((8 - 2 * tables, rows), F32)], axis=0)

    pack_ref[parity, place, me] = pairs(0)
    pair_ref[...] = pairs(1)
    mine = pack_ref.at[parity, place, me]
    stage_sib = push(pair_ref, mine, psnd.at[0], prcv.at[0], (seq, sib))
    stage_sib.start()
    both = pack_ref.at[parity, place, pl.ds(me - core, 2)]
    stage_far = push(both, both, psnd.at[1], prcv.at[1], (seq, far))
    four = pack_ref.at[parity, place]
    stage_level = [
        push(four, four, psnd.at[2 + j], prcv.at[2 + j], (s, me)) for j, s in enumerate(level)
    ]
    plane = pack_ref.at[parity]
    stage_near = push(plane, plane, psnd.at[half + 1], prcv.at[half + 1], (near, me))

    out_ref[me] = wo_ref[...]
    eighth = out_ref.at[me, place, parity]
    out_far = push(eighth, eighth, osnd.at[0], orcv.at[0], (seq, far))
    got_eighth = out_ref.at[far, place, parity]
    out_level = [
        push(got_eighth, got_eighth, osnd.at[2 + j], orcv.at[2 + j], (s, me))
        for j, s in enumerate(level)
    ]
    got_plane = out_ref.at[far, :, parity]
    out_near = push(got_plane, got_plane, osnd.at[half + 1], orcv.at[half + 1], (near, me))
    out_sib = push(out_ref.at[me], out_ref.at[me], osnd.at[1], orcv.at[1], (seq, sib))
    out_on = push(out_ref.at[far], out_ref.at[far], osnd.at[half + 2], orcv.at[half + 2], (seq, sib))

    def own(kind, k, to, block):
        part = n_ref.at[block, chunk(k, size)]
        return push(part, part, snd.at[kind, k], rcv.at[kind, k], (seq, to))

    for k in range(STEPS):
        part = slice(k * size, (k + 1) * size)
        normed, _ = norm_rows(x_ref[part].astype(F32), gain_ref[...])
        n_ref[me, part] = normed.astype(BF)
        if k == 0:
            stage_sib.wait_recv()
            stage_far.start()
            out_far.start()
            out_sib.start()
        own(1, k, far, me).start()
        own(0, k, sib, me).start()

    width = w_ref.shape[2]

    def project(block, k, length):
        part = chunk(k, length)
        for c in range(3):
            qkv_ref[block, part, c * width : (c + 1) * width] = dot(
                n_ref[block, part], w_ref[c]
            ).astype(BF)

    def out_home(block):
        return pltpu.make_async_copy(out_ref.at[block], out_out.at[block], loc.at[2, block])

    out_home(me).start()

    def homes(block):
        return [
            pltpu.make_async_copy(n_ref.at[block], n_out.at[block], loc.at[0, block]),
            pltpu.make_async_copy(qkv_ref.at[block], qkv_out.at[block], loc.at[1, block]),
        ]

    each(lambda k: project(me, k, rows // 2), 2)
    for copy in homes(me):
        copy.start()
    stage_far.wait_recv()
    for copy in stage_level:
        copy.start()
    out_far.wait_recv()
    for copy in out_level:
        copy.start()
    for k in range(STEPS):
        own(0, k, sib, me).wait_recv()
    each(lambda k: project(sib, k, rows // 2), 2)
    for copy in homes(sib):
        copy.start()

    def far_chunk(k):
        own(1, k, far, me).wait_recv()
        own(2, k, sib, far).start()
        project(far, k, size)

    def farsib_chunk(k):
        own(2, k, sib, far).wait_recv()
        project(farsib, k, size)

    far_chunk(0)
    for copy in stage_level:
        copy.wait_recv()
    stage_near.start()

    sum_ref[...] = jnp.zeros_like(sum_ref)
    high_rows = sum_ref.shape[1]
    first = seq * (high_rows * LANES)

    def sums(which):
        def body(b):
            for table in range(tables):
                line = lambda row: jnp.concatenate(
                    [pack_ref[which, b, t, row : row + 1] for t in range(4)], axis=1
                )
                ids = line(table).astype(jnp.int32) - first
                weights = line(table + tables)
                high = lax.broadcasted_iota(jnp.int32, (high_rows, 4 * rows), 0) == (ids >> 8)
                low = lax.broadcasted_iota(jnp.int32, (LANES, 4 * rows), 0) == (ids & (LANES - 1))
                high = jnp.where(high, 1.0, 0.0).astype(BF)
                low = jnp.where(low, weights, 0.0).astype(BF)
                sum_ref[table] += dot_nt(high, low)

        each(body, half)

    sums(parity)
    for copy in out_level:
        copy.wait_recv()
    out_near.start()
    each(lambda k: far_chunk(k + 1), STEPS - 2)
    each(farsib_chunk, STEPS - 1)
    stage_near.wait_recv()
    sums(1 - parity)
    out_near.wait_recv()
    out_on.start()
    out_home(far).start()
    out_sib.wait_recv()
    out_home(sib).start()
    far_chunk(STEPS - 1)
    for copy in homes(far):
        copy.start()
    hash_ref[...] = sum_ref[...].astype(BF)
    out_on.wait_recv()
    out_home(farsib).start()
    farsib_chunk(STEPS - 1)
    for copy in homes(farsib):
        copy.start()
    for k in range(STEPS):
        for kind in range(3):
            own(kind, k, sib, me).wait_send()
    stage_sib.wait_send()
    stage_far.wait_send()
    for copy in stage_level:
        copy.wait_send()
    stage_near.wait_send()
    for copy in [out_far, out_near, out_sib, out_on] + out_level:
        copy.wait_send()
    for block in (me, sib, far, farsib):
        out_home(block).wait()
    for block in (me, sib, far, farsib):
        for copy in homes(block):
            copy.wait()


def front_call(x, gain, w, ids, weights, wo, high_rows):
    seq_count = lax.axis_size("seq")
    rows, model = x.shape
    width = w.shape[0] * w.shape[2]
    tables = ids.shape[0] // 2
    half = seq_count // 2
    dma = pltpu.SemaphoreType.DMA
    return pl.pallas_call(
        functools.partial(front_kernel, seq_count),
        in_specs=[VM] * 6,
        out_specs=[ANY] * 2 + [VM, ANY],
        out_shape=[
            jax.ShapeDtypeStruct((4, rows, model), BF),
            jax.ShapeDtypeStruct((4, rows, width), BF),
            jax.ShapeDtypeStruct((tables, high_rows, LANES), BF),
            jax.ShapeDtypeStruct((4,) + wo.shape, BF),
        ],
        scratch_shapes=[
            pltpu.VMEM((4,) + wo.shape, BF),
            pltpu.VMEM((4, rows, model), BF),
            pltpu.VMEM((4, rows, width), BF),
            pltpu.VMEM((8, rows), F32),
            pltpu.VMEM((2, half, 4, 8, rows), F32),
            pltpu.VMEM((tables, high_rows, LANES), F32),
            dma((3, STEPS)),
            dma((3, STEPS)),
            dma((half + 2,)),
            dma((half + 2,)),
            dma((half + 3,)),
            dma((half + 3,)),
            dma((3, 4)),
        ],
        compiler_params=params(collective_id=0, has_side_effects=True),
        cost_estimate=cost(1_000_000, 1_000_000),
        name="front",
    )(x, gain, w, ids, weights, wo)


def doc_bounds(sc, places):
    _, lengths, valid = sc
    one = lengths[0]
    two = one + lengths[1]
    low = jnp.where(places >= two, two, jnp.where(places >= one, one, 0))
    end = jnp.where(
        places >= two, two + valid[2], jnp.where(places >= one, one + valid[1], valid[0])
    )
    return low, jnp.minimum(places, end - 1)


def head_rows(x, h):
    where = lax.broadcasted_iota(jnp.int32, x.shape, 0) // HEAD_DIM
    return jnp.where(where == h, x, jnp.zeros_like(x))


def attend_kernel(heads, rank, lengths, valid, qkv_ref, heads_ref, lse_ref, vt_ref, qt_ref, acc_ref, score_ref):
    sc = (rank, lengths, valid)
    width = heads * HEAD_DIM
    step = pl.program_id(0)

    @pl.when(step == 0)
    def _():
        for n in range(qkv_ref.shape[0] // QB):
            vt_ref[:, n * QB : (n + 1) * QB] = qkv_ref[n * QB : (n + 1) * QB, 2 * width :].T

    start = pl.multiple_of(step * QB, QB)
    q_t = qkv_ref[pl.ds(start, QB), :width].T * jnp.asarray(HEAD_DIM**-0.5, BF)
    for h in range(heads):
        qt_ref[:, h * QB : (h + 1) * QB] = head_rows(q_t, h)
    acc_ref[...] = jnp.zeros_like(acc_ref)
    places = start + lax.broadcasted_iota(jnp.int32, (1, QB), 1)
    low, high = doc_bounds(sc, places)
    low_first, _ = doc_bounds(sc, start)

    def body(kb, state):
        at = pl.multiple_of(kb * QB, QB)
        keys = qkv_ref[pl.ds(at, QB), width : 2 * width]
        value_t = vt_ref[:, pl.ds(at, QB)]
        spot = at + lax.broadcasted_iota(jnp.int32, (QB, QB), 0)
        allowed = (spot >= low) & (spot <= high)
        score_ref[...] = dot(keys, qt_ref[...])
        fresh = []
        for h in range(heads):
            top, total = state[h]
            scores = jnp.where(allowed, score_ref[:, h * QB : (h + 1) * QB], MASKED)
            new_top = jnp.maximum(top, jnp.max(scores, axis=0, keepdims=True))
            fade = jnp.exp(top - new_top)
            probs = jnp.exp(scores - new_top)
            total = total * fade + jnp.sum(probs, axis=0, keepdims=True)
            part = slice(h * HEAD_DIM, (h + 1) * HEAD_DIM)
            acc_ref[part] = acc_ref[part] * fade + dot(value_t[part], probs.astype(BF))
            fresh.append((new_top, total))
        return tuple(fresh)

    begin = tuple(
        (jnp.full((1, QB), MASKED, F32), jnp.zeros((1, QB), F32)) for _ in range(heads)
    )
    state = lax.fori_loop(low_first // QB, start // QB + 1, body, begin)
    lse_ref[...] = jnp.zeros_like(lse_ref)
    for h in range(heads):
        top, total = state[h]
        part = slice(h * HEAD_DIM, (h + 1) * HEAD_DIM)
        acc_ref[part] = acc_ref[part] * (1.0 / total)
        lse_ref[h : h + 1] = top + jnp.log(total)
    heads_ref[...] = acc_ref[...].T.astype(BF)


def attend_call(sc, qkv):
    rows, width = qkv.shape[0], qkv.shape[1] // 3
    heads = width // HEAD_DIM
    return pl.pallas_call(
        functools.partial(attend_kernel, heads),
        grid_spec=pltpu.PrefetchScalarGridSpec(
            num_scalar_prefetch=3,
            grid=(rows // QB,),
            in_specs=[whole(qkv.shape)],
            out_specs=[
                pl.BlockSpec((QB, width), lambda i, *sc: (i, 0)),
                pl.BlockSpec((8, QB), lambda i, *sc: (0, i)),
            ],
            scratch_shapes=[
                pltpu.VMEM((width, rows), BF),
                pltpu.VMEM((width, heads * QB), BF),
                pltpu.VMEM((width, QB), F32),
                pltpu.VMEM((QB, heads * QB), F32),
            ],
        ),
        out_shape=[
            jax.ShapeDtypeStruct((rows, width), BF),
            jax.ShapeDtypeStruct((8, rows), F32),
        ],
        compiler_params=params(),
        cost_estimate=cost(60_000_000_000, 8_000_000),
        name="attend",
    )(*sc, qkv)


def spread(table_ref, out_ref, flat_ref):
    parities, levels, tables, high_rows, _ = table_ref.shape
    for piece in range(parities * levels):
        p, q = piece % parities, piece // parities
        for n in range(tables):
            for side in range(2):
                flat_ref[side, n * high_rows : (n + 1) * high_rows] = table_ref[
                    p, q, n, :, side * 128 : (side + 1) * 128
                ].astype(F32)

        def body(n, carry):
            for u in range(8):
                row = n * 8 + u
                for side in range(2):
                    at = pl.multiple_of((piece * high_rows + row) * LANES + side * 128, 128)
                    out_ref[:, pl.ds(at, 128)] = flat_ref[side, pl.ds(row, tables, stride=high_rows)]
            return carry

        lax.fori_loop(0, high_rows // 8, body, 0)


def attend_back_kernel(
    heads, rank, lengths, valid, grad_ref, qkv_ref, heads_ref, lse_ref, table_ref, mixed_ref, spread_ref,
    kt_ref, qt_ref, gt_ref, qs_ref, gs_ref, dqt_ref, dk_ref, dv_ref, score_ref, prob_ref, flat_ref,
):
    sc = (rank, lengths, valid)
    width = heads * HEAD_DIM
    step = pl.program_id(0)
    rows = qkv_ref.shape[0]

    @pl.when(step == 0)
    def _():
        for n in range(rows // QB):
            kt_ref[:, n * QB : (n + 1) * QB] = qkv_ref[n * QB : (n + 1) * QB, width : 2 * width].T
        dk_ref[...] = jnp.zeros_like(dk_ref)
        dv_ref[...] = jnp.zeros_like(dv_ref)

    start = pl.multiple_of(step * QB, QB)
    grad = grad_ref[...]
    grad_t = grad.T
    out_t = heads_ref[...].T
    product = grad_t.astype(F32) * out_t.astype(F32)
    query = qkv_ref[pl.ds(start, QB), :width] * jnp.asarray(HEAD_DIM**-0.5, BF)
    q_t = query.T
    inner = []
    for h in range(heads):
        part = slice(h * HEAD_DIM, (h + 1) * HEAD_DIM)
        inner.append(jnp.sum(product[part], axis=0, keepdims=True))
        qt_ref[:, h * QB : (h + 1) * QB] = head_rows(q_t, h)
        gt_ref[:, h * QB : (h + 1) * QB] = head_rows(grad_t, h)
    qs_ref[...] = q_t
    gs_ref[...] = grad_t
    dqt_ref[...] = jnp.zeros_like(dqt_ref)
    places = start + lax.broadcasted_iota(jnp.int32, (1, QB), 1)
    low, high = doc_bounds(sc, places)
    low_first, _ = doc_bounds(sc, start)

    def body(kb, carry):
        at = pl.multiple_of(kb * QB, QB)
        keys = qkv_ref[pl.ds(at, QB), width : 2 * width]
        values = qkv_ref[pl.ds(at, QB), 2 * width :]
        spot = at + lax.broadcasted_iota(jnp.int32, (QB, QB), 0)
        allowed = (spot >= low) & (spot <= high)
        score_ref[...] = dot(keys, qt_ref[...])
        prob_ref[...] = dot(values, gt_ref[...])
        for h in range(heads):
            part = slice(h * HEAD_DIM, (h + 1) * HEAD_DIM)
            lanes = slice(h * QB, (h + 1) * QB)
            scores = jnp.where(allowed, score_ref[:, lanes], MASKED)
            probs = jnp.exp(scores - lse_ref[h : h + 1])
            grad_scores = (probs * (prob_ref[:, lanes] - inner[h])).astype(BF)
            dqt_ref[part] += dot(kt_ref[part, pl.ds(at, QB)], grad_scores)
            dv_ref[part, pl.ds(at, QB)] += dot_nt(gs_ref[part], probs.astype(BF))
            dk_ref[part, pl.ds(at, QB)] += dot_nt(qs_ref[part], grad_scores)
        return carry

    lax.fori_loop(low_first // QB, start // QB + 1, body, 0)
    spread(table_ref, spread_ref, flat_ref)
    dq = (dqt_ref[...] * HEAD_DIM**-0.5).T.astype(BF)
    mixed_ref[pl.ds(start, QB), :width] = dq

    @pl.when(step == pl.num_programs(0) - 1)
    def _():
        for n in range(rows // QB):
            part = slice(n * QB, (n + 1) * QB)
            mixed_ref[part, width : 2 * width] = dk_ref[:, part].T.astype(BF)
            mixed_ref[part, 2 * width :] = dv_ref[:, part].T.astype(BF)


def attend_back_call(sc, grad, qkv, heads_out, lse, tables, hash_rows):
    rows, width = qkv.shape[0], qkv.shape[1] // 3
    heads = width // HEAD_DIM
    parities, levels, count, high_rows, lanes = tables.shape
    per = parities * levels // (rows // QB)
    if per == 1:
        table_spec = pl.BlockSpec(
            (1, 1, count, high_rows, lanes), lambda i, *sc: (i % 2, i // 2, 0, 0, 0)
        )
    else:
        table_spec = pl.BlockSpec(
            (2, per // 2, count, high_rows, lanes), lambda i, *sc: (0, i, 0, 0, 0)
        )
    return pl.pallas_call(
        functools.partial(attend_back_kernel, heads),
        grid_spec=pltpu.PrefetchScalarGridSpec(
            num_scalar_prefetch=3,
            grid=(rows // QB,),
            in_specs=[
                pl.BlockSpec((QB, width), lambda i, *sc: (i, 0)),
                whole(qkv.shape),
                pl.BlockSpec((QB, width), lambda i, *sc: (i, 0)),
                pl.BlockSpec((8, QB), lambda i, *sc: (0, i)),
                table_spec,
            ],
            out_specs=[
                whole((rows, 3 * width)),
                pl.BlockSpec((count, per * high_rows * lanes), lambda i, *sc: (0, i)),
            ],
            scratch_shapes=[
                pltpu.VMEM((width, rows), BF),
                pltpu.VMEM((width, heads * QB), BF),
                pltpu.VMEM((width, heads * QB), BF),
                pltpu.VMEM((width, QB), BF),
                pltpu.VMEM((width, QB), BF),
                pltpu.VMEM((width, QB), F32),
                pltpu.VMEM((width, rows), F32),
                pltpu.VMEM((width, rows), F32),
                pltpu.VMEM((QB, heads * QB), F32),
                pltpu.VMEM((QB, heads * QB), F32),
                pltpu.VMEM((2, count * high_rows, 128), F32),
            ],
        ),
        out_shape=[
            jax.ShapeDtypeStruct((rows, 3 * width), BF),
            jax.ShapeDtypeStruct((count, hash_rows), F32),
        ],
        compiler_params=params(),
        cost_estimate=cost(90_000_000_000, 12_000_000),
        name="attend_back",
    )(*sc, grad, qkv, heads_out, lse, tables)


def middle_kernel(
    seq_count, heads_ref, wo_in, x_in, gain_ref, c0_in, c2_in, wg_in, wu_in, wd_in, *refs
):
    half = seq_count // 2
    early = half // 2 + 1
    table_ins, refs = refs[:early], refs[early:]
    rest_out, fardown_out, grad_out, gain_out, keep_out, send_out = refs[:6]
    ostay_out, oaway_out, gh_out, table_ref = refs[6:10]
    piece_refs, refs = refs[10 : 10 + half], refs[10 + half :]
    (
        rest_ref, grad_ref, wo_ref, c0, c1, c2, c3, x_ref,
        ps_ref, pr_ref, n_ref, wg_ref, wu_ref, wd_ref, act_ref, gg_ref, gu_ref,
        g0_ref, g1s_ref, g1r_ref, d0_ref, d1s_ref, d1r_ref,
        ys_ref, yr_ref, all_ref, gh_ref,
        stay_ref, away_ref, got_ref, up_ref, upgot_ref,
        snd, rcv, xsnd, xrcv, zsnd, zrcv, tsnd, trcv, psnd, prcv, loc, wloc, hloc,
    ) = refs
    fardown_ref, gb_ref, ar_ref, br_ref = x_ref, d0_ref, g1r_ref, d1r_ref
    me, sib, far, farsib, core = places()
    seq = lax.axis_index("seq")
    parity, place = lax.rem(seq, 2), seq // 2
    near = seq + 1 - 2 * parity
    level = [lax.rem(seq + 2 * j, seq_count) for j in range(1, half)]

    loads = [
        pltpu.make_async_copy(w_in, w_ref.at[: w_in.shape[0]], wloc.at[n])
        for n, (w_in, w_ref) in enumerate(((wg_in, wg_ref), (wu_in, wu_ref), (wd_in, wd_ref)))
    ]
    pairs = ((wo_in, wo_ref), (x_in, x_ref), (c0_in, c0), (c2_in, c2), (heads_ref.at[me], all_ref.at[me]))
    first = [
        pltpu.make_async_copy(src, dst, wloc.at[4 + n]) for n, (src, dst) in enumerate(pairs)
    ]
    for load in first + loads:
        load.start()
    greet([(seq, sib), (seq, far), (seq, farsib), (near, me)] + [(s, me) for s in level])
    rows, model = x_in.shape
    size = rows // STEPS
    units = wg_in.shape[0]
    long = rows // 2
    kinds = iter(range(100))

    def maker(src, dst, to, length=size):
        kind = next(kinds)

        def made(k):
            part = chunk(k, length)
            return push(src.at[part], dst.at[part], snd.at[kind, k], rcv.at[kind, k], (seq, to))

        return made

    head_copies = [
        maker(heads_ref.at[to], all_ref.at[me], to) for to in (far, farsib, sib)
    ]
    grad_copies = [maker(gh_ref.at[to], gh_out.at[me], to) for to in (far, farsib, sib)]
    two_sib = maker(n_ref.at[me], n_ref.at[me], sib)
    two_far = maker(n_ref.at[me], n_ref.at[me], far)
    two_on = maker(n_ref.at[far], n_ref.at[far], sib)
    back_one = maker(g1s_ref, g1r_ref, sib, long)
    down_one = maker(d1s_ref, d1r_ref, sib, long)
    back_a = maker(g1s_ref, ar_ref, sib, long)
    back_y = maker(ys_ref, yr_ref, far)
    down_three = maker(d1s_ref, br_ref, sib, long)
    cot_one = maker(c0_in, c1, sib, long)
    cot_three = maker(c2_in, c3, sib, long)

    def grad_home(k):
        part = chunk(k, size)
        return pltpu.make_async_copy(gh_ref.at[me, part], gh_out.at[me, part], loc.at[0, k])

    def table_spot(which, j):
        return table_ref.at[which, lax.rem(place + half - j, half), core]

    def table_home(j):
        return pltpu.make_async_copy(table_ins[j], table_spot(parity, j), hloc.at[j])

    def table_level(j):
        return push(
            table_ins[0], table_ref.at[parity, place, core], tsnd.at[0, j], trcv.at[0, j], (level[j - 1], me)
        )

    def table_near(j):
        spot = table_spot(parity, j)
        return push(table_ins[j] if j < early else spot, spot, tsnd.at[1, j], trcv.at[1, j], (near, me))

    def table_sib(same, j):
        spot = table_spot(parity if same else 1 - parity, j)
        kind = 2 if same else 3
        src = table_ins[j] if same and j < early else spot
        return push(src, spot, tsnd.at[kind, j], trcv.at[kind, j], (seq, sib))

    for k in range(STEPS):
        for made in head_copies:
            made(k).start()
    for j in range(early, half):
        table_level(j).start()
    for j in range(early):
        table_home(j).start()
        table_near(j).start()
        table_sib(True, j).start()
    for k in range(2):
        cot_one(k).start()
        cot_three(k).start()

    wide = act_ref.shape[0]
    if wide > units:
        for ref in (act_ref, gg_ref, gu_ref, wg_ref, wu_ref, wd_ref):
            ref[units:] = jnp.zeros((wide - units, ref.shape[1]), BF)
    for load in first + loads:
        load.wait()
    for k in range(2):
        cot_one(k).wait_recv()
        cot_three(k).wait_recv()

    def feed(m, block_a, block_b, ca, cb):
        part = chunk(m, long)
        normed = jnp.concatenate([n_ref[block_a, part], n_ref[block_b, part]], axis=0)
        cot = jnp.concatenate([ca[part], cb[part]], axis=0)
        gate = dot_nt(wg_ref[:units], normed)
        up = dot_nt(wu_ref[:units], normed)
        sig = jax.nn.sigmoid(gate)
        silu = gate * sig
        act = (silu * up).astype(BF)
        grad_act = dot_nt(wd_ref[:units], cot)
        grad_gate = (grad_act * up * sig * (1.0 + gate * (1.0 - sig))).astype(BF)
        grad_up = (grad_act * silu).astype(BF)
        lanes = [
            pl.ds(pl.multiple_of(block * rows + m * long, long), long) for block in (block_a, block_b)
        ]
        for ref, value in ((act_ref, act), (gg_ref, grad_gate), (gu_ref, grad_up)):
            ref[:units, lanes[0]] = value[:, :long]
            ref[:units, lanes[1]] = value[:, long:]
        pair = lambda ref: jnp.concatenate([ref[:, lanes[0]], ref[:, lanes[1]]], axis=1)
        back = dot_tn(pair(gg_ref), wg_ref[...]) + dot_tn(pair(gu_ref), wu_ref[...])
        return back, dot_tn(pair(act_ref), wd_ref[...])

    def own_chunk(k):
        part = chunk(k, size)
        hidden = x_ref[part].astype(F32) + dot_nt(all_ref[me, part], wo_ref[me])
        for made in head_copies:
            made(k).wait_recv()
        for block in (sib, far, farsib):
            hidden = hidden + dot_nt(all_ref[block, part], wo_ref[block])
        rest_ref[part] = hidden
        normed, _ = norm_rows(hidden, gain_ref[...])
        n_ref[me, part] = normed.astype(BF)
        two_far(k).start()
        two_sib(k).start()

    def own_half(m):
        own_chunk(2 * m)
        own_chunk(2 * m + 1)
        two_sib(2 * m).wait_recv()
        two_sib(2 * m + 1).wait_recv()
        part = chunk(m, long)
        back, down = feed(m, me, sib, c0, c1)
        g0_ref[part] = back[:long].astype(BF)
        g1s_ref[part] = back[long:].astype(BF)
        back_one(m).start()
        d0_ref[part] = down[:long].astype(BF)
        d1s_ref[part] = down[long:].astype(BF)
        down_one(m).start()

    piece = model // seq_count
    span = model // STEPS
    per = half // STEPS
    upright = piece % 128 == 0

    def weight_away(w, b):
        return push(
            away_ref.at[w, b], got_ref.at[w, b], xsnd.at[w, b], xrcv.at[w, b], (near, me)
        )

    def up_away(j):
        b = lax.rem(place + j, half)
        return push(
            up_ref.at[b], upgot_ref.at[j - 1], zsnd.at[j], zrcv.at[j],
            (lax.rem(seq + 2 * j, seq_count), me),
        )

    def weight_tile(w, k, blocks):
        cots = (c0, c1, c2, c3)
        order = (me, sib, far, farsib)
        left = (act_ref, gg_ref, gu_ref)[w]
        total = None
        for r in blocks:
            cols = chunk(k, span)
            right = cots[r][:, cols] if w == 0 else n_ref[order[r], :, cols]
            lanes = pl.ds(pl.multiple_of(order[r] * rows, rows), rows)
            term = dot(left[:units, lanes], right)
            total = term if total is None else total + term
        return total

    def weights_step(kk):
        k = lax.rem(place // per + 1 + kk, STEPS)
        for w in range(3):
            tile = weight_tile(w, k, range(4))
            tile = tile if upright else tile.T

            def put(ref, value):
                ref[...] = value.astype(BF)

            for n in range(per):
                b = k * per + n
                take = lambda i: slice(i * piece, (i + 1) * piece)
                even = tile[:, take(2 * n)] if upright else tile[take(2 * n)]
                odd = tile[:, take(2 * n + 1)] if upright else tile[take(2 * n + 1)]
                if w == 2:
                    put(up_ref.at[b, 0], even)
                    put(up_ref.at[b, 1], odd)

                    @pl.when(b != place)
                    def _():
                        up_away(lax.rem(b + half - place, half)).start()

                else:

                    @pl.when(parity == 0)
                    def _():
                        put(stay_ref.at[w, b], even)
                        put(away_ref.at[w, b], odd)

                    @pl.when(parity == 1)
                    def _():
                        put(stay_ref.at[w, b], odd)
                        put(away_ref.at[w, b], even)

                    weight_away(w, b).start()

    each(own_half, 2)
    for j in range(early, half):
        table_level(j).wait_recv()
        table_near(j).start()
        table_sib(True, j).start()

    def far_sum(k):
        part = chunk(k, size)
        ys_ref[part] = (ys_ref[part].astype(F32) + ar_ref[part].astype(F32)).astype(BF)
        back_y(k).start()

    def far_half(m):
        part = chunk(m, long)
        back_one(m).wait_recv()
        g0_ref[part] = (g0_ref[part].astype(F32) + g1r_ref[part].astype(F32)).astype(BF)
        down_one(m).wait_recv()
        d0_ref[part] = (d0_ref[part].astype(F32) + d1r_ref[part].astype(F32)).astype(BF)
        for k in (2 * m, 2 * m + 1):
            two_far(k).wait_recv()
            two_on(k).start()
        for k in (2 * m, 2 * m + 1):
            two_on(k).wait_recv()
        back, down = feed(m, far, farsib, c2, c3)
        back_one(m).wait_send()
        g1s_ref[part] = back[long:].astype(BF)
        back_a(m).start()
        ys_ref[part] = back[:long].astype(BF)
        down_one(m).wait_send()
        d1s_ref[part] = down[long:].astype(BF)
        down_three(m).start()
        fardown_ref[part] = down[:long].astype(BF)
        back_a(m).wait_recv()
        far_sum(2 * m)
        far_sum(2 * m + 1)

    each(far_half, 2)

    gain_out[...] = jnp.zeros_like(gain_out)

    def leave(k, n, ref, out):
        part = chunk(k, size)
        return pltpu.make_async_copy(ref.at[part], out.at[part], loc.at[1 + n, k])

    def back_chunk(k):
        weights_step(k)
        part = chunk(k, size)
        back_y(k).wait_recv()
        grad_norm = g0_ref[part].astype(F32) + yr_ref[part].astype(F32)
        hidden = rest_ref[part]
        _, scaling = norm_rows(hidden, gain_ref[...])
        grad_rows, grad_gain = norm_back(hidden, scaling, gain_ref[...], grad_norm)
        grad = c0[part].astype(F32) + grad_rows
        grad_ref[part] = grad
        leave(k, 0, grad_ref, grad_out).start()
        rest_ref[part] = hidden + d0_ref[part].astype(F32)
        leave(k, 1, rest_ref, rest_out).start()
        fardown_ref[part] = (fardown_ref[part].astype(F32) + br_ref[part].astype(F32)).astype(BF)
        leave(k, 2, fardown_ref, fardown_out).start()
        gain_out[...] += grad_gain
        gb_ref[part] = grad.astype(BF)
        low = grad.astype(BF)
        for block in (far, farsib, sib, me):
            gh_ref[block, part] = dot(low, wo_ref[block]).astype(BF)
        for made in grad_copies:
            made(k).start()
        grad_home(k).start()

    for m in range(2):
        down_three(m).wait_recv()
    each(back_chunk, STEPS)
    for j in range(half):
        table_near(j).wait_recv()
        table_sib(False, j).start()

    def out_part(block):
        return dot_tn(all_ref[block], gb_ref[...])

    def out_sib(n):
        return push(ps_ref.at[n], pr_ref.at[n], psnd.at[n], prcv.at[n], (seq, sib))

    for n, block in enumerate((farsib, sib)):
        ps_ref[n] = out_part(block).astype(BF)
        out_sib(n).start()
    for n, (block, out) in enumerate(((far, oaway_out), (me, ostay_out))):
        total = out_part(block)
        out_sib(n).wait_recv()
        out[...] = (total + pr_ref[n].astype(F32)).astype(BF).T

    for j in range(half):
        b = lax.rem(place + j, half)
        for w in range(2):
            weight_away(w, b).wait_recv()
            piece_refs[j][w] = (stay_ref[w, b].astype(F32) + got_ref[w, b].astype(F32)).astype(BF)

    def up_sum(which):
        total = up_ref[place, which].astype(F32)
        for j in range(1, half):
            total = total + upgot_ref[j - 1, which].astype(F32)
        return total.astype(BF)

    for j in range(1, half):
        up_away(j).wait_recv()
    keep_out[...] = up_sum(parity)
    send_out[...] = up_sum(1 - parity)

    def close(k):
        grad_home(k).wait()
        leave(k, 0, grad_ref, grad_out).wait()
        leave(k, 1, rest_ref, rest_out).wait()
        leave(k, 2, fardown_ref, fardown_out).wait()
        for made in grad_copies:
            made(k).wait_recv()
        for made in [two_sib, two_far, two_on, back_y] + head_copies + grad_copies:
            made(k).wait_send()

    each(close, STEPS)
    for m in range(2):
        for made in (back_a, down_three, cot_one, cot_three):
            made(m).wait_send()
    for copy in (out_sib(0), out_sib(1)):
        copy.wait_send()
    for j in range(early):
        table_home(j).wait()
    for j in range(half):
        table_sib(True, j).wait_recv()
        table_sib(False, j).wait_recv()
        table_near(j).wait_send()
        table_sib(True, j).wait_send()
        table_sib(False, j).wait_send()
        for w in range(2):
            weight_away(w, j).wait_send()
    for j in range(early, half):
        table_level(j).wait_send()
    for j in range(1, half):
        up_away(j).wait_send()


def middle_call(heads_out, wo, x, gain, cot, cot_far, weights, tables):
    seq_count = lax.axis_size("seq")
    rows, model = x.shape
    half = seq_count // 2
    piece = model // seq_count
    units = weights[0].shape[0]
    wide = units + -units % 256
    block = (units, piece) if piece % 128 == 0 else (piece, units)
    dma = pltpu.SemaphoreType.DMA
    shape = jax.ShapeDtypeStruct
    vm = pltpu.VMEM
    rows_bf = vm((rows, model), BF)
    return pl.pallas_call(
        functools.partial(middle_kernel, seq_count),
        in_specs=[ANY] * 3 + [VM] + [ANY] * (5 + len(tables)),
        out_specs=[ANY] * 3 + [VM] * 5 + [ANY] * 2 + [VM] * half,
        out_shape=[
            shape((rows, model), F32),
            shape((rows, model), BF),
            shape((rows, model), F32),
            shape((1, model), F32),
            shape(block, BF),
            shape(block, BF),
            shape((model, heads_out.shape[2]), BF),
            shape((model, heads_out.shape[2]), BF),
            shape(heads_out.shape, BF),
            shape((2, half, 2) + tables[0].shape, BF),
        ]
        + [shape((2,) + block, BF)] * half,
        scratch_shapes=[vm((rows, model), F32)] * 2
        + [vm(wo.shape, BF)]
        + [rows_bf] * 5
        + [vm((2, wo.shape[2], model), BF)] * 2
        + [vm((4, rows, model), BF)]
        + [vm((wide, model), BF)] * 3
        + [vm((wide, 4 * rows), BF)] * 3
        + [rows_bf] * 8
        + [vm(heads_out.shape, BF)] * 2
        + [vm((2, half) + block, BF)] * 3
        + [vm((half, 2) + block, BF), vm((half - 1, 2) + block, BF)]
        + [dma((20, STEPS))] * 2
        + [dma((2, half))] * 2
        + [dma((half,))] * 2
        + [dma((4, half))] * 2
        + [dma((2,))] * 2
        + [dma((4, STEPS)), dma((9,)), dma((half // 2 + 1,))],
        compiler_params=params(collective_id=1, has_side_effects=True),
        cost_estimate=cost(100_000_000_000, 30_000_000),
        name="middle",
    )(heads_out, wo, x, gain, cot, cot_far, *weights, *tables)


def last_kernel(
    seq_count, mixed_in, w_in, x_in, gain_ref, grad_in, n_in, ostay_in, ogot_in, gain_in,
    out_out, wqkv_ref, wout_ref, gains_ref,
    mixed_ref, w_ref, x_ref, grad_ref, n_ref, ostay_ref, ogot_ref,
    as_ref, ar_ref, ys_ref, yr_ref, bs_ref, br_ref, dw_ref, got_ref, sum_ref, zr_ref, gs_ref, gr_ref,
    snd, rcv, xsnd, xrcv, zsnd, zrcv, gsnd, grcv, loc,
):
    me, sib, far, farsib, core = places()
    seq = lax.axis_index("seq")
    parity, place, half = lax.rem(seq, 2), seq // 2, seq_count // 2
    near = seq + 1 - 2 * parity
    loads = [
        pltpu.make_async_copy(src, dst, loc.at[n])
        for n, (src, dst) in enumerate(
            (
                (mixed_in, mixed_ref), (n_in, n_ref), (ostay_in, ostay_ref),
                (ogot_in, ogot_ref), (w_in, w_ref), (x_in, x_ref), (grad_in, grad_ref),
            )
        )
    ]
    for load in loads:
        load.start()
    greet(
        [(seq, sib), (seq, far), (seq, farsib)]
        + [(lax.rem(seq + j, seq_count), me) for j in range(1, seq_count)]
    )
    rows, model = x_ref.shape
    size = rows // STEPS
    piece = model // seq_count
    wide = mixed_ref.shape[-1]

    def copy(kind, k, src, dst, to):
        return push(
            src.at[chunk(k, size)], dst.at[chunk(k, size)], snd.at[kind, k], rcv.at[kind, k], (seq, to)
        )

    back_a = lambda k: copy(0, k, as_ref, ar_ref, sib)
    back_y = lambda k: copy(1, k, ys_ref, yr_ref, far)
    back_b = lambda k: copy(2, k, bs_ref, br_ref, sib)

    def near_copy(b):
        return push(dw_ref.at[1, b], got_ref.at[b], xsnd.at[b], xrcv.at[b], (near, me))

    def level_copy(j):
        b = lax.rem(place + j, half)
        return push(
            sum_ref.at[b], zr_ref.at[j], zsnd.at[j], zrcv.at[j], (lax.rem(seq + 2 * j, seq_count), me)
        )

    width = w_ref.shape[2]

    def project(block, k):
        part = chunk(k, size)
        terms = [
            dot_nt(mixed_ref[block, part, c * width : (c + 1) * width], w_ref[c]) for c in range(3)
        ]
        return terms[0] + terms[1] + terms[2]

    def send_three(k):
        as_ref[chunk(k, size)] = project(farsib, k).astype(BF)
        back_a(k).start()

    def send_two(k):
        part = project(far, k)
        back_a(k).wait_recv()
        ys_ref[chunk(k, size)] = (part + ar_ref[chunk(k, size)].astype(F32)).astype(BF)
        back_y(k).start()

    def send_one(k):
        bs_ref[chunk(k, size)] = project(sib, k).astype(BF)
        back_b(k).start()

    span = model // STEPS
    per = half // STEPS

    def weights_step(kk):
        k = lax.rem(place // per + 1 + kk, STEPS)
        cols = chunk(k, span)
        total = None
        for r in range(4):
            term = dot_tn(n_ref[r, :, cols], mixed_ref[r])
            total = term if total is None else total + term
        to_out = ostay_ref[cols].astype(F32) + ogot_ref[cols].astype(F32)
        for lanes, value in ((slice(0, wide), total), (slice(wide, wide + width), to_out)):
            tile = value.astype(BF).reshape(per, 2, piece, value.shape[1])
            for j in range(per):
                b = k * per + j

                @pl.when(parity == 0)
                def _():
                    dw_ref[0, b, :, lanes] = tile[j, 0]
                    dw_ref[1, b, :, lanes] = tile[j, 1]

                @pl.when(parity == 1)
                def _():
                    dw_ref[0, b, :, lanes] = tile[j, 1]
                    dw_ref[1, b, :, lanes] = tile[j, 0]

        for j in range(per):
            near_copy(k * per + j).start()

    for load in loads[:4]:
        load.wait()
    weights_step(0)
    loads[4].wait()
    each(send_three, STEPS)
    weights_step(1)
    each(send_two, STEPS)
    each(lambda k: weights_step(k + 2), STEPS - 2)
    each(send_one, STEPS)
    for load in loads[5:]:
        load.wait()

    gs_ref[...] = jnp.zeros_like(gs_ref)

    def leave(k):
        part = chunk(k, size)
        return pltpu.make_async_copy(grad_ref.at[part], out_out.at[part], loc.at[7 + k])

    def own_chunk(k):
        part = chunk(k, size)
        total = project(me, k)
        x = x_ref[part].astype(F32)
        _, scaling = norm_rows(x, gain_ref[...])
        back_b(k).wait_recv()
        back_y(k).wait_recv()
        grad_norm = total + br_ref[part].astype(F32) + yr_ref[part].astype(F32)
        grad_rows, grad_gain = norm_back(x, scaling, gain_ref[...], grad_norm)
        grad_ref[part] = grad_ref[part] + grad_rows
        leave(k).start()
        gs_ref[0, 0:1] += grad_gain

    def near_sum(b):
        near_copy(b).wait_recv()
        sum_ref[b] = (dw_ref[0, b].astype(F32) + got_ref[b].astype(F32)).astype(BF)

        @pl.when(b != place)
        def _():
            level_copy(lax.rem(b + half - place, half)).start()

    def near_sums(kk):
        k = lax.rem(place // per + 1 + kk, STEPS)
        for n in range(per):
            near_sum(k * per + n)

    near_sums(0)

    def both(kk):
        near_sums(kk + 1)
        own_chunk(kk)

    each(both, STEPS - 1)
    own_chunk(STEPS - 1)

    gs_ref[0, 1:2] = gain_in[...]
    rounds = [
        [(seq, sib), (seq, far), (seq, farsib)],
        [(lax.rem(seq + j, seq_count), me) for j in range(1, seq_count)],
    ]

    def gain_copy(stage, n):
        slot = 3 * stage + n
        return push(gs_ref.at[stage], gr_ref.at[slot], gsnd.at[slot], grcv.at[slot], rounds[stage][n])

    gains = gs_ref[0]
    for stage in range(2):
        for n in range(len(rounds[stage])):
            gain_copy(stage, n).start()
        for n in range(len(rounds[stage])):
            gain_copy(stage, n).wait_recv()
            gains = gains + gr_ref[3 * stage + n]
        if stage == 0:
            gs_ref[1] = gains
    gains_ref[...] = gains

    total = sum_ref[place].astype(F32)
    for j in range(1, half):
        level_copy(j).wait_recv()
        total = total + zr_ref[j].astype(F32)
    for c in range(3):
        wqkv_ref[c] = total[:, c * width : (c + 1) * width]
    wout_ref[...] = total[:, wide:]

    def close(k):
        for made in (back_a, back_y, back_b):
            made(k).wait_send()

    each(close, STEPS)
    each(lambda k: leave(k).wait(), STEPS)
    each(lambda b: near_copy(b).wait_send(), half)
    for stage in range(2):
        for n in range(len(rounds[stage])):
            gain_copy(stage, n).wait_send()
    for j in range(1, half):
        level_copy(j).wait_send()


def last_call(mixed, w, x, gain, grad, normed, out_stay, out_got, gain_two):
    seq_count = lax.axis_size("seq")
    rows, model = x.shape
    half = seq_count // 2
    piece = model // seq_count
    wide, width = mixed.shape[-1], w.shape[-1]
    dma = pltpu.SemaphoreType.DMA
    shape = jax.ShapeDtypeStruct
    rows_bf = pltpu.VMEM((rows, model), BF)
    pieces = pltpu.VMEM((half, piece, wide + width), BF)
    return pl.pallas_call(
        functools.partial(last_kernel, seq_count),
        in_specs=[ANY] * 3 + [VM] + [ANY] * 4 + [VM],
        out_specs=[ANY] + [VM] * 3,
        out_shape=[
            shape((rows, model), F32),
            shape((3, piece, width), F32),
            shape((piece, width), F32),
            shape((8, model), F32),
        ],
        scratch_shapes=[
            pltpu.VMEM(a.shape, a.dtype) for a in (mixed, w, x, grad, normed, out_stay, out_got)
        ]
        + [rows_bf] * 6
        + [pltpu.VMEM((2, half, piece, wide + width), BF), pieces, pieces, pieces]
        + [pltpu.VMEM((2, 8, model), F32), pltpu.VMEM((seq_count + 2, 8, model), F32)]
        + [
            dma((3, STEPS)),
            dma((3, STEPS)),
            dma((half,)),
            dma((half,)),
            dma((half,)),
            dma((half,)),
            dma((seq_count + 2,)),
            dma((seq_count + 2,)),
            dma((7 + STEPS,)),
        ],
        compiler_params=params(collective_id=2, has_side_effects=True),
        cost_estimate=cost(90_000_000_000, 30_000_000),
        name="last",
    )(mixed, w, x, gain, grad, normed, out_stay, out_got, gain_two)


def shards(
    latents_in,
    gain_one,
    w_qkv,
    w_out,
    gain_two,
    w_gate,
    w_up,
    w_down,
    cotangent,
    doc_lengths,
    valid_lengths,
    hash_ids,
    hash_weights,
):
    local_rows, model_width = latents_in.shape
    local_width = w_qkv.shape[2]
    group_rows = 4 * local_rows
    units = w_gate.shape[1]
    rank = lax.axis_index("tp")
    seq_count = lax.axis_size("seq")
    sc = (jnp.full((1,), rank, jnp.int32), doc_lengths.reshape(-1), valid_lengths.reshape(-1))
    gain_one, gain_two = gain_one[None], gain_two[None]

    per_seq = -(-HASH_ROWS // seq_count)
    high_rows = -(-per_seq // (LANES * 8)) * 8

    qkv_weight = w_qkv.transpose(1, 0, 2)
    piece = model_width // seq_count
    wo_four = w_out.reshape(seq_count // 2, 2, piece, local_width)
    normed, qkv, sums, wo_all = front_call(
        latents_in, gain_one, qkv_weight, hash_ids, hash_weights, wo_four, high_rows
    )
    wo_all = wo_all.reshape(4, model_width, local_width)
    qkv, cotangent_late = lax.optimization_barrier((qkv, cotangent))

    def level_flip(x, j):
        return lax.ppermute(x, "seq", [(s, (s + 2 * j) % seq_count) for s in range(seq_count)])

    table_parts = [sums] + [level_flip(sums, j) for j in range(1, seq_count // 4 + 1)]
    qkv = qkv.reshape(group_rows, 3 * local_width)
    cot_far = flip(cotangent_late, "tp", 2)
    heads_out, lse = attend_call(sc, qkv)
    heads_four = heads_out.reshape(4, local_rows, local_width)
    (
        rest, far_down, grad_hidden, gain_two_part, up_keep, up_send, out_stay, out_away,
        grad_heads, hash_parts, *pieces,
    ) = middle_call(
        heads_four, wo_all, latents_in, gain_two, cotangent, cot_far,
        (w_gate.T, w_up.T, w_down.T), table_parts,
    )
    out_got = flip(out_away, "tp", 2)
    down_far = flip(far_down, "tp", 2)
    up_got = flip(up_send, "seq", 1)
    arrived = [level_flip(pieces[j], j) for j in range(1, seq_count // 2)]
    hash_parts = hash_parts.reshape(2, seq_count // 2, hash_ids.shape[0], high_rows, LANES)
    mixed, hash_counts = attend_back_call(
        sc, grad_heads.reshape(group_rows, local_width), qkv, heads_out, lse, hash_parts, HASH_ROWS
    )
    mixed, up_got, arrived, down_far, out_got = lax.optimization_barrier(
        (mixed, up_got, arrived, down_far, out_got)
    )
    grad_latents, qkv_total, out_total, gains = last_call(
        mixed.reshape(4, local_rows, -1), qkv_weight, latents_in, gain_one, grad_hidden,
        normed, out_stay, out_got, gain_two_part,
    )
    total = pieces[0].astype(F32)
    for piece in arrived:
        total = total + piece.astype(F32)
    up_total = up_keep.astype(F32) + up_got.astype(F32)
    latents_out = (rest + down_far.astype(F32)).astype(BF)
    upright = lambda w: w.T if w.shape[0] == units else w
    return (
        latents_out,
        grad_latents,
        gains[0],
        qkv_total.transpose(1, 0, 2),
        out_total,
        gains[1],
        upright(total[1]),
        upright(up_total),
        upright(total[0]),
        hash_counts,
    )


def solution(mesh):
    in_specs = (
        P(("seq", "tp"), None),
        P(),
        P(None, None, "tp"),
        P(None, "tp"),
        P(),
        P(None, "tp"),
        P(None, "tp"),
        P(None, "tp"),
        P(("seq", "tp"), None),
        P("seq", None),
        P("seq", None),
        P(None, ("seq", "tp")),
        P(None, ("seq", "tp")),
    )
    out_specs = (
        P(("seq", "tp"), None),
        P(("seq", "tp"), None),
        P(),
        P("seq", None, "tp"),
        P("seq", "tp"),
        P(),
        P("seq", "tp"),
        P("seq", "tp"),
        P("seq", "tp"),
        P(),
    )
    return jax.shard_map(shards, mesh=mesh, in_specs=in_specs, out_specs=out_specs, check_vma=False)
```

```python
import functools

import jax
import jax.numpy as jnp
from jax import lax
from jax.experimental import pallas as pl
from jax.experimental.pallas import tpu as pltpu
from jax.sharding import PartitionSpec as P

HEAD_DIM = 64
HASH_ROWS = 500002
EPSILON = 1e-05
MASKED = -1e30
BF = jnp.bfloat16
F32 = jnp.float32
QB = 256
LANES = 256
STEPS = 4
VMEM_BYTES = 60 * 1024 * 1024
MESH = pl.DeviceIdType.MESH


def flip(x, axis, bits):
    count = lax.axis_size(axis)
    return lax.ppermute(x, axis, [(i, i ^ bits) for i in range(count)])


def dot(a, b):
    return lax.dot_general(a, b, (((1,), (0,)), ((), ())), preferred_element_type=F32)


def dot_nt(a, b):
    return lax.dot_general(a, b, (((1,), (1,)), ((), ())), preferred_element_type=F32)


def dot_tn(a, b):
    return lax.dot_general(a, b, (((0,), (0,)), ((), ())), preferred_element_type=F32)


def cost(flops, moved):
    return pl.CostEstimate(flops=flops, bytes_accessed=moved, transcendentals=0)


def params(**more):
    return pltpu.CompilerParams(vmem_limit_bytes=VMEM_BYTES, **more)


def whole(shape):
    return pl.BlockSpec(shape, lambda i, *sc: (0,) * len(shape))


VM = pl.BlockSpec(memory_space=pltpu.VMEM)
ANY = pl.BlockSpec(memory_space=pl.ANY)


def places():
    me = lax.axis_index("tp")
    core = lax.rem(me, 2)
    sib = me + 1 - 2 * core
    far = lax.rem(me + 2, 4)
    return me, sib, far, lax.rem(sib + 2, 4), core


def push(src, dst, send, recv, where):
    return pltpu.make_async_remote_copy(
        src_ref=src,
        dst_ref=dst,
        send_sem=send,
        recv_sem=recv,
        device_id={"seq": where[0], "tp": where[1]},
        device_id_type=MESH,
    )


def greet(others):
    barrier = pltpu.get_barrier_semaphore()
    for seq, tp in others:
        pl.semaphore_signal(
            barrier, inc=1, device_id={"seq": seq, "tp": tp}, device_id_type=MESH
        )
    pl.semaphore_wait(barrier, len(others))


def each(body, count):
    lax.fori_loop(0, count, lambda k, c: (body(k), c)[1], 0)


def chunk(k, size):
    return pl.ds(pl.multiple_of(k * size, size), size)


def norm_rows(row_data, gain):
    scaling = lax.rsqrt(jnp.mean(row_data * row_data, axis=-1, keepdims=True) + EPSILON)
    return (row_data * scaling * gain, scaling)


def norm_back(row_data, scaling, gain, grad_norm):
    weighted = grad_norm * gain
    inner_mean = jnp.mean(weighted * row_data, axis=-1, keepdims=True)
    grad_rows = scaling * weighted - row_data * scaling * scaling * scaling * inner_mean
    grad_gain = jnp.sum(grad_norm * row_data * scaling, axis=0, keepdims=True)
    return (grad_rows, grad_gain)


def front_kernel(
    seq_count, x_ref, gain_ref, w_ref, ids_ref, weights_ref, wo_ref, n_out, qkv_out, hash_ref, out_out,
    out_ref, n_ref, qkv_ref, pair_ref, pack_ref, sum_ref, snd, rcv, psnd, prcv, osnd, orcv, loc,
):
    me, sib, far, farsib, core = places()
    seq = lax.axis_index("seq")
    near = seq + 1 - 2 * lax.rem(seq, 2)
    parity, place, half = lax.rem(seq, 2), seq // 2, seq_count // 2
    level = [lax.rem(seq + 2 * j, seq_count) for j in range(1, half)]
    greet([(seq, sib), (seq, far), (near, me)] + [(s, me) for s in level])
    rows = x_ref.shape[0]
    size = rows // STEPS
    tables = ids_ref.shape[0] // 2

    def pairs(low):
        ids = jnp.where(core == low, ids_ref[:tables], ids_ref[tables:]).astype(F32)
        weights = jnp.where(core == low, weights_ref[:tables], weights_ref[tables:])
        return jnp.concatenate([ids, weights, jnp.zeros((8 - 2 * tables, rows), F32)], axis=0)

    pack_ref[parity, place, me] = pairs(0)
    pair_ref[...] = pairs(1)
    mine = pack_ref.at[parity, place, me]
    stage_sib = push(pair_ref, mine, psnd.at[0], prcv.at[0], (seq, sib))
    stage_sib.start()
    both = pack_ref.at[parity, place, pl.ds(me - core, 2)]
    stage_far = push(both, both, psnd.at[1], prcv.at[1], (seq, far))
    four = pack_ref.at[parity, place]
    stage_level = [
        push(four, four, psnd.at[2 + j], prcv.at[2 + j], (s, me)) for j, s in enumerate(level)
    ]
    plane = pack_ref.at[parity]
    stage_near = push(plane, plane, psnd.at[half + 1], prcv.at[half + 1], (near, me))

    out_ref[me] = wo_ref[...]
    eighth = out_ref.at[me, place, parity]
    out_far = push(eighth, eighth, osnd.at[0], orcv.at[0], (seq, far))
    got_eighth = out_ref.at[far, place, parity]
    out_level = [
        push(got_eighth, got_eighth, osnd.at[2 + j], orcv.at[2 + j], (s, me))
        for j, s in enumerate(level)
    ]
    got_plane = out_ref.at[far, :, parity]
    out_near = push(got_plane, got_plane, osnd.at[half + 1], orcv.at[half + 1], (near, me))
    out_sib = push(out_ref.at[me], out_ref.at[me], osnd.at[1], orcv.at[1], (seq, sib))
    out_on = push(out_ref.at[far], out_ref.at[far], osnd.at[half + 2], orcv.at[half + 2], (seq, sib))

    def own(kind, k, to, block):
        part = n_ref.at[block, chunk(k, size)]
        return push(part, part, snd.at[kind, k], rcv.at[kind, k], (seq, to))

    for k in range(STEPS):
        part = slice(k * size, (k + 1) * size)
        normed, _ = norm_rows(x_ref[part].astype(F32), gain_ref[...])
        n_ref[me, part] = normed.astype(BF)
        if k == 0:
            stage_sib.wait_recv()
            stage_far.start()
            out_far.start()
            out_sib.start()
        own(1, k, far, me).start()
        own(0, k, sib, me).start()

    width = w_ref.shape[2]

    def project(block, k, length):
        part = chunk(k, length)
        for c in range(3):
            qkv_ref[block, part, c * width : (c + 1) * width] = dot(
                n_ref[block, part], w_ref[c]
            ).astype(BF)

    def out_home(block):
        return pltpu.make_async_copy(out_ref.at[block], out_out.at[block], loc.at[2, block])

    out_home(me).start()

    def homes(block):
        return [
            pltpu.make_async_copy(n_ref.at[block], n_out.at[block], loc.at[0, block]),
            pltpu.make_async_copy(qkv_ref.at[block], qkv_out.at[block], loc.at[1, block]),
        ]

    each(lambda k: project(me, k, rows // 2), 2)
    for copy in homes(me):
        copy.start()
    stage_far.wait_recv()
    for copy in stage_level:
        copy.start()
    out_far.wait_recv()
    for copy in out_level:
        copy.start()
    for k in range(STEPS):
        own(0, k, sib, me).wait_recv()
    each(lambda k: project(sib, k, rows // 2), 2)
    for copy in homes(sib):
        copy.start()

    def far_chunk(k):
        own(1, k, far, me).wait_recv()
        own(2, k, sib, far).start()
        project(far, k, size)

    def farsib_chunk(k):
        own(2, k, sib, far).wait_recv()
        project(farsib, k, size)

    far_chunk(0)
    for copy in stage_level:
        copy.wait_recv()
    stage_near.start()

    sum_ref[...] = jnp.zeros_like(sum_ref)
    high_rows = sum_ref.shape[1]
    first = seq * (high_rows * LANES)

    def sums(which):
        def body(b):
            for table in range(tables):
                line = lambda row: jnp.concatenate(
                    [pack_ref[which, b, t, row : row + 1] for t in range(4)], axis=1
                )
                ids = line(table).astype(jnp.int32) - first
                weights = line(table + tables)
                high = lax.broadcasted_iota(jnp.int32, (high_rows, 4 * rows), 0) == (ids >> 8)
                low = lax.broadcasted_iota(jnp.int32, (LANES, 4 * rows), 0) == (ids & (LANES - 1))
                high = jnp.where(high, 1.0, 0.0).astype(BF)
                low = jnp.where(low, weights, 0.0).astype(BF)
                sum_ref[table] += dot_nt(high, low)

        each(body, half)

    sums(parity)
    for copy in out_level:
        copy.wait_recv()
    out_near.start()
    each(lambda k: far_chunk(k + 1), STEPS - 2)
    each(farsib_chunk, STEPS - 1)
    stage_near.wait_recv()
    sums(1 - parity)
    out_near.wait_recv()
    out_on.start()
    out_home(far).start()
    out_sib.wait_recv()
    out_home(sib).start()
    far_chunk(STEPS - 1)
    for copy in homes(far):
        copy.start()
    hash_ref[...] = sum_ref[...].astype(BF)
    out_on.wait_recv()
    out_home(farsib).start()
    farsib_chunk(STEPS - 1)
    for copy in homes(farsib):
        copy.start()
    for k in range(STEPS):
        for kind in range(3):
            own(kind, k, sib, me).wait_send()
    stage_sib.wait_send()
    stage_far.wait_send()
    for copy in stage_level:
        copy.wait_send()
    stage_near.wait_send()
    for copy in [out_far, out_near, out_sib, out_on] + out_level:
        copy.wait_send()
    for block in (me, sib, far, farsib):
        out_home(block).wait()
    for block in (me, sib, far, farsib):
        for copy in homes(block):
            copy.wait()


def front_call(x, gain, w, ids, weights, wo, high_rows):
    seq_count = lax.axis_size("seq")
    rows, model = x.shape
    width = w.shape[0] * w.shape[2]
    tables = ids.shape[0] // 2
    half = seq_count // 2
    dma = pltpu.SemaphoreType.DMA
    return pl.pallas_call(
        functools.partial(front_kernel, seq_count),
        in_specs=[VM] * 6,
        out_specs=[ANY] * 2 + [VM, ANY],
        out_shape=[
            jax.ShapeDtypeStruct((4, rows, model), BF),
            jax.ShapeDtypeStruct((4, rows, width), BF),
            jax.ShapeDtypeStruct((tables, high_rows, LANES), BF),
            jax.ShapeDtypeStruct((4,) + wo.shape, BF),
        ],
        scratch_shapes=[
            pltpu.VMEM((4,) + wo.shape, BF),
            pltpu.VMEM((4, rows, model), BF),
            pltpu.VMEM((4, rows, width), BF),
            pltpu.VMEM((8, rows), F32),
            pltpu.VMEM((2, half, 4, 8, rows), F32),
            pltpu.VMEM((tables, high_rows, LANES), F32),
            dma((3, STEPS)),
            dma((3, STEPS)),
            dma((half + 2,)),
            dma((half + 2,)),
            dma((half + 3,)),
            dma((half + 3,)),
            dma((3, 4)),
        ],
        compiler_params=params(collective_id=0, has_side_effects=True),
        cost_estimate=cost(1_000_000, 1_000_000),
        name="front",
    )(x, gain, w, ids, weights, wo)


def doc_bounds(sc, places):
    _, lengths, valid = sc
    one = lengths[0]
    two = one + lengths[1]
    low = jnp.where(places >= two, two, jnp.where(places >= one, one, 0))
    end = jnp.where(
        places >= two, two + valid[2], jnp.where(places >= one, one + valid[1], valid[0])
    )
    return low, jnp.minimum(places, end - 1)


def head_rows(x, h):
    where = lax.broadcasted_iota(jnp.int32, x.shape, 0) // HEAD_DIM
    return jnp.where(where == h, x, jnp.zeros_like(x))


def attend_kernel(heads, rank, lengths, valid, qkv_ref, heads_ref, lse_ref, vt_ref, qt_ref, acc_ref, score_ref):
    sc = (rank, lengths, valid)
    width = heads * HEAD_DIM
    step = pl.program_id(0)

    @pl.when(step == 0)
    def _():
        for n in range(qkv_ref.shape[0] // QB):
            vt_ref[:, n * QB : (n + 1) * QB] = qkv_ref[n * QB : (n + 1) * QB, 2 * width :].T

    start = pl.multiple_of(step * QB, QB)
    q_t = qkv_ref[pl.ds(start, QB), :width].T * jnp.asarray(HEAD_DIM**-0.5, BF)
    for h in range(heads):
        qt_ref[:, h * QB : (h + 1) * QB] = head_rows(q_t, h)
    acc_ref[...] = jnp.zeros_like(acc_ref)
    places = start + lax.broadcasted_iota(jnp.int32, (1, QB), 1)
    low, high = doc_bounds(sc, places)
    low_first, _ = doc_bounds(sc, start)

    def body(kb, state):
        at = pl.multiple_of(kb * QB, QB)
        keys = qkv_ref[pl.ds(at, QB), width : 2 * width]
        value_t = vt_ref[:, pl.ds(at, QB)]
        spot = at + lax.broadcasted_iota(jnp.int32, (QB, QB), 0)
        allowed = (spot >= low) & (spot <= high)
        score_ref[...] = dot(keys, qt_ref[...])
        fresh = []
        for h in range(heads):
            top, total = state[h]
            scores = jnp.where(allowed, score_ref[:, h * QB : (h + 1) * QB], MASKED)
            new_top = jnp.maximum(top, jnp.max(scores, axis=0, keepdims=True))
            fade = jnp.exp(top - new_top)
            probs = jnp.exp(scores - new_top)
            total = total * fade + jnp.sum(probs, axis=0, keepdims=True)
            part = slice(h * HEAD_DIM, (h + 1) * HEAD_DIM)
            acc_ref[part] = acc_ref[part] * fade + dot(value_t[part], probs.astype(BF))
            fresh.append((new_top, total))
        return tuple(fresh)

    begin = tuple(
        (jnp.full((1, QB), MASKED, F32), jnp.zeros((1, QB), F32)) for _ in range(heads)
    )
    state = lax.fori_loop(low_first // QB, start // QB + 1, body, begin)
    lse_ref[...] = jnp.zeros_like(lse_ref)
    for h in range(heads):
        top, total = state[h]
        part = slice(h * HEAD_DIM, (h + 1) * HEAD_DIM)
        acc_ref[part] = acc_ref[part] * (1.0 / total)
        lse_ref[h : h + 1] = top + jnp.log(total)
    heads_ref[...] = acc_ref[...].T.astype(BF)


def attend_call(sc, qkv):
    rows, width = qkv.shape[0], qkv.shape[1] // 3
    heads = width // HEAD_DIM
    return pl.pallas_call(
        functools.partial(attend_kernel, heads),
        grid_spec=pltpu.PrefetchScalarGridSpec(
            num_scalar_prefetch=3,
            grid=(rows // QB,),
            in_specs=[whole(qkv.shape)],
            out_specs=[
                pl.BlockSpec((QB, width), lambda i, *sc: (i, 0)),
                pl.BlockSpec((8, QB), lambda i, *sc: (0, i)),
            ],
            scratch_shapes=[
                pltpu.VMEM((width, rows), BF),
                pltpu.VMEM((width, heads * QB), BF),
                pltpu.VMEM((width, QB), F32),
                pltpu.VMEM((QB, heads * QB), F32),
            ],
        ),
        out_shape=[
            jax.ShapeDtypeStruct((rows, width), BF),
            jax.ShapeDtypeStruct((8, rows), F32),
        ],
        compiler_params=params(),
        cost_estimate=cost(60_000_000_000, 8_000_000),
        name="attend",
    )(*sc, qkv)


def spread(table_ref, out_ref, flat_ref):
    parities, levels, tables, high_rows, _ = table_ref.shape
    unroll = next(u for u in (62, 32, 8) if high_rows % u == 0)
    for piece in range(parities * levels):
        p, q = piece % parities, piece // parities
        for n in range(tables):
            for side in range(2):
                flat_ref[side, n * high_rows : (n + 1) * high_rows] = table_ref[
                    p, q, n, :, side * 128 : (side + 1) * 128
                ].astype(F32)

        def body(n, carry):
            for u in range(unroll):
                row = n * unroll + u
                for side in range(2):
                    at = pl.multiple_of((piece * high_rows + row) * LANES + side * 128, 128)
                    out_ref[:, pl.ds(at, 128)] = flat_ref[side, pl.ds(row, tables, stride=high_rows)]
            return carry

        lax.fori_loop(0, high_rows // unroll, body, 0)


def attend_back_kernel(
    heads, rank, lengths, valid, grad_ref, qkv_ref, heads_ref, lse_ref, table_ref, mixed_ref, spread_ref,
    kt_ref, qt_ref, gt_ref, qs_ref, gs_ref, dqt_ref, dk_ref, dv_ref, score_ref, prob_ref, flat_ref,
):
    sc = (rank, lengths, valid)
    width = heads * HEAD_DIM
    step = pl.program_id(0)
    rows = qkv_ref.shape[0]

    @pl.when(step == 0)
    def _():
        for n in range(rows // QB):
            kt_ref[:, n * QB : (n + 1) * QB] = qkv_ref[n * QB : (n + 1) * QB, width : 2 * width].T
        dk_ref[...] = jnp.zeros_like(dk_ref)
        dv_ref[...] = jnp.zeros_like(dv_ref)

    start = pl.multiple_of(step * QB, QB)
    grad = grad_ref[...]
    grad_t = grad.T
    out_t = heads_ref[...].T
    product = grad_t.astype(F32) * out_t.astype(F32)
    query = qkv_ref[pl.ds(start, QB), :width] * jnp.asarray(HEAD_DIM**-0.5, BF)
    q_t = query.T
    inner = []
    for h in range(heads):
        part = slice(h * HEAD_DIM, (h + 1) * HEAD_DIM)
        inner.append(jnp.sum(product[part], axis=0, keepdims=True))
        qt_ref[:, h * QB : (h + 1) * QB] = head_rows(q_t, h)
        gt_ref[:, h * QB : (h + 1) * QB] = head_rows(grad_t, h)
    qs_ref[...] = q_t
    gs_ref[...] = grad_t
    dqt_ref[...] = jnp.zeros_like(dqt_ref)
    places = start + lax.broadcasted_iota(jnp.int32, (1, QB), 1)
    low, high = doc_bounds(sc, places)
    low_first, _ = doc_bounds(sc, start)

    def body(kb, carry):
        at = pl.multiple_of(kb * QB, QB)
        keys = qkv_ref[pl.ds(at, QB), width : 2 * width]
        values = qkv_ref[pl.ds(at, QB), 2 * width :]
        spot = at + lax.broadcasted_iota(jnp.int32, (QB, QB), 0)
        allowed = (spot >= low) & (spot <= high)
        score_ref[...] = dot(keys, qt_ref[...])
        prob_ref[...] = dot(values, gt_ref[...])
        for h in range(heads):
            part = slice(h * HEAD_DIM, (h + 1) * HEAD_DIM)
            lanes = slice(h * QB, (h + 1) * QB)
            scores = jnp.where(allowed, score_ref[:, lanes], MASKED)
            probs = jnp.exp(scores - lse_ref[h : h + 1])
            grad_scores = (probs * (prob_ref[:, lanes] - inner[h])).astype(BF)
            dqt_ref[part] += dot(kt_ref[part, pl.ds(at, QB)], grad_scores)
            dv_ref[part, pl.ds(at, QB)] += dot_nt(gs_ref[part], probs.astype(BF))
            dk_ref[part, pl.ds(at, QB)] += dot_nt(qs_ref[part], grad_scores)
        return carry

    lax.fori_loop(low_first // QB, start // QB + 1, body, 0)
    spread(table_ref, spread_ref, flat_ref)
    dq = (dqt_ref[...] * HEAD_DIM**-0.5).T.astype(BF)
    mixed_ref[pl.ds(start, QB), :width] = dq

    @pl.when(step == pl.num_programs(0) - 1)
    def _():
        for n in range(rows // QB):
            part = slice(n * QB, (n + 1) * QB)
            mixed_ref[part, width : 2 * width] = dk_ref[:, part].T.astype(BF)
            mixed_ref[part, 2 * width :] = dv_ref[:, part].T.astype(BF)


def attend_back_call(sc, grad, qkv, heads_out, lse, tables, hash_rows):
    rows, width = qkv.shape[0], qkv.shape[1] // 3
    heads = width // HEAD_DIM
    parities, levels, count, high_rows, lanes = tables.shape
    per = parities * levels // (rows // QB)
    if per == 1:
        table_spec = pl.BlockSpec(
            (1, 1, count, high_rows, lanes), lambda i, *sc: (i % 2, i // 2, 0, 0, 0)
        )
    else:
        table_spec = pl.BlockSpec(
            (2, per // 2, count, high_rows, lanes), lambda i, *sc: (0, i, 0, 0, 0)
        )
    return pl.pallas_call(
        functools.partial(attend_back_kernel, heads),
        grid_spec=pltpu.PrefetchScalarGridSpec(
            num_scalar_prefetch=3,
            grid=(rows // QB,),
            in_specs=[
                pl.BlockSpec((QB, width), lambda i, *sc: (i, 0)),
                whole(qkv.shape),
                pl.BlockSpec((QB, width), lambda i, *sc: (i, 0)),
                pl.BlockSpec((8, QB), lambda i, *sc: (0, i)),
                table_spec,
            ],
            out_specs=[
                whole((rows, 3 * width)),
                pl.BlockSpec((count, per * high_rows * lanes), lambda i, *sc: (0, i)),
            ],
            scratch_shapes=[
                pltpu.VMEM((width, rows), BF),
                pltpu.VMEM((width, heads * QB), BF),
                pltpu.VMEM((width, heads * QB), BF),
                pltpu.VMEM((width, QB), BF),
                pltpu.VMEM((width, QB), BF),
                pltpu.VMEM((width, QB), F32),
                pltpu.VMEM((width, rows), F32),
                pltpu.VMEM((width, rows), F32),
                pltpu.VMEM((QB, heads * QB), F32),
                pltpu.VMEM((QB, heads * QB), F32),
                pltpu.VMEM((2, count * high_rows, 128), F32),
            ],
        ),
        out_shape=[
            jax.ShapeDtypeStruct((rows, 3 * width), BF),
            jax.ShapeDtypeStruct((count, hash_rows), F32),
        ],
        compiler_params=params(),
        cost_estimate=cost(90_000_000_000, 12_000_000),
        name="attend_back",
    )(*sc, grad, qkv, heads_out, lse, tables)


def middle_kernel(
    seq_count, heads_ref, wo_in, x_in, gain_ref, c0_in, c2_in, wg_in, wu_in, wd_in, *refs
):
    half = seq_count // 2
    early = half // 2 + 1
    table_ins, refs = refs[:early], refs[early:]
    rest_out, fardown_out, grad_out, gain_out, keep_out, send_out = refs[:6]
    ostay_out, oaway_out, gh_out, table_ref = refs[6:10]
    piece_refs, refs = refs[10 : 10 + half], refs[10 + half :]
    (
        rest_ref, grad_ref, wo_ref, c0, c1, c2, c3, x_ref,
        ps_ref, pr_ref, n_ref, wg_ref, wu_ref, wd_ref, act_ref, gg_ref, gu_ref,
        g0_ref, g1s_ref, g1r_ref, d0_ref, d1s_ref, d1r_ref,
        ys_ref, yr_ref, all_ref, gh_ref,
        stay_ref, away_ref, got_ref, up_ref, upgot_ref,
        snd, rcv, xsnd, xrcv, zsnd, zrcv, tsnd, trcv, psnd, prcv, loc, wloc, hloc,
    ) = refs
    fardown_ref, gb_ref, ar_ref, br_ref = x_ref, d0_ref, g1r_ref, d1r_ref
    me, sib, far, farsib, core = places()
    seq = lax.axis_index("seq")
    parity, place = lax.rem(seq, 2), seq // 2
    near = seq + 1 - 2 * parity
    level = [lax.rem(seq + 2 * j, seq_count) for j in range(1, half)]

    loads = [
        pltpu.make_async_copy(w_in, w_ref.at[: w_in.shape[0]], wloc.at[n])
        for n, (w_in, w_ref) in enumerate(((wg_in, wg_ref), (wu_in, wu_ref), (wd_in, wd_ref)))
    ]
    pairs = ((wo_in, wo_ref), (x_in, x_ref), (c0_in, c0), (c2_in, c2), (heads_ref.at[me], all_ref.at[me]))
    first = [
        pltpu.make_async_copy(src, dst, wloc.at[4 + n]) for n, (src, dst) in enumerate(pairs)
    ]
    for load in first + loads:
        load.start()
    greet([(seq, sib), (seq, far), (seq, farsib), (near, me)] + [(s, me) for s in level])
    rows, model = x_in.shape
    size = rows // STEPS
    units = wg_in.shape[0]
    long = rows // 2
    kinds = iter(range(100))

    def maker(src, dst, to, length=size):
        kind = next(kinds)

        def made(k):
            part = chunk(k, length)
            return push(src.at[part], dst.at[part], snd.at[kind, k], rcv.at[kind, k], (seq, to))

        return made

    head_copies = [
        maker(heads_ref.at[to], all_ref.at[me], to) for to in (far, farsib, sib)
    ]
    grad_copies = [maker(gh_ref.at[to], gh_out.at[me], to) for to in (far, farsib, sib)]
    two_sib = maker(n_ref.at[me], n_ref.at[me], sib)
    two_far = maker(n_ref.at[me], n_ref.at[me], far)
    two_on = maker(n_ref.at[far], n_ref.at[far], sib)
    back_one = maker(g1s_ref, g1r_ref, sib, long)
    down_one = maker(d1s_ref, d1r_ref, sib, long)
    back_a = maker(g1s_ref, ar_ref, sib, long)
    back_y = maker(ys_ref, yr_ref, far)
    down_three = maker(d1s_ref, br_ref, sib, long)
    cot_one = maker(c0_in, c1, sib, long)
    cot_three = maker(c2_in, c3, sib, long)

    def grad_home(k):
        part = chunk(k, size)
        return pltpu.make_async_copy(gh_ref.at[me, part], gh_out.at[me, part], loc.at[0, k])

    def table_spot(which, j):
        return table_ref.at[which, lax.rem(place + half - j, half), core]

    def table_home(j):
        return pltpu.make_async_copy(table_ins[j], table_spot(parity, j), hloc.at[j])

    def table_level(j):
        return push(
            table_ins[0], table_ref.at[parity, place, core], tsnd.at[0, j], trcv.at[0, j], (level[j - 1], me)
        )

    def table_near(j):
        spot = table_spot(parity, j)
        return push(table_ins[j] if j < early else spot, spot, tsnd.at[1, j], trcv.at[1, j], (near, me))

    def table_sib(same, j):
        spot = table_spot(parity if same else 1 - parity, j)
        kind = 2 if same else 3
        src = table_ins[j] if same and j < early else spot
        return push(src, spot, tsnd.at[kind, j], trcv.at[kind, j], (seq, sib))

    for k in range(STEPS):
        for made in head_copies:
            made(k).start()
    for j in range(early, half):
        table_level(j).start()
    for j in range(early):
        table_home(j).start()
        table_near(j).start()
        table_sib(True, j).start()
    for k in range(2):
        cot_one(k).start()
        cot_three(k).start()

    wide = act_ref.shape[0]
    if wide > units:
        for ref in (act_ref, gg_ref, gu_ref, wg_ref, wu_ref, wd_ref):
            ref[units:] = jnp.zeros((wide - units, ref.shape[1]), BF)
    for load in first + loads:
        load.wait()
    for k in range(2):
        cot_one(k).wait_recv()
        cot_three(k).wait_recv()

    def feed(m, block_a, block_b, ca, cb):
        part = chunk(m, long)
        normed = jnp.concatenate([n_ref[block_a, part], n_ref[block_b, part]], axis=0)
        cot = jnp.concatenate([ca[part], cb[part]], axis=0)
        gate = dot_nt(wg_ref[:units], normed)
        up = dot_nt(wu_ref[:units], normed)
        sig = jax.nn.sigmoid(gate)
        silu = gate * sig
        act = (silu * up).astype(BF)
        grad_act = dot_nt(wd_ref[:units], cot)
        grad_gate = (grad_act * up * sig * (1.0 + gate * (1.0 - sig))).astype(BF)
        grad_up = (grad_act * silu).astype(BF)
        lanes = [
            pl.ds(pl.multiple_of(block * rows + m * long, long), long) for block in (block_a, block_b)
        ]
        for ref, value in ((act_ref, act), (gg_ref, grad_gate), (gu_ref, grad_up)):
            ref[:units, lanes[0]] = value[:, :long]
            ref[:units, lanes[1]] = value[:, long:]
        pair = lambda ref: jnp.concatenate([ref[:, lanes[0]], ref[:, lanes[1]]], axis=1)
        back = dot_tn(pair(gg_ref), wg_ref[...]) + dot_tn(pair(gu_ref), wu_ref[...])
        return back, dot_tn(pair(act_ref), wd_ref[...])

    def own_chunk(k):
        part = chunk(k, size)
        hidden = x_ref[part].astype(F32) + dot_nt(all_ref[me, part], wo_ref[me])
        for made in head_copies:
            made(k).wait_recv()
        for block in (sib, far, farsib):
            hidden = hidden + dot_nt(all_ref[block, part], wo_ref[block])
        rest_ref[part] = hidden
        normed, _ = norm_rows(hidden, gain_ref[...])
        n_ref[me, part] = normed.astype(BF)
        two_far(k).start()
        two_sib(k).start()

    def own_half(m):
        own_chunk(2 * m)
        own_chunk(2 * m + 1)
        two_sib(2 * m).wait_recv()
        two_sib(2 * m + 1).wait_recv()
        part = chunk(m, long)
        back, down = feed(m, me, sib, c0, c1)
        g0_ref[part] = back[:long].astype(BF)
        g1s_ref[part] = back[long:].astype(BF)
        back_one(m).start()
        d0_ref[part] = down[:long].astype(BF)
        d1s_ref[part] = down[long:].astype(BF)
        down_one(m).start()

    piece = model // seq_count
    span = model // STEPS
    per = half // STEPS
    upright = piece % 128 == 0

    def weight_away(w, b):
        return push(
            away_ref.at[w, b], got_ref.at[w, b], xsnd.at[w, b], xrcv.at[w, b], (near, me)
        )

    def up_away(j):
        b = lax.rem(place + j, half)
        return push(
            up_ref.at[b], upgot_ref.at[j - 1], zsnd.at[j], zrcv.at[j],
            (lax.rem(seq + 2 * j, seq_count), me),
        )

    def weight_tile(w, k, blocks):
        cots = (c0, c1, c2, c3)
        order = (me, sib, far, farsib)
        left = (act_ref, gg_ref, gu_ref)[w]
        total = None
        for r in blocks:
            cols = chunk(k, span)
            right = cots[r][:, cols] if w == 0 else n_ref[order[r], :, cols]
            lanes = pl.ds(pl.multiple_of(order[r] * rows, rows), rows)
            term = dot(left[:units, lanes], right)
            total = term if total is None else total + term
        return total

    def weights_step(kk):
        k = lax.rem(place // per + 1 + kk, STEPS)
        for w in range(3):
            tile = weight_tile(w, k, range(4))
            tile = tile if upright else tile.T

            def put(ref, value):
                ref[...] = value.astype(BF)

            for n in range(per):
                b = k * per + n
                take = lambda i: slice(i * piece, (i + 1) * piece)
                even = tile[:, take(2 * n)] if upright else tile[take(2 * n)]
                odd = tile[:, take(2 * n + 1)] if upright else tile[take(2 * n + 1)]
                if w == 2:
                    put(up_ref.at[b, 0], even)
                    put(up_ref.at[b, 1], odd)

                    @pl.when(b != place)
                    def _():
                        up_away(lax.rem(b + half - place, half)).start()

                else:

                    @pl.when(parity == 0)
                    def _():
                        put(stay_ref.at[w, b], even)
                        put(away_ref.at[w, b], odd)

                    @pl.when(parity == 1)
                    def _():
                        put(stay_ref.at[w, b], odd)
                        put(away_ref.at[w, b], even)

                    weight_away(w, b).start()

    each(own_half, 2)
    for j in range(early, half):
        table_level(j).wait_recv()
        table_near(j).start()
        table_sib(True, j).start()

    def far_sum(k):
        part = chunk(k, size)
        ys_ref[part] = (ys_ref[part].astype(F32) + ar_ref[part].astype(F32)).astype(BF)
        back_y(k).start()

    def far_half(m):
        part = chunk(m, long)
        back_one(m).wait_recv()
        g0_ref[part] = (g0_ref[part].astype(F32) + g1r_ref[part].astype(F32)).astype(BF)
        down_one(m).wait_recv()
        d0_ref[part] = (d0_ref[part].astype(F32) + d1r_ref[part].astype(F32)).astype(BF)
        for k in (2 * m, 2 * m + 1):
            two_far(k).wait_recv()
            two_on(k).start()
        for k in (2 * m, 2 * m + 1):
            two_on(k).wait_recv()
        back, down = feed(m, far, farsib, c2, c3)
        back_one(m).wait_send()
        g1s_ref[part] = back[long:].astype(BF)
        back_a(m).start()
        ys_ref[part] = back[:long].astype(BF)
        down_one(m).wait_send()
        d1s_ref[part] = down[long:].astype(BF)
        down_three(m).start()
        fardown_ref[part] = down[:long].astype(BF)
        back_a(m).wait_recv()
        far_sum(2 * m)
        far_sum(2 * m + 1)

    each(far_half, 2)

    gain_out[...] = jnp.zeros_like(gain_out)

    def leave(k, n, ref, out):
        part = chunk(k, size)
        return pltpu.make_async_copy(ref.at[part], out.at[part], loc.at[1 + n, k])

    def back_chunk(k):
        weights_step(k)
        part = chunk(k, size)
        back_y(k).wait_recv()
        grad_norm = g0_ref[part].astype(F32) + yr_ref[part].astype(F32)
        hidden = rest_ref[part]
        _, scaling = norm_rows(hidden, gain_ref[...])
        grad_rows, grad_gain = norm_back(hidden, scaling, gain_ref[...], grad_norm)
        grad = c0[part].astype(F32) + grad_rows
        grad_ref[part] = grad
        leave(k, 0, grad_ref, grad_out).start()
        rest_ref[part] = hidden + d0_ref[part].astype(F32)
        leave(k, 1, rest_ref, rest_out).start()
        fardown_ref[part] = (fardown_ref[part].astype(F32) + br_ref[part].astype(F32)).astype(BF)
        leave(k, 2, fardown_ref, fardown_out).start()
        gain_out[...] += grad_gain
        gb_ref[part] = grad.astype(BF)
        low = grad.astype(BF)
        for block in (far, farsib, sib, me):
            gh_ref[block, part] = dot(low, wo_ref[block]).astype(BF)
        for made in grad_copies:
            made(k).start()
        grad_home(k).start()

    for m in range(2):
        down_three(m).wait_recv()
    each(back_chunk, STEPS)
    for j in range(half):
        table_near(j).wait_recv()
        table_sib(False, j).start()

    def out_part(block):
        return dot_tn(all_ref[block], gb_ref[...])

    def out_sib(n):
        return push(ps_ref.at[n], pr_ref.at[n], psnd.at[n], prcv.at[n], (seq, sib))

    for n, block in enumerate((farsib, sib)):
        ps_ref[n] = out_part(block).astype(BF)
        out_sib(n).start()
    for n, (block, out) in enumerate(((far, oaway_out), (me, ostay_out))):
        total = out_part(block)
        out_sib(n).wait_recv()
        out[...] = (total + pr_ref[n].astype(F32)).astype(BF).T

    for j in range(half):
        b = lax.rem(place + j, half)
        for w in range(2):
            weight_away(w, b).wait_recv()
            piece_refs[j][w] = (stay_ref[w, b].astype(F32) + got_ref[w, b].astype(F32)).astype(BF)

    def up_sum(which):
        total = up_ref[place, which].astype(F32)
        for j in range(1, half):
            total = total + upgot_ref[j - 1, which].astype(F32)
        return total.astype(BF)

    for j in range(1, half):
        up_away(j).wait_recv()
    keep_out[...] = up_sum(parity)
    send_out[...] = up_sum(1 - parity)

    def close(k):
        grad_home(k).wait()
        leave(k, 0, grad_ref, grad_out).wait()
        leave(k, 1, rest_ref, rest_out).wait()
        leave(k, 2, fardown_ref, fardown_out).wait()
        for made in grad_copies:
            made(k).wait_recv()
        for made in [two_sib, two_far, two_on, back_y] + head_copies + grad_copies:
            made(k).wait_send()

    each(close, STEPS)
    for m in range(2):
        for made in (back_a, down_three, cot_one, cot_three):
            made(m).wait_send()
    for copy in (out_sib(0), out_sib(1)):
        copy.wait_send()
    for j in range(early):
        table_home(j).wait()
    for j in range(half):
        table_sib(True, j).wait_recv()
        table_sib(False, j).wait_recv()
        table_near(j).wait_send()
        table_sib(True, j).wait_send()
        table_sib(False, j).wait_send()
        for w in range(2):
            weight_away(w, j).wait_send()
    for j in range(early, half):
        table_level(j).wait_send()
    for j in range(1, half):
        up_away(j).wait_send()


def middle_call(heads_out, wo, x, gain, cot, cot_far, weights, tables):
    seq_count = lax.axis_size("seq")
    rows, model = x.shape
    half = seq_count // 2
    piece = model // seq_count
    units = weights[0].shape[0]
    wide = units + -units % 256
    block = (units, piece) if piece % 128 == 0 else (piece, units)
    dma = pltpu.SemaphoreType.DMA
    shape = jax.ShapeDtypeStruct
    vm = pltpu.VMEM
    rows_bf = vm((rows, model), BF)
    return pl.pallas_call(
        functools.partial(middle_kernel, seq_count),
        in_specs=[ANY] * 3 + [VM] + [ANY] * (5 + len(tables)),
        out_specs=[ANY] * 3 + [VM] * 5 + [ANY] * 2 + [VM] * half,
        out_shape=[
            shape((rows, model), F32),
            shape((rows, model), BF),
            shape((rows, model), F32),
            shape((1, model), F32),
            shape(block, BF),
            shape(block, BF),
            shape((model, heads_out.shape[2]), BF),
            shape((model, heads_out.shape[2]), BF),
            shape(heads_out.shape, BF),
            shape((2, half, 2) + tables[0].shape, BF),
        ]
        + [shape((2,) + block, BF)] * half,
        scratch_shapes=[vm((rows, model), F32)] * 2
        + [vm(wo.shape, BF)]
        + [rows_bf] * 5
        + [vm((2, wo.shape[2], model), BF)] * 2
        + [vm((4, rows, model), BF)]
        + [vm((wide, model), BF)] * 3
        + [vm((wide, 4 * rows), BF)] * 3
        + [rows_bf] * 8
        + [vm(heads_out.shape, BF)] * 2
        + [vm((2, half) + block, BF)] * 3
        + [vm((half, 2) + block, BF), vm((half - 1, 2) + block, BF)]
        + [dma((20, STEPS))] * 2
        + [dma((2, half))] * 2
        + [dma((half,))] * 2
        + [dma((4, half))] * 2
        + [dma((2,))] * 2
        + [dma((4, STEPS)), dma((9,)), dma((half // 2 + 1,))],
        compiler_params=params(collective_id=1, has_side_effects=True),
        cost_estimate=cost(100_000_000_000, 30_000_000),
        name="middle",
    )(heads_out, wo, x, gain, cot, cot_far, *weights, *tables)


def last_kernel(
    seq_count, mixed_in, w_in, x_in, gain_ref, grad_in, n_in, ostay_in, ogot_in, gain_in,
    out_out, wqkv_ref, wout_ref, gains_ref,
    mixed_ref, w_ref, x_ref, grad_ref, n_ref, ostay_ref, ogot_ref,
    as_ref, ar_ref, ys_ref, yr_ref, bs_ref, br_ref, dw_ref, got_ref, sum_ref, zr_ref, gs_ref, gr_ref,
    snd, rcv, xsnd, xrcv, zsnd, zrcv, gsnd, grcv, loc,
):
    me, sib, far, farsib, core = places()
    seq = lax.axis_index("seq")
    parity, place, half = lax.rem(seq, 2), seq // 2, seq_count // 2
    near = seq + 1 - 2 * parity
    loads = [
        pltpu.make_async_copy(src, dst, loc.at[n])
        for n, (src, dst) in enumerate(
            (
                (mixed_in, mixed_ref), (n_in, n_ref), (ostay_in, ostay_ref),
                (ogot_in, ogot_ref), (w_in, w_ref), (x_in, x_ref), (grad_in, grad_ref),
            )
        )
    ]
    for load in loads:
        load.start()
    greet(
        [(seq, sib), (seq, far), (seq, farsib)]
        + [(lax.rem(seq + j, seq_count), me) for j in range(1, seq_count)]
    )
    rows, model = x_ref.shape
    size = rows // STEPS
    piece = model // seq_count
    wide = mixed_ref.shape[-1]

    def copy(kind, k, src, dst, to):
        return push(
            src.at[chunk(k, size)], dst.at[chunk(k, size)], snd.at[kind, k], rcv.at[kind, k], (seq, to)
        )

    back_a = lambda k: copy(0, k, as_ref, ar_ref, sib)
    back_y = lambda k: copy(1, k, ys_ref, yr_ref, far)
    back_b = lambda k: copy(2, k, bs_ref, br_ref, sib)

    def near_copy(b):
        return push(dw_ref.at[1, b], got_ref.at[b], xsnd.at[b], xrcv.at[b], (near, me))

    def level_copy(j):
        b = lax.rem(place + j, half)
        return push(
            sum_ref.at[b], zr_ref.at[j], zsnd.at[j], zrcv.at[j], (lax.rem(seq + 2 * j, seq_count), me)
        )

    width = w_ref.shape[2]

    def project(block, k):
        part = chunk(k, size)
        terms = [
            dot_nt(mixed_ref[block, part, c * width : (c + 1) * width], w_ref[c]) for c in range(3)
        ]
        return terms[0] + terms[1] + terms[2]

    def send_three(k):
        as_ref[chunk(k, size)] = project(farsib, k).astype(BF)
        back_a(k).start()

    def send_two(k):
        part = project(far, k)
        back_a(k).wait_recv()
        ys_ref[chunk(k, size)] = (part + ar_ref[chunk(k, size)].astype(F32)).astype(BF)
        back_y(k).start()

    def send_one(k):
        bs_ref[chunk(k, size)] = project(sib, k).astype(BF)
        back_b(k).start()

    span = model // STEPS
    per = half // STEPS

    def weights_step(kk):
        k = lax.rem(place // per + 1 + kk, STEPS)
        cols = chunk(k, span)
        total = None
        for r in range(4):
            term = dot_tn(n_ref[r, :, cols], mixed_ref[r])
            total = term if total is None else total + term
        to_out = ostay_ref[cols].astype(F32) + ogot_ref[cols].astype(F32)
        for lanes, value in ((slice(0, wide), total), (slice(wide, wide + width), to_out)):
            tile = value.astype(BF).reshape(per, 2, piece, value.shape[1])
            for j in range(per):
                b = k * per + j

                @pl.when(parity == 0)
                def _():
                    dw_ref[0, b, :, lanes] = tile[j, 0]
                    dw_ref[1, b, :, lanes] = tile[j, 1]

                @pl.when(parity == 1)
                def _():
                    dw_ref[0, b, :, lanes] = tile[j, 1]
                    dw_ref[1, b, :, lanes] = tile[j, 0]

        for j in range(per):
            near_copy(k * per + j).start()

    for load in loads[:4]:
        load.wait()
    weights_step(0)
    loads[4].wait()
    each(send_three, STEPS)
    weights_step(1)
    each(send_two, STEPS)
    each(lambda k: weights_step(k + 2), STEPS - 2)
    each(send_one, STEPS)
    for load in loads[5:]:
        load.wait()

    gs_ref[...] = jnp.zeros_like(gs_ref)

    def leave(k):
        part = chunk(k, size)
        return pltpu.make_async_copy(grad_ref.at[part], out_out.at[part], loc.at[7 + k])

    def own_chunk(k):
        part = chunk(k, size)
        total = project(me, k)
        x = x_ref[part].astype(F32)
        _, scaling = norm_rows(x, gain_ref[...])
        back_b(k).wait_recv()
        back_y(k).wait_recv()
        grad_norm = total + br_ref[part].astype(F32) + yr_ref[part].astype(F32)
        grad_rows, grad_gain = norm_back(x, scaling, gain_ref[...], grad_norm)
        grad_ref[part] = grad_ref[part] + grad_rows
        leave(k).start()
        gs_ref[0, 0:1] += grad_gain

    def near_sum(b):
        near_copy(b).wait_recv()
        sum_ref[b] = (dw_ref[0, b].astype(F32) + got_ref[b].astype(F32)).astype(BF)

        @pl.when(b != place)
        def _():
            level_copy(lax.rem(b + half - place, half)).start()

    def near_sums(kk):
        k = lax.rem(place // per + 1 + kk, STEPS)
        for n in range(per):
            near_sum(k * per + n)

    near_sums(0)

    def both(kk):
        near_sums(kk + 1)
        own_chunk(kk)

    each(both, STEPS - 1)
    own_chunk(STEPS - 1)

    gs_ref[0, 1:2] = gain_in[...]
    rounds = [
        [(seq, sib), (seq, far), (seq, farsib)],
        [(lax.rem(seq + j, seq_count), me) for j in range(1, seq_count)],
    ]

    def gain_copy(stage, n):
        slot = 3 * stage + n
        return push(gs_ref.at[stage], gr_ref.at[slot], gsnd.at[slot], grcv.at[slot], rounds[stage][n])

    gains = gs_ref[0]
    for stage in range(2):
        for n in range(len(rounds[stage])):
            gain_copy(stage, n).start()
        for n in range(len(rounds[stage])):
            gain_copy(stage, n).wait_recv()
            gains = gains + gr_ref[3 * stage + n]
        if stage == 0:
            gs_ref[1] = gains
    gains_ref[...] = gains

    total = sum_ref[place].astype(F32)
    for j in range(1, half):
        level_copy(j).wait_recv()
        total = total + zr_ref[j].astype(F32)
    for c in range(3):
        wqkv_ref[c] = total[:, c * width : (c + 1) * width]
    wout_ref[...] = total[:, wide:]

    def close(k):
        for made in (back_a, back_y, back_b):
            made(k).wait_send()

    each(close, STEPS)
    each(lambda k: leave(k).wait(), STEPS)
    each(lambda b: near_copy(b).wait_send(), half)
    for stage in range(2):
        for n in range(len(rounds[stage])):
            gain_copy(stage, n).wait_send()
    for j in range(1, half):
        level_copy(j).wait_send()


def last_call(mixed, w, x, gain, grad, normed, out_stay, out_got, gain_two):
    seq_count = lax.axis_size("seq")
    rows, model = x.shape
    half = seq_count // 2
    piece = model // seq_count
    wide, width = mixed.shape[-1], w.shape[-1]
    dma = pltpu.SemaphoreType.DMA
    shape = jax.ShapeDtypeStruct
    rows_bf = pltpu.VMEM((rows, model), BF)
    pieces = pltpu.VMEM((half, piece, wide + width), BF)
    return pl.pallas_call(
        functools.partial(last_kernel, seq_count),
        in_specs=[ANY] * 3 + [VM] + [ANY] * 4 + [VM],
        out_specs=[ANY] + [VM] * 3,
        out_shape=[
            shape((rows, model), F32),
            shape((3, piece, width), F32),
            shape((piece, width), F32),
            shape((8, model), F32),
        ],
        scratch_shapes=[
            pltpu.VMEM(a.shape, a.dtype) for a in (mixed, w, x, grad, normed, out_stay, out_got)
        ]
        + [rows_bf] * 6
        + [pltpu.VMEM((2, half, piece, wide + width), BF), pieces, pieces, pieces]
        + [pltpu.VMEM((2, 8, model), F32), pltpu.VMEM((seq_count + 2, 8, model), F32)]
        + [
            dma((3, STEPS)),
            dma((3, STEPS)),
            dma((half,)),
            dma((half,)),
            dma((half,)),
            dma((half,)),
            dma((seq_count + 2,)),
            dma((seq_count + 2,)),
            dma((7 + STEPS,)),
        ],
        compiler_params=params(collective_id=2, has_side_effects=True),
        cost_estimate=cost(90_000_000_000, 30_000_000),
        name="last",
    )(mixed, w, x, gain, grad, normed, out_stay, out_got, gain_two)


def shards(
    latents_in,
    gain_one,
    w_qkv,
    w_out,
    gain_two,
    w_gate,
    w_up,
    w_down,
    cotangent,
    doc_lengths,
    valid_lengths,
    hash_ids,
    hash_weights,
):
    local_rows, model_width = latents_in.shape
    local_width = w_qkv.shape[2]
    group_rows = 4 * local_rows
    units = w_gate.shape[1]
    rank = lax.axis_index("tp")
    seq_count = lax.axis_size("seq")
    sc = (jnp.full((1,), rank, jnp.int32), doc_lengths.reshape(-1), valid_lengths.reshape(-1))
    gain_one, gain_two = gain_one[None], gain_two[None]

    per_seq = -(-HASH_ROWS // seq_count)
    high_rows = -(-per_seq // (LANES * 8)) * 8

    qkv_weight = w_qkv.transpose(1, 0, 2)
    piece = model_width // seq_count
    wo_four = w_out.reshape(seq_count // 2, 2, piece, local_width)
    normed, qkv, sums, wo_all = front_call(
        latents_in, gain_one, qkv_weight, hash_ids, hash_weights, wo_four, high_rows
    )
    wo_all = wo_all.reshape(4, model_width, local_width)
    qkv, cotangent_late = lax.optimization_barrier((qkv, cotangent))

    def level_flip(x, j):
        return lax.ppermute(x, "seq", [(s, (s + 2 * j) % seq_count) for s in range(seq_count)])

    table_parts = [sums] + [level_flip(sums, j) for j in range(1, seq_count // 4 + 1)]
    qkv = qkv.reshape(group_rows, 3 * local_width)
    cot_far = flip(cotangent_late, "tp", 2)
    heads_out, lse = attend_call(sc, qkv)
    heads_four = heads_out.reshape(4, local_rows, local_width)
    (
        rest, far_down, grad_hidden, gain_two_part, up_keep, up_send, out_stay, out_away,
        grad_heads, hash_parts, *pieces,
    ) = middle_call(
        heads_four, wo_all, latents_in, gain_two, cotangent, cot_far,
        (w_gate.T, w_up.T, w_down.T), table_parts,
    )
    out_got = flip(out_away, "tp", 2)
    down_far = flip(far_down, "tp", 2)
    up_got = flip(up_send, "seq", 1)
    arrived = [level_flip(pieces[j], j) for j in range(1, seq_count // 2)]
    hash_parts = hash_parts.reshape(2, seq_count // 2, hash_ids.shape[0], high_rows, LANES)
    mixed, hash_counts = attend_back_call(
        sc, grad_heads.reshape(group_rows, local_width), qkv, heads_out, lse, hash_parts, HASH_ROWS
    )
    mixed, up_got, arrived, down_far, out_got = lax.optimization_barrier(
        (mixed, up_got, arrived, down_far, out_got)
    )
    grad_latents, qkv_total, out_total, gains = last_call(
        mixed.reshape(4, local_rows, -1), qkv_weight, latents_in, gain_one, grad_hidden,
        normed, out_stay, out_got, gain_two_part,
    )
    total = pieces[0].astype(F32)
    for piece in arrived:
        total = total + piece.astype(F32)
    up_total = up_keep.astype(F32) + up_got.astype(F32)
    latents_out = (rest + down_far.astype(F32)).astype(BF)
    upright = lambda w: w.T if w.shape[0] == units else w
    return (
        latents_out,
        grad_latents,
        gains[0],
        qkv_total.transpose(1, 0, 2),
        out_total,
        gains[1],
        upright(total[1]),
        upright(up_total),
        upright(total[0]),
        hash_counts,
    )


def solution(mesh):
    in_specs = (
        P(("seq", "tp"), None),
        P(),
        P(None, None, "tp"),
        P(None, "tp"),
        P(),
        P(None, "tp"),
        P(None, "tp"),
        P(None, "tp"),
        P(("seq", "tp"), None),
        P("seq", None),
        P("seq", None),
        P(None, ("seq", "tp")),
        P(None, ("seq", "tp")),
    )
    out_specs = (
        P(("seq", "tp"), None),
        P(("seq", "tp"), None),
        P(),
        P("seq", None, "tp"),
        P("seq", "tp"),
        P(),
        P("seq", "tp"),
        P("seq", "tp"),
        P("seq", "tp"),
        P(),
    )
    return jax.shard_map(shards, mesh=mesh, in_specs=in_specs, out_specs=out_specs, check_vma=False)
```
